32 devices in a mesh: section: 4 (over y, x), dp: 8 (over z, core).
Axes of the slice: x: 2, y: 2, z: 4, core: 2. Of those that a mesh axis runs over, the one named last changes fastest.
Arguments:
- query_gradient_stack: float32 [4, 4096, 2048], P('section', 'dp'), may hold values from -6 to 6
- train_grads: float32 [4, 4096, 2048], P('section', 'dp'), may hold values from -6 to 6
- factor_slots: float32 [4, 8, 2048, 512], P('section', 'dp'), as said below
- owner: int32 [4, 4], P('section'), may hold values from 0 to 7, as said below
- train_count: int32 [8], P('dp'), may hold values from 128 to 512, as said below
Outputs:
- scores: float32 [8, 512, 1536], P('dp', 'section')
The draws below stay inside these ranges and needn't reach their ends.
Inputs may be any that keep to these rules, and one draw needn't show every extreme that they name: `owner`: for each layer the 4 entries are distinct data indices. `train_count`: some data index has all 512 training examples live. `factor_slots`: the diagonal entries of each factor lie between 0.9 and 2.1.
All inputs are finite; a program needn't handle non-finite values.
Results may differ from the reference program's by a relative error of at most 0.00019.
Values sent between devices are 32-bit elements; how exact they have to be, the bound alone decides.
No kernel may reach another device: no remote copies, remote signals or barrier semaphores. Data moves between devices by JAX's collectives and lax.ppermute only.
A program may use at most 128 MiB of HBM per device.

```python
import math
import jax
import jax.numpy as jnp
from jax import lax

COORDS = 2048
PANEL = 512
PANELS = 4
ROWS = 512
LAYERS = 4
N_DP = 8


def panel_owners(key):
    layer_keys = jax.random.split(jax.random.fold_in(key, 7), LAYERS)
    return jax.vmap(lambda layer_key: jax.random.permutation(layer_key, N_DP)[:PANELS])(layer_keys).astype(jnp.int32)


def draw_owner(key, part):
    return panel_owners(key)


def draw_factor_slots(key, part):
    owner_list = panel_owners(key)
    noise_part = jax.random.normal(jax.random.fold_in(key, 11), (LAYERS, N_DP, COORDS, PANEL), jnp.float32) * (0.5 / math.sqrt(COORDS))
    diagonal = jax.random.uniform(jax.random.fold_in(key, 13), (LAYERS, COORDS), jnp.float32, 1.0, 2.0)
    block_keeper = (owner_list[:, :, None] == jnp.arange(N_DP)[None, None, :]).astype(jnp.float32)
    row_index = jnp.arange(COORDS)
    row_panel_lookup = (row_index[:, None] // PANEL == jnp.arange(PANELS)[None, :]).astype(jnp.float32)
    diagonal_flag = (row_index[:, None] % PANEL == jnp.arange(PANEL)[None, :]).astype(jnp.float32)
    row_in_slot = jnp.einsum('fda,od->fao', block_keeper, row_panel_lookup)
    boosted = row_in_slot * diagonal[:, None, :]
    return noise_part + boosted[:, :, :, None] * diagonal_flag[None, None, :, :]


def draw_train_count(key, part):
    counts = jax.random.randint(jax.random.fold_in(key, 17), (N_DP,), ROWS // 4, ROWS + 1)
    fullest = jax.random.randint(jax.random.fold_in(key, 19), (), 0, N_DP)
    return jnp.where(jnp.arange(N_DP) == fullest, ROWS, counts).astype(jnp.int32)


def steps_of(key, shape, cuts, low, top_value):
    level, own = 1.0, jax.random.fold_in(key, 6)
    for dim, parts in cuts:
        draws = jnp.exp(jax.random.uniform(jax.random.fold_in(own, dim), (parts,), jnp.float32, low / len(cuts), top_value / len(cuts)))
        level = level * jnp.repeat(draws, shape[dim] // parts).reshape([-1 if axis == dim else 1 for axis in range(len(shape))])
    return level


def scatter_about(stream_key, extent, deviation, limit, pieces=(), kind=jnp.bfloat16):
    entries = jax.random.normal(stream_key, extent, jnp.float32) * deviation
    if len(pieces) > 0:
        entries = steps_of(stream_key, extent, pieces, -0.22, 0.18) * entries
    return jnp.clip(entries, min=-limit, max=limit).astype(kind)


def setup_inputs(seed: int = 0) -> dict:
    key_of = jax.random.split(jax.random.key(seed), 6)
    return {
        "query_gradient_stack": scatter_about(key_of[0], (LAYERS, ROWS * N_DP, COORDS), 1.0, 6.0, ((0, 4), (1, 8)), jnp.float32),
        "train_grads": scatter_about(key_of[1], (LAYERS, ROWS * N_DP, COORDS), 1.0, 6.0, ((0, 4), (1, 8)), jnp.float32),
        "factor_slots": draw_factor_slots(jax.random.fold_in(key_of[5], 71), 0),
        "owner": draw_owner(jax.random.fold_in(key_of[5], 71), 0),
        "train_count": draw_train_count(jax.random.fold_in(key_of[5], 71), 0),
    }


def solve_layer(factor_full, gradient_rows):
    return lax.linalg.triangular_solve(factor_full, gradient_rows, left_side=False, lower=True, transpose_a=True)

def reference(query_gradient_stack, train_grads, factor_slots, owner, train_count):
    running = jnp.zeros((N_DP, ROWS, 3 * ROWS), jnp.float32)
    for layer_index in range(LAYERS):
        panel_set = factor_slots[layer_index][owner[layer_index]]
        factor_full = jnp.tril(jnp.transpose(panel_set, (1, 0, 2)).reshape(COORDS, COORDS))
        query_solved = solve_layer(factor_full, query_gradient_stack[layer_index]).reshape(N_DP, ROWS, COORDS)
        train_solved = solve_layer(factor_full, train_grads[layer_index]).reshape(N_DP, ROWS, COORDS)
        columns = jnp.concatenate([train_solved, jnp.roll(train_solved, 1, axis=0), jnp.roll(train_solved, 2, axis=0)], axis=1)
        running = running + jnp.einsum('dik,djk->dij', query_solved, columns, precision=lax.Precision.HIGHEST)
    counts = jnp.stack([train_count, jnp.roll(train_count, 1), jnp.roll(train_count, 2)], axis=1)
    valid = (jnp.arange(ROWS, dtype=jnp.int32)[None, None, :] < counts[:, :, None]).astype(jnp.float32)
    valid = valid.reshape(N_DP, 3 * ROWS)
    score_scale = (COORDS * LAYERS) ** (-0.5)
    return running * (score_scale * valid)[:, None, :]
```

```python
import jax
import jax.numpy as jnp
from jax import lax
from jax.experimental import pallas as pl
from jax.experimental.pallas import tpu as pltpu
from jax.sharding import PartitionSpec as P

HIGH = lax.Precision.HIGH
HIGHEST = lax.Precision.HIGHEST
TILE = 128
CHUNKS = 8
SKEW = 1
TRAIN_CUTS = (128, 128, 96, 96, 64)


def dot_nt(a, b, precision=HIGH):
    return lax.dot_general(
        a, b, (((1,), (1,)), ((), ())), precision=precision, preferred_element_type=jnp.float32
    )


def dot_nn(a, b, precision=HIGH):
    return lax.dot_general(
        a, b, (((1,), (0,)), ((), ())), precision=precision, preferred_element_type=jnp.float32
    )


def after(value, *others):
    return lax.optimization_barrier((value, *others))[0]


def invert_kernel(panel_ref, block_ref, packed_ref):
    size = block_ref.shape[0]
    count = size // TILE
    row = lax.broadcasted_iota(jnp.int32, (TILE, TILE), 0)
    col = lax.broadcasted_iota(jnp.int32, (TILE, TILE), 1)
    spans = [slice(i * TILE, (i + 1) * TILE) for i in range(count)]
    low = [block_ref[s, s] for s in spans]
    inv = []
    for tile in low:
        diagonal = jnp.sum(jnp.where(row == col, tile, 0.0), axis=1, keepdims=True)
        inv.append(jnp.where(row == col, 1.0 / diagonal, 0.0))
    width = 1
    while width < TILE:
        joins = (row // (2 * width) == col // (2 * width)) & (row // width > col // width)
        half = [dot_nn(jnp.where(joins, low[i], 0.0), inv[i], HIGHEST) for i in range(count)]
        inv = [inv[i] - dot_nn(inv[i], half[i], HIGHEST) for i in range(count)]
        width *= 2
    while len(inv) > 1:
        size_now = inv[0].shape[0]
        zero = jnp.zeros((size_now, size_now), jnp.float32)
        merged = []
        for i in range(0, len(inv), 2):
            below = block_ref[(i + 1) * size_now : (i + 2) * size_now, i * size_now : (i + 1) * size_now]
            corner = -dot_nn(inv[i + 1], dot_nn(below, inv[i], HIGHEST), HIGHEST)
            merged.append(
                jnp.concatenate(
                    [
                        jnp.concatenate([inv[i], zero], axis=1),
                        jnp.concatenate([corner, inv[i + 1]], axis=1),
                    ],
                    axis=0,
                )
            )
        inv = merged
    whole = inv[0]
    half_width = size // 2
    packed_ref[0:TILE, :] = whole[3 * TILE : 4 * TILE, :]
    packed_ref[TILE : 2 * TILE, 0 : 3 * TILE] = whole[2 * TILE : 3 * TILE, 0 : 3 * TILE]
    packed_ref[TILE : 2 * TILE, 3 * TILE :] = whole[0:TILE, 0:TILE]
    mid = TILE + TILE // 2
    packed_ref[2 * TILE :, 0:half_width] = whole[TILE:mid, 0:half_width]
    packed_ref[2 * TILE :, half_width:] = whole[mid : 2 * TILE, 0:half_width]


def inverted_diagonal(slot, panel):
    size = slot.shape[1]
    rows = 2 * TILE + TILE // 2
    return pl.pallas_call(
        invert_kernel,
        out_shape=jax.ShapeDtypeStruct((rows, size), jnp.float32),
        grid_spec=pltpu.PrefetchScalarGridSpec(
            num_scalar_prefetch=1,
            grid=(1,),
            in_specs=[pl.BlockSpec((size, size), lambda i, which: (which[0], 0))],
            out_specs=pl.BlockSpec((rows, size), lambda i, which: (0, 0)),
        ),
        compiler_params=pltpu.CompilerParams(vmem_limit_bytes=16 * 1024 * 1024),
        cost_estimate=pl.CostEstimate(flops=500_000_000, bytes_accessed=2_000_000, transcendentals=0),
    )(panel.reshape(1), slot)


def unpacked(packed):
    half_width = packed.shape[1] // 2
    zeros = lambda tiles: jnp.zeros((TILE, tiles * TILE), jnp.float32)
    row_0 = jnp.concatenate([packed[TILE : 2 * TILE, 3 * TILE :], zeros(3)], axis=1)
    second = jnp.concatenate([packed[2 * TILE :, :half_width], packed[2 * TILE :, half_width:]], axis=0)
    row_1 = jnp.concatenate([second, zeros(2)], axis=1)
    row_2 = jnp.concatenate([packed[TILE : 2 * TILE, : 3 * TILE], zeros(1)], axis=1)
    return jnp.concatenate([row_0, row_1, row_2, packed[:TILE]], axis=0)


def body(query_gradient_stack, train_grads, factor_slots, owner, train_count):
    query, train, slot, owners = query_gradient_stack[0], train_grads[0], factor_slots[0, 0], owner[0]
    rows, coords = query.shape
    size = slot.shape[1]
    panels = coords // size
    n_dp, n_sec = lax.axis_size("dp"), lax.axis_size("section")
    chips = n_dp // 2
    me = lax.axis_index("dp")
    chip, core = me // 2, me % 2
    first_core = core == 0

    swap_pairs = [(d, d ^ 1) for d in range(n_dp)]
    next_chip = [(d, (d + 2) % n_dp) for d in range(n_dp)]

    def swapped(value):
        return lax.ppermute(value, "dp", swap_pairs)

    cuts = [sum(TRAIN_CUTS[:i]) for i in range(len(TRAIN_CUTS) + 1)]
    train_parts = [train[a:b] for a, b in zip(cuts, cuts[1:])]
    far_parts = [None] * len(train_parts)

    def send_train(index, *deps):
        part = after(train_parts[index], *deps) if deps else train_parts[index]
        far_parts[index] = lax.ppermute(part, "dp", next_chip)

    send_train(0)

    held = jnp.argmax(owners == me).astype(jnp.int32)
    split = slot.reshape(panels, 2, size // 2, size)
    own_half = lax.dynamic_index_in_dim(split, core, 1, keepdims=False)
    sent_half = lax.dynamic_index_in_dim(split[1:], 1 - core, 1, keepdims=False)
    peer_half = swapped(sent_half)
    packed = inverted_diagonal(slot, held)
    packed_rows = packed.shape[0] // 2
    packed_split = packed.reshape(2, packed_rows, size)
    own_packed = lax.dynamic_index_in_dim(packed_split, core, 0, keepdims=False)
    peer_packed = swapped(lax.dynamic_index_in_dim(packed_split, 1 - core, 0, keepdims=False))

    pieces, piece_panel, piece_rows = [], [], []
    for j in range(panels):
        mine = owners[j] == me
        if j + 1 < panels:
            piece = jnp.where(mine, own_half[j + 1 :], peer_half[j:])
            pieces.append(piece.reshape(-1, size))
            piece_panel.append(j)
            piece_rows.append(pieces[-1].shape[0])
        pieces.append(jnp.where(mine, own_packed, peer_packed))
        piece_panel.append(j)
        piece_rows.append(packed_rows)
    stream = jnp.concatenate(pieces, axis=0)
    total = stream.shape[0]
    step_rows = total // CHUNKS
    source = jnp.concatenate(
        [jnp.full((r, 1), owners[j] // 2, jnp.int32) for j, r in zip(piece_panel, piece_rows)], axis=0
    )
    below, above = source < chip, source > chip

    def chain(place, from_before):
        got = {}

        def step(number, *deps):
            index = number - SKEW * place(chip)
            start = index * step_rows
            block = lax.dynamic_slice_in_dim(stream, start, step_rows, 0)
            if number - SKEW in got:
                choose = lax.dynamic_slice_in_dim(from_before, start, step_rows, 0)
                block = jnp.where(choose, got[number - SKEW], block)
            if deps:
                block = after(block, *deps)
            pairs = []
            for z in range(chips):
                if place(z) < chips - 1 and 0 <= number - SKEW * place(z) < CHUNKS:
                    to = [y for y in range(chips) if place(y) == place(z) + 1][0]
                    pairs += [(2 * z + c, 2 * to + c) for c in range(2)]
            got[number] = lax.ppermute(block, "dp", pairs)
            return got[number]

        def chunk(index):
            value = got[index]
            for p in range(2, chips):
                value = jnp.where(place(chip) == p, got[index + SKEW * (p - 1)], value)
            return value

        return step, chunk

    up_step, up_chunk = chain(lambda z: z, below)
    down_step, down_chunk = chain(lambda z: chips - 1 - z, above)
    steps = CHUNKS + SKEW * (chips - 2)
    merged = []

    def finish(index):
        span = slice(index * step_rows, (index + 1) * step_rows)
        value = jnp.where(
            below[span], up_chunk(index), jnp.where(above[span], down_chunk(index), stream[span])
        )
        other = swapped(value)
        merged.append((jnp.where(first_core, value, other), jnp.where(first_core, other, value)))

    def stream_piece(number):
        start = sum(piece_rows[:number])
        stop = start + piece_rows[number]
        halves = []
        for half in range(2):
            parts = []
            for i in range(start // step_rows, (stop - 1) // step_rows + 1):
                low, high = max(start, i * step_rows), min(stop, (i + 1) * step_rows)
                parts.append(merged[i][half][low - i * step_rows : high - i * step_rows])
            halves.append(jnp.concatenate(parts, axis=0))
        return halves

    off_blocks, inverses, solved, pending = [], [], [], query
    piece_number = 0

    def forward_ready():
        nonlocal piece_number, pending
        while len(solved) < panels:
            j = len(solved)
            last = piece_number + (1 if j + 1 < panels else 0)
            if sum(piece_rows[: last + 1]) > len(merged) * step_rows:
                return
            if j + 1 < panels:
                low, high = stream_piece(piece_number)
                shape = (panels - 1 - j, 1, size // 2, size)
                off = jnp.concatenate([low.reshape(shape), high.reshape(shape)], axis=1)
                off_blocks.append(off.reshape(-1, size))
            low, high = stream_piece(last)
            inverses.append(unpacked(jnp.concatenate([low, high], axis=0)))
            piece_number = last + 1
            part = dot_nt(pending[:, :size], inverses[j])
            solved.append(part)
            if j + 1 < panels:
                pending = pending[:, size:] - dot_nt(part, off_blocks[j])

    for number in range(steps):
        sent_up = up_step(number)
        sent_down = down_step(number)
        ready = number - SKEW * (chips - 2)
        if ready >= 0:
            finish(ready)
            forward_ready()
    for index in range(1, len(train_parts)):
        send_train(index, sent_up, sent_down)

    answer = [None] * panels
    for j in reversed(range(panels)):
        right = solved[j]
        if j + 1 < panels:
            right = right - dot_nn(jnp.concatenate(answer[j + 1 :], axis=1), off_blocks[j])
        answer[j] = dot_nn(right, inverses[j])
    weights = jnp.concatenate(answer, axis=1)

    count_2 = lax.ppermute(train_count, "dp", next_chip)
    count_1 = lax.ppermute(train_count, "dp", [(d, (d + 1) % n_dp) for d in range(n_dp)])
    scale = (coords * n_sec) ** (-0.5)
    section = lax.axis_index("section")
    out_rows = rows // n_sec

    def reduced(part, counts, first, length):
        live = jnp.arange(first, first + length, dtype=jnp.int32)
        factor = jnp.concatenate([jnp.where(live < c[0], scale, 0.0) for c in counts]).astype(jnp.float32)
        part = part * factor[None, :]
        blocks = part.reshape(n_sec, out_rows, -1)
        total_part = lax.dynamic_index_in_dim(blocks, section, 0, keepdims=False)
        for k in range(1, n_sec):
            if n_sec & (n_sec - 1) == 0:
                pairs = [(s, s ^ k) for s in range(n_sec)]
                target = section ^ k
            else:
                pairs = [(s, (s + k) % n_sec) for s in range(n_sec)]
                target = (section + k) % n_sec
            block = lax.dynamic_index_in_dim(blocks, target, 0, keepdims=False)
            total_part = total_part + lax.ppermute(block, "section", pairs)
        return total_part

    own_scores = reduced(dot_nt(weights, train), [train_count], 0, rows)
    near_scores, far_scores = [], []
    for index, far in enumerate(far_parts):
        near = swapped(jnp.where(first_core, train_parts[index], far))
        length = cuts[index + 1] - cuts[index]
        both = dot_nt(weights, jnp.concatenate([near, far], axis=0))
        part = reduced(both, [count_1, count_2], cuts[index], length)
        near_scores.append(part[:, :length])
        far_scores.append(part[:, length:])
    return jnp.concatenate([own_scores] + near_scores + far_scores, axis=1)[None]


def solution(mesh):
    in_specs = (
        P("section", "dp", None),
        P("section", "dp", None),
        P("section", "dp", None, None),
        P("section", None),
        P("dp"),
    )
    out_specs = P("dp", "section", None)
    return jax.shard_map(body, mesh=mesh, in_specs=in_specs, out_specs=out_specs, check_vma=False)
```

```python
import functools

import jax
import jax.numpy as jnp
from jax import lax
from jax.experimental import pallas as pl
from jax.experimental.pallas import tpu as pltpu
from jax.sharding import PartitionSpec as P

HIGHEST = lax.Precision.HIGHEST
CHUNKS = 8
SKEW = 2
GROUPS = ((0, 5), (5, 8))
TRAIN_CUTS = (128, 128, 128, 96, 32)
MIB = 1024 * 1024
ANY = pl.BlockSpec(memory_space=pl.ANY)
SMEM = pl.BlockSpec(memory_space=pltpu.SMEM)
VMEM = pl.BlockSpec(memory_space=pltpu.VMEM)


def dot(a, b, contract, precision=None):
    return lax.dot_general(
        a, b, (((1,), (contract,)), ((), ())), precision=precision, preferred_element_type=jnp.float32
    )


def parts_of(value):
    high = value.astype(jnp.bfloat16)
    return high, (value - high.astype(jnp.float32)).astype(jnp.bfloat16)


def dot_parts(a, b, contract):
    return dot(a[0], b[0], contract) + (dot(a[0], b[1], contract) + dot(a[1], b[0], contract))


def after(value, *others):
    return lax.optimization_barrier((value, *others))[0]


def partner(section, k, n_sec):
    if n_sec & (n_sec - 1) == 0:
        return section ^ k
    return lax.rem(section + k, n_sec)


def param(limit_mib):
    return pltpu.CompilerParams(vmem_limit_bytes=limit_mib * MIB)


def cost(flops, moved):
    return pl.CostEstimate(flops=flops, bytes_accessed=moved, transcendentals=0)


def invert_kernel(panel_ref, block_ref, packed_ref):
    size = block_ref.shape[0]
    count = 4
    tile = size // count
    row = lax.broadcasted_iota(jnp.int32, (tile, tile), 0)
    col = lax.broadcasted_iota(jnp.int32, (tile, tile), 1)
    spans = [slice(i * tile, (i + 1) * tile) for i in range(count)]
    low = [block_ref[s, s] for s in spans]
    inv = []
    for block in low:
        diagonal = jnp.sum(jnp.where(row == col, block, 0.0), axis=1, keepdims=True)
        inv.append(jnp.where(row == col, 1.0 / diagonal, 0.0))
    width = 1
    while width < tile:
        joins = (row // (2 * width) == col // (2 * width)) & (row // width > col // width)
        half = [dot(jnp.where(joins, low[i], 0.0), inv[i], 0, HIGHEST) for i in range(count)]
        inv = [inv[i] - dot(inv[i], half[i], 0, HIGHEST) for i in range(count)]
        width *= 2
    while len(inv) > 1:
        width = inv[0].shape[0]
        zero = jnp.zeros((width, width), jnp.float32)
        merged = []
        for i in range(0, len(inv), 2):
            below = block_ref[(i + 1) * width : (i + 2) * width, i * width : (i + 1) * width]
            corner = -dot(inv[i + 1], dot(below, inv[i], 0, HIGHEST), 0, HIGHEST)
            top = jnp.concatenate([inv[i], zero], axis=1)
            merged.append(jnp.concatenate([top, jnp.concatenate([corner, inv[i + 1]], axis=1)], axis=0))
        inv = merged
    whole = inv[0]
    mid = tile + tile // 2
    packed_ref[0:tile, :] = whole[3 * tile :, :]
    packed_ref[tile : 2 * tile, 0 : 3 * tile] = whole[2 * tile : 3 * tile, 0 : 3 * tile]
    packed_ref[tile : 2 * tile, 3 * tile :] = whole[0:tile, 0:tile]
    packed_ref[2 * tile :, 0 : 2 * tile] = whole[tile:mid, 0 : 2 * tile]
    packed_ref[2 * tile :, 2 * tile :] = whole[mid : 2 * tile, 0 : 2 * tile]


def inverted_diagonal(slot, panel):
    size = slot.shape[1]
    rows = size // 2 + size // 8
    return pl.pallas_call(
        invert_kernel,
        out_shape=jax.ShapeDtypeStruct((rows, size), jnp.float32),
        grid_spec=pltpu.PrefetchScalarGridSpec(
            num_scalar_prefetch=1,
            grid=(1,),
            in_specs=[pl.BlockSpec((size, size), lambda i, which: (which[0], 0))],
            out_specs=pl.BlockSpec((rows, size), lambda i, which: (0, 0)),
        ),
        compiler_params=param(16),
        cost_estimate=cost(4_000_000_000, 2_000_000),
    )(panel, slot)


class Stream:
    def __init__(self, panels, size):
        self.panels, self.size, self.half = panels, size, size // 2
        self.packed = (size // 2 + size // 8) // 2
        self.pieces, self.starts, start = [], [], 0
        for j in range(panels):
            for k in [*range(j + 1, panels), None]:
                self.pieces.append((j, k))
                self.starts.append(start)
                start += self.packed if k is None else self.half
        self.total = start
        self.step = start // CHUNKS

    def rows(self, piece):
        return self.packed if self.pieces[piece][1] is None else self.half

    def panel_start(self, j):
        last = self.panels - 1
        return j * self.packed + self.half * (j * last - (j * (j - 1)) // 2)

    def panel_ends(self):
        return [self.panel_start(j + 1) for j in range(self.panels)]


def build_kernel(stream, chips, info, slot, peer, packed, peer_packed, up, down, sems):
    chip, core, me = info[0], info[1], info[2]
    shift = SKEW * stream.step
    number = 0
    pending = []
    for piece, (j, k) in enumerate(stream.pieces):
        count = stream.rows(piece)
        if k is None:
            mine = packed.at[pl.ds(pl.multiple_of(core * count, 8), count)]
            theirs = peer_packed
        else:
            mine = slot.at[pl.ds(pl.multiple_of(k * stream.size + core * count, 8), count)]
            theirs = peer.at[k - 1]
        is_mine = info[4 + j] == me
        for place, out in ((chip, up), (chips - 1 - chip, down)):
            target = out.at[pl.ds(pl.multiple_of(place * shift + stream.starts[piece], 8), count)]
            own_copy = pltpu.make_async_copy(mine, target, sems.at[number])
            peer_copy = pltpu.make_async_copy(theirs, target, sems.at[number])
            pl.when(is_mine)(own_copy.start)
            pl.when(jnp.logical_not(is_mine))(peer_copy.start)
            pending.append(peer_copy)
            number += 1
    for copy in pending:
        copy.wait()


def build_streams(stream, chips, info, slot, peer, packed, peer_packed):
    rows = stream.total + SKEW * stream.step * (chips - 1)
    shape = jax.ShapeDtypeStruct((rows, stream.size), jnp.float32)
    return pl.pallas_call(
        functools.partial(build_kernel, stream, chips),
        out_shape=(shape, shape),
        in_specs=[SMEM, ANY, ANY, ANY, ANY],
        out_specs=(ANY, ANY),
        scratch_shapes=[pltpu.SemaphoreType.DMA((2 * len(stream.pieces),))],
        compiler_params=param(8),
        cost_estimate=cost(0, 16_000_000),
    )(info, slot, peer, packed, peer_packed)


def collect_kernel(stream, chips, first, last, info, up, *refs):
    sent = SKEW * (chips - 2) + last - first
    ups, downs, out, sems = refs[:sent], refs[sent : 2 * sent], refs[-2], refs[-1]
    chip = info[0]
    pending = []
    number = 0
    for i in range(first, last):
        for piece, (j, _) in enumerate(stream.pieces):
            low = max(stream.starts[piece], i * stream.step)
            high = min(stream.starts[piece] + stream.rows(piece), (i + 1) * stream.step)
            if low >= high:
                continue
            count = high - low
            origin = info[4 + j] >> 1
            target = out.at[pl.ds(low - first * stream.step, count)]
            inside = pl.ds(low - i * stream.step, count)
            start = pl.multiple_of(chip * SKEW * stream.step + low, 8)
            own_copy = pltpu.make_async_copy(up.at[pl.ds(start, count)], target, sems.at[number])
            pl.when(origin == chip)(own_copy.start)
            for p in range(1, chips):
                at = i - first + SKEW * (p - 1)
                rising = pltpu.make_async_copy(ups[at].at[inside], target, sems.at[number])
                pl.when((chip == p) & (origin < chip))(rising.start)
                falling = pltpu.make_async_copy(downs[at].at[inside], target, sems.at[number])
                pl.when((chip == chips - 1 - p) & (origin > chip))(falling.start)
            pending.append(own_copy)
            number += 1
    for copy in pending:
        copy.wait()


def collected(stream, chips, first, last, info, up, got_up, got_down):
    steps = range(first, last + SKEW * (chips - 2))
    received = [got_up[s] for s in steps] + [got_down[s] for s in steps]
    return pl.pallas_call(
        functools.partial(collect_kernel, stream, chips, first, last),
        out_shape=jax.ShapeDtypeStruct(((last - first) * stream.step, stream.size), jnp.float32),
        in_specs=[SMEM] + [ANY] * (1 + len(received)),
        out_specs=ANY,
        scratch_shapes=[pltpu.SemaphoreType.DMA(((last - first) * len(stream.pieces),))],
        compiler_params=param(8),
        cost_estimate=cost(0, 4_000_000),
    )(info, up, *received)


def sweep_kernel(stream, n_sec, info, query, *refs):
    groups = len(GROUPS)
    own, other = refs[:groups], refs[groups : 2 * groups]
    out_high, out_low, low_high, low_low, inv_high, inv_low, pending, part_high, part_low = refs[2 * groups :]
    core, section = info[1], info[3]
    panels, size, half = stream.panels, stream.size, stream.half
    rows = query.shape[0]
    block = rows // n_sec
    tile = size // 4
    step = stream.step

    for (first, last), mine, theirs in zip(GROUPS, own, other):
        for source, place in ((mine, core), (theirs, 1 - core)):

            @pl.loop(0, last - first)
            def _(i):
                start = pl.multiple_of(i * step, 16)
                target = pl.ds(pl.multiple_of((first + i) * step, 16), step)
                high, low = parts_of(source[pl.ds(start, step), :])
                low_high[place, target, :] = high
                low_low[place, target, :] = low

    for k in range(n_sec):
        start = pl.multiple_of(partner(section, k, n_sec) * block, block)
        for j in range(panels):
            pending[j, k * block : (k + 1) * block, :] = query[pl.ds(start, block), j * size : (j + 1) * size]

    split = stream.packed - tile
    for j in range(panels):
        s = stream.panel_start(j + 1) - stream.packed
        for source, target in ((low_high, inv_high), (low_low, inv_low)):
            target[j] = jnp.zeros((size, size), jnp.bfloat16)
            target[j, 3 * tile :, :] = source[0, s : s + tile, :]
            target[j, 2 * tile : 2 * tile + split, : 3 * tile] = source[0, s + tile : s + tile + split, : 3 * tile]
            target[j, 2 * tile + split : 3 * tile, : 3 * tile] = source[1, s : s + tile - split, : 3 * tile]
            target[j, :split, :tile] = source[0, s + tile : s + tile + split, 3 * tile :]
            target[j, split:tile, :tile] = source[1, s : s + tile - split, 3 * tile :]
            rest = source[1, s + tile - split : s + stream.packed, :]
            target[j, tile : tile + tile // 2, : 2 * tile] = rest[:, : 2 * tile]
            target[j, tile + tile // 2 : 2 * tile, : 2 * tile] = rest[:, 2 * tile :]

    def below(j, k, h):
        start = stream.panel_start(j) + (k - j - 1) * half
        span = pl.ds(pl.multiple_of(start, 16), half)
        return low_high[h, span, :], low_low[h, span, :]

    @pl.loop(0, panels)
    def _(j):
        solved = dot_parts(parts_of(pending[j]), (inv_high[j], inv_low[j]), 1)
        pending[j] = solved
        part_high[...], part_low[...] = parts_of(solved)

        @pl.loop(j + 1, panels)
        def _(k):
            for h in range(2):
                span = slice(h * half, (h + 1) * half)
                update = dot_parts((part_high[...], part_low[...]), below(j, k, h), 1)
                pending[k, :, span] = pending[k, :, span] - update

    @pl.loop(0, panels)
    def _(step_number):
        j = panels - 1 - step_number

        @pl.loop(j + 1, panels)
        def _(k):
            update = jnp.zeros((rows, size), jnp.float32)
            for h in range(2):
                span = slice(h * half, (h + 1) * half)
                update += dot_parts((out_high[k, :, span], out_low[k, :, span]), below(j, k, h), 0)
            pending[j] = pending[j] - update

        answer = dot_parts(parts_of(pending[j]), (inv_high[j], inv_low[j]), 0)
        out_high[j], out_low[j] = parts_of(answer)


def swept(stream, n_sec, info, query, own, other):
    rows = query.shape[0]
    panels, size, total = stream.panels, stream.size, stream.total
    out = jax.ShapeDtypeStruct((panels, rows, size), jnp.bfloat16)
    return pl.pallas_call(
        functools.partial(sweep_kernel, stream, n_sec),
        out_shape=(out, out),
        in_specs=[SMEM] + [VMEM] * (1 + len(own) + len(other)),
        out_specs=(VMEM, VMEM),
        scratch_shapes=[
            pltpu.VMEM((2, total, size), jnp.bfloat16),
            pltpu.VMEM((2, total, size), jnp.bfloat16),
            pltpu.VMEM((panels, size, size), jnp.bfloat16),
            pltpu.VMEM((panels, size, size), jnp.bfloat16),
            pltpu.VMEM((panels, rows, size), jnp.float32),
            pltpu.VMEM((rows, size), jnp.bfloat16),
            pltpu.VMEM((rows, size), jnp.bfloat16),
        ],
        compiler_params=param(46),
        cost_estimate=cost(18_000_000_000, 20_000_000),
    )(info, query, *own, *other)


def score_kernel(n_sec, scale, first, counts, high, low, *refs):
    blocks = len(refs) - n_sec - 3
    trains, outs = refs[:blocks], refs[blocks : blocks + n_sec]
    train_high, train_low, total = refs[-3:]
    panels, rows, size = high.shape
    length = trains[0].shape[0]
    for b, train in enumerate(trains):
        for p in range(panels):
            span = slice(b * length, (b + 1) * length)
            train_high[p, span, :], train_low[p, span, :] = parts_of(train[:, p * size : (p + 1) * size])
    total[...] = jnp.zeros_like(total)

    @pl.loop(0, panels)
    def _(p):
        total[...] += dot_parts((high[p], low[p]), (train_high[p], train_low[p]), 1)

    col = lax.broadcasted_iota(jnp.int32, (1, blocks * length), 1)
    limit = jnp.full_like(col, counts[0] - first)
    for b in range(1, blocks):
        limit = jnp.where(col >= b * length, counts[b] - first + b * length, limit)
    factor = jnp.where(col < limit, scale, 0.0).astype(jnp.float32)
    share = rows // n_sec
    for k in range(n_sec):
        outs[k][...] = total[k * share : (k + 1) * share, :] * factor


def scored(n_sec, scale, first, counts, high, low, trains):
    panels, rows, size = high.shape
    cols = sum(t.shape[0] for t in trains)
    return pl.pallas_call(
        functools.partial(score_kernel, n_sec, scale, first),
        out_shape=tuple(jax.ShapeDtypeStruct((rows // n_sec, cols), jnp.float32) for _ in range(n_sec)),
        in_specs=[SMEM] + [VMEM] * (2 + len(trains)),
        out_specs=tuple(VMEM for _ in range(n_sec)),
        scratch_shapes=[
            pltpu.VMEM((panels, cols, size), jnp.bfloat16),
            pltpu.VMEM((panels, cols, size), jnp.bfloat16),
            pltpu.VMEM((rows, cols), jnp.float32),
        ],
        compiler_params=param(24),
        cost_estimate=cost(6 * panels * size * rows * cols, 4_000_000 + 12 * cols * panels * size),
    )(counts, high, low, *trains)


def body(query_gradient_stack, train_grads, factor_slots, owner, train_count):
    query, train, slot, owners = query_gradient_stack[0], train_grads[0], factor_slots[0, 0], owner[0]
    rows, coords = query.shape
    size = slot.shape[1]
    panels = coords // size
    half = size // 2
    n_dp, n_sec = lax.axis_size("dp"), lax.axis_size("section")
    chips = n_dp // 2
    stream = Stream(panels, size)
    step_rows = stream.step
    me = lax.axis_index("dp")
    section = lax.axis_index("section")
    chip, core = lax.shift_right_logical(me, 1), me & 1
    first_core = core == 0
    info = jnp.concatenate([jnp.stack([chip, core, me, section]).astype(jnp.int32), owners])

    swap_pairs = [(d, d ^ 1) for d in range(n_dp)]
    next_chip = [(d, (d + 2) % n_dp) for d in range(n_dp)]

    def swapped(value):
        return lax.ppermute(value, "dp", swap_pairs)

    cuts = [sum(TRAIN_CUTS[:i]) for i in range(len(TRAIN_CUTS) + 1)]
    train_parts = [train[a:b] for a, b in zip(cuts, cuts[1:])]
    far = [None] * len(train_parts)

    def send_train(index, *deps):
        part = after(train_parts[index], *deps) if deps else train_parts[index]
        far[index] = lax.ppermute(part, "dp", next_chip)

    send_train(0)

    split = slot.reshape(panels, 2, half, size)
    to_peer = jnp.where(first_core, split[1:, 1], split[1:, 0])
    peer = swapped(to_peer)
    held = jnp.argmax(owners == me).astype(jnp.int32).reshape(1)
    packed = inverted_diagonal(slot, held)
    peer_packed = swapped(jnp.where(first_core, packed[stream.packed :], packed[: stream.packed]))
    up, down = build_streams(stream, chips, info, slot, peer, packed, peer_packed)

    position = lax.broadcasted_iota(jnp.int32, up.shape[:1] + (1,), 0)
    owner_chip = lax.shift_right_logical(owners, 1)

    def origin(place):
        row = position - place * (SKEW * step_rows)
        value = jnp.broadcast_to(owner_chip[0], row.shape)
        for j, end in enumerate(stream.panel_ends()[:-1]):
            value = jnp.where(row >= end, owner_chip[j + 1], value)
        return value

    lines = []
    for place, own_rows in ((lambda z: z, up), (lambda z: chips - 1 - z, down)):
        from_before = origin(place(chip)) < chip if own_rows is up else origin(place(chip)) > chip
        lines.append((place, own_rows, from_before, {}))

    def move(line, number):
        place, own_rows, from_before, got = line
        span = slice(number * step_rows, (number + 1) * step_rows)
        block = own_rows[span]
        if number >= SKEW:
            block = jnp.where(from_before[span], got[number - SKEW], block)
        pairs = []
        for z in range(chips):
            if place(z) < chips - 1 and 0 <= number - SKEW * place(z) < CHUNKS:
                to = [y for y in range(chips) if place(y) == place(z) + 1][0]
                pairs += [(2 * z + c, 2 * to + c) for c in range(2)]
        got[number] = lax.ppermute(block, "dp", pairs)
        return block

    own, other = [], []
    for number in range(CHUNKS + SKEW * (chips - 2)):
        sent = [move(line, number) for line in lines]
        for first, last in GROUPS:
            if number == last - 1 + SKEW * (chips - 2):
                value = collected(stream, chips, first, last, info, up, lines[0][3], lines[1][3])
                own.append(value)
                other.append(swapped(value))
    send_train(1, *sent)
    send_train(2, *sent)
    for index in range(3, len(train_parts)):
        send_train(index, far[index - 2])

    high, low = swept(stream, n_sec, info, query, own, other)

    count_2 = lax.ppermute(train_count, "dp", next_chip)
    count_1 = lax.ppermute(train_count, "dp", [(d, (d + 1) % n_dp) for d in range(n_dp)])
    near_counts = jnp.concatenate([count_1, count_2])
    scale = (coords * n_sec) ** (-0.5)

    def summed(parts):
        total = parts[0]
        for k in range(1, n_sec):
            if n_sec & (n_sec - 1) == 0:
                pairs = [(s, s ^ k) for s in range(n_sec)]
            else:
                pairs = [(s, (s + k) % n_sec) for s in range(n_sec)]
            total = total + lax.ppermute(parts[k], "section", pairs)
        return total

    own_scores = summed(scored(n_sec, scale, 0, train_count, high, low, [train]))
    near_scores, far_scores = [], []
    for index, far_part in enumerate(far):
        near_part = swapped(jnp.where(first_core, train_parts[index], far_part))
        length = cuts[index + 1] - cuts[index]
        both = summed(scored(n_sec, scale, cuts[index], near_counts, high, low, [near_part, far_part]))
        near_scores.append(both[:, :length])
        far_scores.append(both[:, length:])
    return jnp.concatenate([own_scores] + near_scores + far_scores, axis=1)[None]


def solution(mesh):
    in_specs = (
        P("section", "dp", None),
        P("section", "dp", None),
        P("section", "dp", None, None),
        P("section", None),
        P("dp"),
    )
    out_specs = P("dp", "section", None)
    return jax.shard_map(body, mesh=mesh, in_specs=in_specs, out_specs=out_specs, check_vma=False)
```

```python
import functools

import jax
import jax.numpy as jnp
from jax import lax
from jax.experimental import pallas as pl
from jax.experimental.pallas import tpu as pltpu
from jax.sharding import PartitionSpec as P

HIGHEST = lax.Precision.HIGHEST
CHUNKS = 8
SKEW = 2
GROUPS = ((0, 5), (5, 8))
TRAIN_CUTS = (128, 256, 96, 32)
MIB = 1024 * 1024
ANY = pl.BlockSpec(memory_space=pl.ANY)
SMEM = pl.BlockSpec(memory_space=pltpu.SMEM)
VMEM = pl.BlockSpec(memory_space=pltpu.VMEM)


def dot(a, b, contract, precision=None):
    return lax.dot_general(
        a, b, (((1,), (contract,)), ((), ())), precision=precision, preferred_element_type=jnp.float32
    )


def parts_of(value):
    high = value.astype(jnp.bfloat16)
    return high, (value - high.astype(jnp.float32)).astype(jnp.bfloat16)


def dot_parts(a, b, contract):
    return dot(a[0], b[0], contract) + (dot(a[0], b[1], contract) + dot(a[1], b[0], contract))


def after(value, *others):
    return lax.optimization_barrier((value, *others))[0]


def partner(section, k, n_sec):
    if n_sec & (n_sec - 1) == 0:
        return section ^ k
    return lax.rem(section + k, n_sec)


def param(limit_mib):
    return pltpu.CompilerParams(vmem_limit_bytes=limit_mib * MIB)


def cost(flops, moved):
    return pl.CostEstimate(flops=flops, bytes_accessed=moved, transcendentals=0)


def invert_kernel(panel_ref, block_ref, packed_ref):
    size = block_ref.shape[0]
    count = 4
    tile = size // count
    row = lax.broadcasted_iota(jnp.int32, (tile, tile), 0)
    col = lax.broadcasted_iota(jnp.int32, (tile, tile), 1)
    spans = [slice(i * tile, (i + 1) * tile) for i in range(count)]
    low = [block_ref[s, s] for s in spans]
    inv = []
    for block in low:
        diagonal = jnp.sum(jnp.where(row == col, block, 0.0), axis=1, keepdims=True)
        inv.append(jnp.where(row == col, 1.0 / diagonal, 0.0))
    width = 1
    while width < tile:
        joins = (row // (2 * width) == col // (2 * width)) & (row // width > col // width)
        half = [dot(jnp.where(joins, low[i], 0.0), inv[i], 0, HIGHEST) for i in range(count)]
        inv = [inv[i] - dot(inv[i], half[i], 0, HIGHEST) for i in range(count)]
        width *= 2
    while len(inv) > 1:
        width = inv[0].shape[0]
        zero = jnp.zeros((width, width), jnp.float32)
        merged = []
        for i in range(0, len(inv), 2):
            below = block_ref[(i + 1) * width : (i + 2) * width, i * width : (i + 1) * width]
            corner = -dot(inv[i + 1], dot(below, inv[i], 0, HIGHEST), 0, HIGHEST)
            top = jnp.concatenate([inv[i], zero], axis=1)
            merged.append(jnp.concatenate([top, jnp.concatenate([corner, inv[i + 1]], axis=1)], axis=0))
        inv = merged
    whole = inv[0]
    mid = tile + tile // 2
    packed_ref[0:tile, :] = whole[3 * tile :, :]
    packed_ref[tile : 2 * tile, 0 : 3 * tile] = whole[2 * tile : 3 * tile, 0 : 3 * tile]
    packed_ref[tile : 2 * tile, 3 * tile :] = whole[0:tile, 0:tile]
    packed_ref[2 * tile :, 0 : 2 * tile] = whole[tile:mid, 0 : 2 * tile]
    packed_ref[2 * tile :, 2 * tile :] = whole[mid : 2 * tile, 0 : 2 * tile]


def inverted_diagonal(slot, panel):
    size = slot.shape[1]
    rows = size // 2 + size // 8
    return pl.pallas_call(
        invert_kernel,
        out_shape=jax.ShapeDtypeStruct((rows, size), jnp.float32),
        grid_spec=pltpu.PrefetchScalarGridSpec(
            num_scalar_prefetch=1,
            grid=(1,),
            in_specs=[pl.BlockSpec((size, size), lambda i, which: (which[0], 0))],
            out_specs=pl.BlockSpec((rows, size), lambda i, which: (0, 0)),
        ),
        compiler_params=param(16),
        cost_estimate=cost(4_000_000_000, 2_000_000),
    )(panel, slot)


class Stream:
    def __init__(self, panels, size):
        self.panels, self.size, self.half = panels, size, size // 2
        self.packed = (size // 2 + size // 8) // 2
        self.pieces, self.starts, start = [], [], 0
        for j in range(panels):
            for k in [*range(j + 1, panels), None]:
                self.pieces.append((j, k))
                self.starts.append(start)
                start += self.packed if k is None else self.half
        self.total = start
        self.step = start // CHUNKS

    def rows(self, piece):
        return self.packed if self.pieces[piece][1] is None else self.half

    def panel_start(self, j):
        last = self.panels - 1
        return j * self.packed + self.half * (j * last - (j * (j - 1)) // 2)

    def panel_ends(self):
        return [self.panel_start(j + 1) for j in range(self.panels)]


def build_kernel(stream, chips, info, slot, peer, packed, peer_packed, up, down, sems):
    chip, core, me = info[0], info[1], info[2]
    shift = SKEW * stream.step
    number = 0
    pending = []
    for piece, (j, k) in enumerate(stream.pieces):
        count = stream.rows(piece)
        if k is None:
            mine = packed.at[pl.ds(pl.multiple_of(core * count, 8), count)]
            theirs = peer_packed
        else:
            mine = slot.at[pl.ds(pl.multiple_of(k * stream.size + core * count, 8), count)]
            theirs = peer.at[k - 1]
        is_mine = info[4 + j] == me
        for place, out in ((chip, up), (chips - 1 - chip, down)):
            target = out.at[pl.ds(pl.multiple_of(place * shift + stream.starts[piece], 8), count)]
            own_copy = pltpu.make_async_copy(mine, target, sems.at[number])
            peer_copy = pltpu.make_async_copy(theirs, target, sems.at[number])
            pl.when(is_mine)(own_copy.start)
            pl.when(jnp.logical_not(is_mine))(peer_copy.start)
            pending.append(peer_copy)
            number += 1
    for copy in pending:
        copy.wait()


def build_streams(stream, chips, info, slot, peer, packed, peer_packed):
    rows = stream.total + SKEW * stream.step * (chips - 1)
    shape = jax.ShapeDtypeStruct((rows, stream.size), jnp.float32)
    return pl.pallas_call(
        functools.partial(build_kernel, stream, chips),
        out_shape=(shape, shape),
        in_specs=[SMEM, ANY, ANY, ANY, ANY],
        out_specs=(ANY, ANY),
        scratch_shapes=[pltpu.SemaphoreType.DMA((2 * len(stream.pieces),))],
        compiler_params=param(8),
        cost_estimate=cost(0, 16_000_000),
    )(info, slot, peer, packed, peer_packed)


def collect_kernel(stream, chips, first, last, info, up, *refs):
    sent = SKEW * (chips - 2) + last - first
    ups, downs, out, sems = refs[:sent], refs[sent : 2 * sent], refs[-2], refs[-1]
    chip = info[0]
    pending = []
    number = 0
    for i in range(first, last):
        for piece, (j, _) in enumerate(stream.pieces):
            low = max(stream.starts[piece], i * stream.step)
            high = min(stream.starts[piece] + stream.rows(piece), (i + 1) * stream.step)
            if low >= high:
                continue
            count = high - low
            origin = info[4 + j] >> 1
            target = out.at[pl.ds(low - first * stream.step, count)]
            inside = pl.ds(low - i * stream.step, count)
            start = pl.multiple_of(chip * SKEW * stream.step + low, 8)
            own_copy = pltpu.make_async_copy(up.at[pl.ds(start, count)], target, sems.at[number])
            pl.when(origin == chip)(own_copy.start)
            for p in range(1, chips):
                at = i - first + SKEW * (p - 1)
                rising = pltpu.make_async_copy(ups[at].at[inside], target, sems.at[number])
                pl.when((chip == p) & (origin < chip))(rising.start)
                falling = pltpu.make_async_copy(downs[at].at[inside], target, sems.at[number])
                pl.when((chip == chips - 1 - p) & (origin > chip))(falling.start)
            pending.append(own_copy)
            number += 1
    for copy in pending:
        copy.wait()


def collected(stream, chips, first, last, info, up, got_up, got_down):
    steps = range(first, last + SKEW * (chips - 2))
    received = [got_up[s] for s in steps] + [got_down[s] for s in steps]
    return pl.pallas_call(
        functools.partial(collect_kernel, stream, chips, first, last),
        out_shape=jax.ShapeDtypeStruct(((last - first) * stream.step, stream.size), jnp.float32),
        in_specs=[SMEM] + [ANY] * (1 + len(received)),
        out_specs=ANY,
        scratch_shapes=[pltpu.SemaphoreType.DMA(((last - first) * len(stream.pieces),))],
        compiler_params=param(8),
        cost_estimate=cost(0, 4_000_000),
    )(info, up, *received)


def sweep_kernel(stream, n_sec, info, query, *refs):
    groups = len(GROUPS)
    own, other = refs[:groups], refs[groups : 2 * groups]
    out_high, out_low, low_high, low_low, inv_high, inv_low, pending, part_high, part_low = refs[2 * groups : -2]
    arrived, sems = refs[-2:]
    core, section = info[1], info[3]
    panels, size, half = stream.panels, stream.size, stream.half
    rows = query.shape[0]
    block = rows // n_sec
    tile = size // 4
    step = stream.step

    copies = []
    for number, ((first, last), mine, theirs) in enumerate(zip(GROUPS, own, other)):
        span = pl.ds(first * step, (last - first) * step)
        for side, source in enumerate((mine, theirs)):
            copies.append(pltpu.make_async_copy(source, arrived.at[side, span], sems.at[2 * number + side]))
            copies[-1].start()

    for k in range(n_sec):
        start = pl.multiple_of(partner(section, k, n_sec) * block, block)
        for j in range(panels):
            pending[j, k * block : (k + 1) * block, :] = query[pl.ds(start, block), j * size : (j + 1) * size]

    for number, (first, last) in enumerate(GROUPS):
        for side, place in ((0, core), (1, 1 - core)):
            copies[2 * number + side].wait()

            @pl.loop(first, last)
            def _(i):
                span = pl.ds(pl.multiple_of(i * step, 16), step)
                high, low = parts_of(arrived[side, span, :])
                low_high[place, span, :] = high
                low_low[place, span, :] = low

    split = stream.packed - tile
    for j in range(panels):
        s = stream.panel_start(j + 1) - stream.packed
        for source, target in ((low_high, inv_high), (low_low, inv_low)):
            target[j] = jnp.zeros((size, size), jnp.bfloat16)
            target[j, 3 * tile :, :] = source[0, s : s + tile, :]
            target[j, 2 * tile : 2 * tile + split, : 3 * tile] = source[0, s + tile : s + tile + split, : 3 * tile]
            target[j, 2 * tile + split : 3 * tile, : 3 * tile] = source[1, s : s + tile - split, : 3 * tile]
            target[j, :split, :tile] = source[0, s + tile : s + tile + split, 3 * tile :]
            target[j, split:tile, :tile] = source[1, s : s + tile - split, 3 * tile :]
            rest = source[1, s + tile - split : s + stream.packed, :]
            target[j, tile : tile + tile // 2, : 2 * tile] = rest[:, : 2 * tile]
            target[j, tile + tile // 2 : 2 * tile, : 2 * tile] = rest[:, 2 * tile :]

    def below(j, k, h):
        start = stream.panel_start(j) + (k - j - 1) * half
        span = pl.ds(pl.multiple_of(start, 16), half)
        return low_high[h, span, :], low_low[h, span, :]

    @pl.loop(0, panels)
    def _(j):
        solved = dot_parts(parts_of(pending[j]), (inv_high[j], inv_low[j]), 1)
        pending[j] = solved
        part_high[...], part_low[...] = parts_of(solved)

        @pl.loop(j + 1, panels)
        def _(k):
            for h in range(2):
                span = slice(h * half, (h + 1) * half)
                update = dot_parts((part_high[...], part_low[...]), below(j, k, h), 1)
                pending[k, :, span] = pending[k, :, span] - update

    @pl.loop(0, panels)
    def _(step_number):
        j = panels - 1 - step_number

        @pl.loop(j + 1, panels)
        def _(k):
            update = jnp.zeros((rows, size), jnp.float32)
            for h in range(2):
                span = slice(h * half, (h + 1) * half)
                update += dot_parts((out_high[k, :, span], out_low[k, :, span]), below(j, k, h), 0)
            pending[j] = pending[j] - update

        answer = dot_parts(parts_of(pending[j]), (inv_high[j], inv_low[j]), 0)
        out_high[j], out_low[j] = parts_of(answer)


def swept(stream, n_sec, info, query, own, other):
    rows = query.shape[0]
    panels, size, total = stream.panels, stream.size, stream.total
    out = jax.ShapeDtypeStruct((panels, rows, size), jnp.bfloat16)
    return pl.pallas_call(
        functools.partial(sweep_kernel, stream, n_sec),
        out_shape=(out, out),
        in_specs=[SMEM, VMEM] + [ANY] * (len(own) + len(other)),
        out_specs=(VMEM, VMEM),
        scratch_shapes=[
            pltpu.VMEM((2, total, size), jnp.bfloat16),
            pltpu.VMEM((2, total, size), jnp.bfloat16),
            pltpu.VMEM((panels, size, size), jnp.bfloat16),
            pltpu.VMEM((panels, size, size), jnp.bfloat16),
            pltpu.VMEM((panels, rows, size), jnp.float32),
            pltpu.VMEM((rows, size), jnp.bfloat16),
            pltpu.VMEM((rows, size), jnp.bfloat16),
            pltpu.VMEM((2, total, size), jnp.float32),
            pltpu.SemaphoreType.DMA((2 * len(own),)),
        ],
        compiler_params=param(46),
        cost_estimate=cost(18_000_000_000, 20_000_000),
    )(info, query, *own, *other)


def score_kernel(n_sec, scale, first, counts, high, low, *refs):
    blocks = len(refs) - n_sec - 3
    trains, outs = refs[:blocks], refs[blocks : blocks + n_sec]
    train_high, train_low, total = refs[-3:]
    panels, rows, size = high.shape
    length = trains[0].shape[0]
    for b, train in enumerate(trains):
        for p in range(panels):
            span = slice(b * length, (b + 1) * length)
            train_high[p, span, :], train_low[p, span, :] = parts_of(train[:, p * size : (p + 1) * size])
    total[...] = jnp.zeros_like(total)

    @pl.loop(0, panels)
    def _(p):
        total[...] += dot_parts((high[p], low[p]), (train_high[p], train_low[p]), 1)

    col = lax.broadcasted_iota(jnp.int32, (1, blocks * length), 1)
    limit = jnp.full_like(col, counts[0] - first)
    for b in range(1, blocks):
        limit = jnp.where(col >= b * length, counts[b] - first + b * length, limit)
    factor = jnp.where(col < limit, scale, 0.0).astype(jnp.float32)
    share = rows // n_sec
    for k in range(n_sec):
        outs[k][...] = total[k * share : (k + 1) * share, :] * factor


def scored(n_sec, scale, first, counts, high, low, trains):
    panels, rows, size = high.shape
    cols = sum(t.shape[0] for t in trains)
    return pl.pallas_call(
        functools.partial(score_kernel, n_sec, scale, first),
        out_shape=tuple(jax.ShapeDtypeStruct((rows // n_sec, cols), jnp.float32) for _ in range(n_sec)),
        in_specs=[SMEM] + [VMEM] * (2 + len(trains)),
        out_specs=tuple(VMEM for _ in range(n_sec)),
        scratch_shapes=[
            pltpu.VMEM((panels, cols, size), jnp.bfloat16),
            pltpu.VMEM((panels, cols, size), jnp.bfloat16),
            pltpu.VMEM((rows, cols), jnp.float32),
        ],
        compiler_params=param(24),
        cost_estimate=cost(6 * panels * size * rows * cols, 4_000_000 + 12 * cols * panels * size),
    )(counts, high, low, *trains)


def body(query_gradient_stack, train_grads, factor_slots, owner, train_count):
    query, train, slot, owners = query_gradient_stack[0], train_grads[0], factor_slots[0, 0], owner[0]
    rows, coords = query.shape
    size = slot.shape[1]
    panels = coords // size
    half = size // 2
    n_dp, n_sec = lax.axis_size("dp"), lax.axis_size("section")
    chips = n_dp // 2
    stream = Stream(panels, size)
    step_rows = stream.step
    me = lax.axis_index("dp")
    section = lax.axis_index("section")
    chip, core = lax.shift_right_logical(me, 1), me & 1
    first_core = core == 0
    info = jnp.concatenate([jnp.stack([chip, core, me, section]).astype(jnp.int32), owners])

    swap_pairs = [(d, d ^ 1) for d in range(n_dp)]
    next_chip = [(d, (d + 2) % n_dp) for d in range(n_dp)]

    def swapped(value):
        return lax.ppermute(value, "dp", swap_pairs)

    cuts = [sum(TRAIN_CUTS[:i]) for i in range(len(TRAIN_CUTS) + 1)]
    train_parts = [train[a:b] for a, b in zip(cuts, cuts[1:])]
    far = [None] * len(train_parts)

    def send_train(index, *deps):
        part = after(train_parts[index], *deps) if deps else train_parts[index]
        far[index] = lax.ppermute(part, "dp", next_chip)

    count_2 = lax.ppermute(train_count, "dp", next_chip)
    count_1 = lax.ppermute(train_count, "dp", [(d, (d + 1) % n_dp) for d in range(n_dp)])
    near_counts = jnp.concatenate([count_1, count_2])
    send_train(0)

    split = slot.reshape(panels, 2, half, size)
    to_peer = jnp.where(first_core, split[1:, 1], split[1:, 0])
    peer = swapped(to_peer)
    held = jnp.argmax(owners == me).astype(jnp.int32).reshape(1)
    packed = inverted_diagonal(slot, held)
    peer_packed = swapped(jnp.where(first_core, packed[stream.packed :], packed[: stream.packed]))
    up, down = build_streams(stream, chips, info, slot, peer, packed, peer_packed)

    position = lax.broadcasted_iota(jnp.int32, up.shape[:1] + (1,), 0)
    owner_chip = lax.shift_right_logical(owners, 1)

    def origin(place):
        row = position - place * (SKEW * step_rows)
        value = jnp.broadcast_to(owner_chip[0], row.shape)
        for j, end in enumerate(stream.panel_ends()[:-1]):
            value = jnp.where(row >= end, owner_chip[j + 1], value)
        return value

    lines = []
    for place, own_rows in ((lambda z: z, up), (lambda z: chips - 1 - z, down)):
        from_before = origin(place(chip)) < chip if own_rows is up else origin(place(chip)) > chip
        lines.append((place, own_rows, from_before, {}))

    def move(line, number, *deps):
        place, own_rows, from_before, got = line
        span = slice(number * step_rows, (number + 1) * step_rows)
        block = own_rows[span]
        if number >= SKEW:
            block = jnp.where(from_before[span], after(got[number - SKEW], *deps), block)
        else:
            block = after(block, *deps)
        pairs = []
        for z in range(chips):
            if place(z) < chips - 1 and 0 <= number - SKEW * place(z) < CHUNKS:
                to = [y for y in range(chips) if place(y) == place(z) + 1][0]
                pairs += [(2 * z + c, 2 * to + c) for c in range(2)]
        got[number] = lax.ppermute(block, "dp", pairs)
        return block

    own, other = [], []
    sent = [far[0], near_counts]
    for number in range(CHUNKS + SKEW * (chips - 2)):
        sent = [move(line, number, *sent) for line in lines]
        for first, last in GROUPS:
            if number == last - 1 + SKEW * (chips - 2):
                value = collected(stream, chips, first, last, info, up, lines[0][3], lines[1][3])
                own.append(value)
                other.append(swapped(value))
    send_train(1, *sent)
    high, low = swept(stream, n_sec, info, query, own, other)
    for index in range(2, len(train_parts)):
        send_train(index, high)

    scale = (coords * n_sec) ** (-0.5)

    def summed(parts):
        total = parts[0]
        for k in range(1, n_sec):
            if n_sec & (n_sec - 1) == 0:
                pairs = [(s, s ^ k) for s in range(n_sec)]
            else:
                pairs = [(s, (s + k) % n_sec) for s in range(n_sec)]
            total = total + lax.ppermute(parts[k], "section", pairs)
        return total

    near = []
    for part, far_part in zip(train_parts, far):
        near.append(swapped(jnp.where(first_core, part, after(far_part, high))))
    parts = scored(n_sec, scale, 0, train_count, high, low, [train])
    own_scores = summed(parts)
    near_scores, far_scores = [], []
    for index, pair in enumerate(zip(near, far)):
        length = cuts[index + 1] - cuts[index]
        parts = scored(n_sec, scale, cuts[index], after(near_counts, *parts), high, low, list(pair))
        both = summed(parts)
        near_scores.append(both[:, :length])
        far_scores.append(both[:, length:])
    return jnp.concatenate([own_scores] + near_scores + far_scores, axis=1)[None]


def solution(mesh):
    in_specs = (
        P("section", "dp", None),
        P("section", "dp", None),
        P("section", "dp", None, None),
        P("section", None),
        P("dp"),
    )
    out_specs = P("dp", "section", None)
    return jax.shard_map(body, mesh=mesh, in_specs=in_specs, out_specs=out_specs, check_vma=False)
```

```python
import functools

import jax
import jax.numpy as jnp
from jax import lax
from jax.experimental import pallas as pl
from jax.experimental.pallas import tpu as pltpu
from jax.sharding import PartitionSpec as P

HIGHEST = lax.Precision.HIGHEST
CHUNKS = 17
SKEW = 2
GROUPS = ((0, 9), (9, 14), (14, 17))
TRAIN_CUTS = (128, 256, 128)
MIB = 1024 * 1024
ANY = pl.BlockSpec(memory_space=pl.ANY)
SMEM = pl.BlockSpec(memory_space=pltpu.SMEM)
VMEM = pl.BlockSpec(memory_space=pltpu.VMEM)


def dot(a, b, contract, precision=None):
    return lax.dot_general(
        a, b, (((1,), (contract,)), ((), ())), precision=precision, preferred_element_type=jnp.float32
    )


def parts_of(value):
    high = value.astype(jnp.bfloat16)
    return high, (value - high.astype(jnp.float32)).astype(jnp.bfloat16)


def dot_parts(a, b, contract):
    return dot(a[0], b[0], contract) + (dot(a[0], b[1], contract) + dot(a[1], b[0], contract))


def after(value, *others):
    return lax.optimization_barrier((value, *others))[0]


def partner(section, k, n_sec):
    if n_sec & (n_sec - 1) == 0:
        return section ^ k
    return lax.rem(section + k, n_sec)


def param(limit_mib):
    return pltpu.CompilerParams(vmem_limit_bytes=limit_mib * MIB)


def cost(flops, moved):
    return pl.CostEstimate(flops=flops, bytes_accessed=moved, transcendentals=0)


def invert_kernel(panel_ref, block_ref, packed_ref):
    size = block_ref.shape[0]
    count = 4
    tile = size // count
    row = lax.broadcasted_iota(jnp.int32, (tile, tile), 0)
    col = lax.broadcasted_iota(jnp.int32, (tile, tile), 1)
    spans = [slice(i * tile, (i + 1) * tile) for i in range(count)]
    low = [block_ref[s, s] for s in spans]
    inv = []
    for block in low:
        diagonal = jnp.sum(jnp.where(row == col, block, 0.0), axis=1, keepdims=True)
        inv.append(jnp.where(row == col, 1.0 / diagonal, 0.0))
    width = 1
    while width < tile:
        joins = (row // (2 * width) == col // (2 * width)) & (row // width > col // width)
        half = [dot(jnp.where(joins, low[i], 0.0), inv[i], 0, HIGHEST) for i in range(count)]
        inv = [inv[i] - dot(inv[i], half[i], 0, HIGHEST) for i in range(count)]
        width *= 2
    while len(inv) > 1:
        width = inv[0].shape[0]
        zero = jnp.zeros((width, width), jnp.float32)
        merged = []
        for i in range(0, len(inv), 2):
            below = block_ref[(i + 1) * width : (i + 2) * width, i * width : (i + 1) * width]
            corner = -dot(inv[i + 1], dot(below, inv[i], 0, HIGHEST), 0, HIGHEST)
            top = jnp.concatenate([inv[i], zero], axis=1)
            merged.append(jnp.concatenate([top, jnp.concatenate([corner, inv[i + 1]], axis=1)], axis=0))
        inv = merged
    whole = inv[0]
    mid = tile + tile // 2
    packed_ref[0:tile, :] = whole[3 * tile :, :]
    packed_ref[tile : 2 * tile, 0 : 3 * tile] = whole[2 * tile : 3 * tile, 0 : 3 * tile]
    packed_ref[tile : 2 * tile, 3 * tile :] = whole[0:tile, 0:tile]
    packed_ref[2 * tile :, 0 : 2 * tile] = whole[tile:mid, 0 : 2 * tile]
    packed_ref[2 * tile :, 2 * tile :] = whole[mid : 2 * tile, 0 : 2 * tile]


def inverted_diagonal(slot, panel):
    size = slot.shape[1]
    rows = size // 2 + size // 8
    return pl.pallas_call(
        invert_kernel,
        out_shape=jax.ShapeDtypeStruct((rows, size), jnp.float32),
        grid_spec=pltpu.PrefetchScalarGridSpec(
            num_scalar_prefetch=1,
            grid=(1,),
            in_specs=[pl.BlockSpec((size, size), lambda i, which: (which[0], 0))],
            out_specs=pl.BlockSpec((rows, size), lambda i, which: (0, 0)),
        ),
        compiler_params=param(16),
        cost_estimate=cost(0, 1000),
    )(panel, slot)


class Stream:
    def __init__(self, panels, size):
        self.panels, self.size = panels, size
        self.packed = size // 2 + size // 8
        self.pieces, self.starts, start = [], [], 0
        for j in range(panels):
            for k in [*range(j + 1, panels), None]:
                self.pieces.append((j, k))
                self.starts.append(start)
                start += self.packed if k is None else size
        self.total = start
        self.step = start // CHUNKS

    def rows(self, piece):
        return self.packed if self.pieces[piece][1] is None else self.size

    def panel_start(self, j):
        last = self.panels - 1
        return j * self.packed + self.size * (j * last - (j * (j - 1)) // 2)

    def cuts(self, edges):
        found = []
        for piece, (j, _) in enumerate(self.pieces):
            stop = self.starts[piece] + self.rows(piece)
            for number, (low, high) in enumerate(edges):
                low, high = max(low, self.starts[piece]), min(high, stop)
                if low < high:
                    found.append((j, number, low, high - low))
        return found


def build_kernel(stream, info, slot, peer, packed, peer_packed, out, sems):
    place, me = info[2], info[3]
    pending = []
    for piece, (j, k) in enumerate(stream.pieces):
        count = stream.rows(piece)
        mine, theirs = packed, peer_packed
        if k is not None:
            span = pl.ds(k * stream.size, count)
            mine, theirs = slot.at[span], peer.at[span]
        is_mine = info[5 + j] == me
        target = out.at[pl.ds(pl.multiple_of(place * (SKEW * stream.step) + stream.starts[piece], 8), count)]
        own_copy = pltpu.make_async_copy(mine, target, sems.at[piece])
        peer_copy = pltpu.make_async_copy(theirs, target, sems.at[piece])
        pl.when(is_mine)(own_copy.start)
        pl.when(jnp.logical_not(is_mine))(peer_copy.start)
        pending.append(peer_copy)
    for copy in pending:
        copy.wait()


def build_stream(stream, chips, info, slot, peer, packed, peer_packed):
    rows = stream.total + SKEW * stream.step * (chips - 1)
    return pl.pallas_call(
        functools.partial(build_kernel, stream),
        out_shape=jax.ShapeDtypeStruct((rows, stream.size), jnp.float32),
        in_specs=[SMEM, ANY, ANY, ANY, ANY],
        out_specs=ANY,
        scratch_shapes=[pltpu.SemaphoreType.DMA((len(stream.pieces),))],
        compiler_params=param(4),
        cost_estimate=cost(0, 1000),
    )(info, slot, peer, packed, peer_packed)


def collect_kernel(stream, chips, first, last, info, own, *refs):
    received, out, sems = refs[:-2], refs[-2], refs[-1]
    place = info[2]
    pending = []
    step = stream.step
    edges = [(i * step, (i + 1) * step) for i in range(first, last)]
    for number, (j, i, low, count) in enumerate(stream.cuts(edges)):
        here = info[5 + stream.panels + j] >= place
        target = out.at[pl.ds(low - first * step, count)]
        start = pl.multiple_of(place * (SKEW * step) + low, 8)
        own_copy = pltpu.make_async_copy(own.at[pl.ds(start, count)], target, sems.at[number])
        pl.when(here)(own_copy.start)
        for p in range(1, chips):
            source = received[i + SKEW * (p - 1)].at[pl.ds(low - (first + i) * step, count)]
            copy = pltpu.make_async_copy(source, target, sems.at[number])
            pl.when(jnp.logical_not(here) & (place == p))(copy.start)
        pending.append(own_copy)
    for copy in pending:
        copy.wait()


def collected(stream, chips, first, last, info, own, got):
    received = [got[s] for s in range(first, last + SKEW * (chips - 2))]
    return pl.pallas_call(
        functools.partial(collect_kernel, stream, chips, first, last),
        out_shape=jax.ShapeDtypeStruct(((last - first) * stream.step, stream.size), jnp.float32),
        in_specs=[SMEM] + [ANY] * (1 + len(received)),
        out_specs=ANY,
        scratch_shapes=[pltpu.SemaphoreType.DMA(((last - first) * len(stream.pieces),))],
        compiler_params=param(4),
        cost_estimate=cost(0, 1000),
    )(info, own, *received)


def sweep_kernel(stream, n_sec, info, query, *refs):
    groups = len(GROUPS)
    own, other = refs[:groups], refs[groups : 2 * groups]
    out_high, out_low, low_high, low_low, inv_high, inv_low, pending, part_high, part_low = refs[2 * groups : -2]
    arrived, sems = refs[-2:]
    place, section = info[2], info[4]
    panels, size, step = stream.panels, stream.size, stream.step
    rows = query.shape[0]
    block = rows // n_sec
    tile = size // 4

    copies = []
    for j, group, low, count in stream.cuts([(first * step, last * step) for first, last in GROUPS]):
        inside = pl.ds(low - GROUPS[group][0] * step, count)
        target = arrived.at[pl.ds(low, count)]
        number = len(copies)
        own_copy = pltpu.make_async_copy(own[group].at[inside], target, sems.at[number])
        other_copy = pltpu.make_async_copy(other[group].at[inside], target, sems.at[number])
        ahead = info[5 + panels + j] > place
        pl.when(ahead)(other_copy.start)
        pl.when(jnp.logical_not(ahead))(own_copy.start)
        copies.append((low, count, own_copy))

    for k in range(n_sec):
        start = pl.multiple_of(partner(section, k, n_sec) * block, block)
        for j in range(panels):
            pending[j, k * block : (k + 1) * block, :] = query[pl.ds(start, block), j * size : (j + 1) * size]

    for low, count, copy in copies:
        copy.wait()

        @pl.loop(0, count // 64)
        def _(i):
            span = pl.ds(pl.multiple_of(low + i * 64, 64), 64)
            low_high[span, :], low_low[span, :] = parts_of(arrived[span, :])

    for j in range(panels):
        s = stream.panel_start(j + 1) - stream.packed
        for source, target in ((low_high, inv_high), (low_low, inv_low)):
            target[j] = jnp.zeros((size, size), jnp.bfloat16)
            target[j, 3 * tile :, :] = source[s : s + tile, :]
            target[j, 2 * tile : 3 * tile, : 3 * tile] = source[s + tile : s + 2 * tile, : 3 * tile]
            target[j, :tile, :tile] = source[s + tile : s + 2 * tile, 3 * tile :]
            middle = tile + tile // 2
            target[j, tile:middle, : 2 * tile] = source[s + 2 * tile : s + stream.packed, : 2 * tile]
            target[j, middle : 2 * tile, : 2 * tile] = source[s + 2 * tile : s + stream.packed, 2 * tile :]

    def below(j, k):
        span = pl.ds(pl.multiple_of(stream.panel_start(j) + (k - j - 1) * size, 64), size)
        return low_high[span, :], low_low[span, :]

    @pl.loop(0, panels)
    def _(j):
        solved = dot_parts(parts_of(pending[j]), (inv_high[j], inv_low[j]), 1)
        pending[j] = solved
        part_high[...], part_low[...] = parts_of(solved)

        @pl.loop(j + 1, panels)
        def _(k):
            pending[k] = pending[k] - dot_parts((part_high[...], part_low[...]), below(j, k), 1)

    @pl.loop(0, panels)
    def _(step_number):
        j = panels - 1 - step_number

        @pl.loop(j + 1, panels)
        def _(k):
            pending[j] = pending[j] - dot_parts((out_high[k], out_low[k]), below(j, k), 0)

        answer = dot_parts(parts_of(pending[j]), (inv_high[j], inv_low[j]), 0)
        out_high[j], out_low[j] = parts_of(answer)


def swept(stream, n_sec, info, query, own, other):
    rows = query.shape[0]
    panels, size, total = stream.panels, stream.size, stream.total
    out = jax.ShapeDtypeStruct((panels, rows, size), jnp.bfloat16)
    return pl.pallas_call(
        functools.partial(sweep_kernel, stream, n_sec),
        out_shape=(out, out),
        in_specs=[SMEM, VMEM] + [ANY] * (len(own) + len(other)),
        out_specs=(VMEM, VMEM),
        scratch_shapes=[
            pltpu.VMEM((total, size), jnp.bfloat16),
            pltpu.VMEM((total, size), jnp.bfloat16),
            pltpu.VMEM((panels, size, size), jnp.bfloat16),
            pltpu.VMEM((panels, size, size), jnp.bfloat16),
            pltpu.VMEM((panels, rows, size), jnp.float32),
            pltpu.VMEM((rows, size), jnp.bfloat16),
            pltpu.VMEM((rows, size), jnp.bfloat16),
            pltpu.VMEM((total, size), jnp.float32),
            pltpu.SemaphoreType.DMA((len(stream.pieces) + len(GROUPS),)),
        ],
        compiler_params=param(46),
        cost_estimate=cost(0, 1000),
    )(info, query, *own, *other)


def score_kernel(n_sec, scale, first, counts, high, low, *refs):
    blocks = len(refs) - n_sec - 3
    trains, outs = refs[:blocks], refs[blocks : blocks + n_sec]
    train_high, train_low, total = refs[-3:]
    panels, rows, size = high.shape
    length = trains[0].shape[0]
    for b, train in enumerate(trains):
        for p in range(panels):
            span = slice(b * length, (b + 1) * length)
            train_high[p, span, :], train_low[p, span, :] = parts_of(train[:, p * size : (p + 1) * size])
    total[...] = jnp.zeros_like(total)

    @pl.loop(0, panels)
    def _(p):
        total[...] += dot_parts((high[p], low[p]), (train_high[p], train_low[p]), 1)

    col = lax.broadcasted_iota(jnp.int32, (1, blocks * length), 1)
    limit = jnp.full_like(col, counts[0] - first)
    for b in range(1, blocks):
        limit = jnp.where(col >= b * length, counts[b] - first + b * length, limit)
    factor = jnp.where(col < limit, scale, 0.0).astype(jnp.float32)
    share = rows // n_sec
    for k in range(n_sec):
        outs[k][...] = total[k * share : (k + 1) * share, :] * factor


def scored(n_sec, scale, first, counts, high, low, trains):
    panels, rows, size = high.shape
    cols = sum(t.shape[0] for t in trains)
    return pl.pallas_call(
        functools.partial(score_kernel, n_sec, scale, first),
        out_shape=tuple(jax.ShapeDtypeStruct((rows // n_sec, cols), jnp.float32) for _ in range(n_sec)),
        in_specs=[SMEM] + [VMEM] * (2 + len(trains)),
        out_specs=tuple(VMEM for _ in range(n_sec)),
        scratch_shapes=[
            pltpu.VMEM((panels, cols, size), jnp.bfloat16),
            pltpu.VMEM((panels, cols, size), jnp.bfloat16),
            pltpu.VMEM((rows, cols), jnp.float32),
        ],
        compiler_params=param(24),
        cost_estimate=cost(0, 1000),
    )(counts, high, low, *trains)


def body(query_gradient_stack, train_grads, factor_slots, owner, train_count):
    query, train, slot, owners = query_gradient_stack[0], train_grads[0], factor_slots[0, 0], owner[0]
    rows, coords = query.shape
    size = slot.shape[1]
    panels = coords // size
    n_dp, n_sec = lax.axis_size("dp"), lax.axis_size("section")
    chips = n_dp // 2
    stream = Stream(panels, size)
    step_rows = stream.step
    me = lax.axis_index("dp")
    section = lax.axis_index("section")
    chip, core = lax.shift_right_logical(me, 1), me & 1
    first_core = core == 0
    place = jnp.where(first_core, chip, chips - 1 - chip)
    owner_chip = lax.shift_right_logical(owners, 1)
    owner_place = jnp.where(first_core, owner_chip, chips - 1 - owner_chip)
    info = jnp.concatenate([jnp.stack([chip, core, place, me, section]), owners, owner_place])

    swap_pairs = [(d, d ^ 1) for d in range(n_dp)]
    next_chip = [(d, (d + 2) % n_dp) for d in range(n_dp)]

    def swapped(value):
        return lax.ppermute(value, "dp", swap_pairs)

    cuts = [sum(TRAIN_CUTS[:i]) for i in range(len(TRAIN_CUTS) + 1)]
    train_parts = [train[a:b] for a, b in zip(cuts, cuts[1:])]
    far = [None] * len(train_parts)

    def send_train(index, *deps):
        part = after(train_parts[index], *deps) if deps else train_parts[index]
        far[index] = lax.ppermute(part, "dp", next_chip)

    send_train(0)
    slot, train_count, owners = lax.optimization_barrier((slot, train_count, owners, train_parts[0]))[:3]
    count_2 = lax.ppermute(train_count, "dp", next_chip)
    count_1 = lax.ppermute(train_count, "dp", [(d, (d + 1) % n_dp) for d in range(n_dp)])
    near_counts = jnp.concatenate([count_1, count_2])

    peer = swapped(slot)
    held = jnp.argmax(owners == me).astype(jnp.int32).reshape(1)
    packed = inverted_diagonal(slot, held)
    own_rows = build_stream(stream, chips, info, slot, peer, packed, swapped(packed))

    row = lax.broadcasted_iota(jnp.int32, own_rows.shape[:1] + (1,), 0) - place * (SKEW * step_rows)
    origin = jnp.broadcast_to(owner_place[0], row.shape)
    for j in range(1, panels):
        origin = jnp.where(row >= stream.panel_start(j), owner_place[j], origin)
    from_before = origin < place

    got, own, other = {}, [], []
    sent = [far[0], near_counts]
    for number in range(CHUNKS + SKEW * (chips - 2)):
        span = slice(number * step_rows, (number + 1) * step_rows)
        if number >= SKEW:
            block = jnp.where(from_before[span], after(got[number - SKEW], *sent), own_rows[span])
        else:
            block = after(own_rows[span], *sent)
        pairs = []
        for p in range(chips - 1):
            if 0 <= number - SKEW * p < CHUNKS:
                pairs += [(2 * p, 2 * p + 2), (2 * (chips - 1 - p) + 1, 2 * (chips - 2 - p) + 1)]
        got[number] = lax.ppermute(block, "dp", pairs)
        sent = [block]
        for first, last in GROUPS:
            if number == last - 1 + SKEW * (chips - 2):
                value = collected(stream, chips, first, last, info, own_rows, got)
                own.append(value)
                other.append(swapped(value))
    send_train(1, *sent)
    high, low = swept(stream, n_sec, info, query, own, other)
    for index in range(2, len(train_parts)):
        send_train(index, high)

    scale = (coords * n_sec) ** (-0.5)

    def summed(parts):
        total = parts[0]
        for k in range(1, n_sec):
            if n_sec & (n_sec - 1) == 0:
                pairs = [(s, s ^ k) for s in range(n_sec)]
            else:
                pairs = [(s, (s + k) % n_sec) for s in range(n_sec)]
            total = total + lax.ppermute(parts[k], "section", pairs)
        return total

    parts = scored(n_sec, scale, 0, train_count, high, low, [train])
    own_scores = summed(parts)
    near_scores, far_scores = [], []
    for index, (part, far_part) in enumerate(zip(train_parts, far)):
        near_part = swapped(jnp.where(first_core, part, after(far_part, high if index < 2 else parts[0])))
        length = cuts[index + 1] - cuts[index]
        parts = scored(n_sec, scale, cuts[index], after(near_counts, parts[0]), high, low, [near_part, far_part])
        both = summed(parts)
        near_scores.append(both[:, :length])
        far_scores.append(both[:, length:])
    return jnp.concatenate([own_scores] + near_scores + far_scores, axis=1)[None]


def solution(mesh):
    in_specs = (
        P("section", "dp", None),
        P("section", "dp", None),
        P("section", "dp", None, None),
        P("section", None),
        P("dp"),
    )
    out_specs = P("dp", "section", None)
    return jax.shard_map(body, mesh=mesh, in_specs=in_specs, out_specs=out_specs, check_vma=False)
```

```python
import functools

import jax
import jax.numpy as jnp
from jax import lax
from jax.experimental import pallas as pl
from jax.experimental.pallas import tpu as pltpu
from jax.sharding import PartitionSpec as P

HIGHEST = lax.Precision.HIGHEST
CHUNKS = 17
SKEW = 2
GROUPS = ((0, 9), (9, 14), (14, 17))
TRAIN_CUTS = (96, 256, 160)
MIB = 1024 * 1024
HBM = pl.BlockSpec(memory_space=pltpu.HBM)
SMEM = pl.BlockSpec(memory_space=pltpu.SMEM)
VMEM = pl.BlockSpec(memory_space=pltpu.VMEM)


def dot(a, b, contract, precision=None):
    return lax.dot_general(
        a, b, (((1,), (contract,)), ((), ())), precision=precision, preferred_element_type=jnp.float32
    )


def parts_of(value):
    high = value.astype(jnp.bfloat16)
    return high, (value - high.astype(jnp.float32)).astype(jnp.bfloat16)


def dot_parts(a, b, contract):
    return dot(a[0], b[0], contract) + (dot(a[0], b[1], contract) + dot(a[1], b[0], contract))


def partner(section, k, n_sec):
    if n_sec & (n_sec - 1) == 0:
        return section ^ k
    return lax.rem(section + k, n_sec)


def param(limit_mib):
    return pltpu.CompilerParams(vmem_limit_bytes=limit_mib * MIB)


def cost(flops, moved):
    return pl.CostEstimate(flops=flops, bytes_accessed=moved, transcendentals=0)


def copy_kernel(start, source, *refs):
    out, sem = refs[-2:]
    copy = pltpu.make_async_copy(source.at[pl.ds(start, out.shape[0])], out, sem)
    copy.start()
    copy.wait()


def copied(source, start, length, *earlier):
    return pl.pallas_call(
        functools.partial(copy_kernel, start),
        out_shape=jax.ShapeDtypeStruct((length, source.shape[1]), source.dtype),
        in_specs=[HBM] * (1 + len(earlier)),
        out_specs=HBM,
        scratch_shapes=[pltpu.SemaphoreType.DMA],
        compiler_params=param(4),
        cost_estimate=cost(0, 1000),
    )(source, *earlier)


def choose_kernel(start, info, train, far, *refs):
    out, sem = refs[-2:]
    own_copy = pltpu.make_async_copy(train.at[pl.ds(start, out.shape[0])], out, sem)
    far_copy = pltpu.make_async_copy(far, out, sem)
    pl.when(info[1] == 0)(own_copy.start)
    pl.when(info[1] != 0)(far_copy.start)
    own_copy.wait()


def chosen(info, train, start, far, *earlier):
    return pl.pallas_call(
        functools.partial(choose_kernel, start),
        out_shape=jax.ShapeDtypeStruct(far.shape, far.dtype),
        in_specs=[SMEM] + [HBM] * (2 + len(earlier)),
        out_specs=HBM,
        scratch_shapes=[pltpu.SemaphoreType.DMA],
        compiler_params=param(4),
        cost_estimate=cost(0, 1000),
    )(info, train, far, *earlier)


def corner(value):
    return value[:8, :128]


def invert_kernel(panels, info, slot, packed_ref, block_ref, sem):
    size = block_ref.shape[0]
    held = 0
    for j in range(1, panels):
        held = jnp.where(info[5 + j] == info[3], j, held)
    copy = pltpu.make_async_copy(slot.at[pl.ds(pl.multiple_of(held * size, size), size)], block_ref, sem)
    copy.start()
    copy.wait()
    count = 4
    tile = size // count
    row = lax.broadcasted_iota(jnp.int32, (tile, tile), 0)
    col = lax.broadcasted_iota(jnp.int32, (tile, tile), 1)
    spans = [slice(i * tile, (i + 1) * tile) for i in range(count)]
    low = [block_ref[s, s] for s in spans]
    inv = []
    for block in low:
        diagonal = jnp.sum(jnp.where(row == col, block, 0.0), axis=1, keepdims=True)
        inv.append(jnp.where(row == col, 1.0 / diagonal, 0.0))
    width = 1
    while width < tile:
        joins = (row // (2 * width) == col // (2 * width)) & (row // width > col // width)
        half = [dot(jnp.where(joins, low[i], 0.0), inv[i], 0, HIGHEST) for i in range(count)]
        inv = [inv[i] - dot(inv[i], half[i], 0, HIGHEST) for i in range(count)]
        width *= 2
    while len(inv) > 1:
        width = inv[0].shape[0]
        zero = jnp.zeros((width, width), jnp.float32)
        merged = []
        for i in range(0, len(inv), 2):
            below = block_ref[(i + 1) * width : (i + 2) * width, i * width : (i + 1) * width]
            corner = -dot(inv[i + 1], dot(below, inv[i], 0, HIGHEST), 0, HIGHEST)
            top = jnp.concatenate([inv[i], zero], axis=1)
            merged.append(jnp.concatenate([top, jnp.concatenate([corner, inv[i + 1]], axis=1)], axis=0))
        inv = merged
    whole = inv[0]
    mid = tile + tile // 2
    packed_ref[0:tile, :] = whole[3 * tile :, :]
    packed_ref[tile : 2 * tile, 0 : 3 * tile] = whole[2 * tile : 3 * tile, 0 : 3 * tile]
    packed_ref[tile : 2 * tile, 3 * tile :] = whole[0:tile, 0:tile]
    packed_ref[2 * tile :, 0 : 2 * tile] = whole[tile:mid, 0 : 2 * tile]
    packed_ref[2 * tile :, 2 * tile :] = whole[mid : 2 * tile, 0 : 2 * tile]


def inverted_diagonal(panels, info, slot):
    size = slot.shape[1]
    rows = size // 2 + size // 8
    return pl.pallas_call(
        functools.partial(invert_kernel, panels),
        out_shape=jax.ShapeDtypeStruct((rows, size), jnp.float32),
        in_specs=[SMEM, HBM],
        out_specs=VMEM,
        scratch_shapes=[pltpu.VMEM((size, size), jnp.float32), pltpu.SemaphoreType.DMA],
        compiler_params=param(16),
        cost_estimate=cost(0, 1000),
    )(info, slot)


class Stream:
    def __init__(self, panels, size):
        self.panels, self.size = panels, size
        self.packed = size // 2 + size // 8
        self.pieces, self.starts, start = [], [], 0
        for j in range(panels):
            for k in [*range(j + 1, panels), None]:
                self.pieces.append((j, k))
                self.starts.append(start)
                start += self.packed if k is None else size
        self.total = start
        self.step = start // CHUNKS

    def rows(self, piece):
        return self.packed if self.pieces[piece][1] is None else self.size

    def panel_start(self, j):
        last = self.panels - 1
        return j * self.packed + self.size * (j * last - (j * (j - 1)) // 2)

    def cuts(self, edges):
        found = []
        for piece, (j, _) in enumerate(self.pieces):
            stop = self.starts[piece] + self.rows(piece)
            for number, (low, high) in enumerate(edges):
                low, high = max(low, self.starts[piece]), min(high, stop)
                if low < high:
                    found.append((j, number, low, high - low))
        return found


def build_kernel(stream, info, slot, peer, packed, peer_packed, earlier, out, sems):
    place, me = info[2], info[3]
    pending = []
    for piece, (j, k) in enumerate(stream.pieces):
        count = stream.rows(piece)
        mine, theirs = packed, peer_packed
        if k is not None:
            span = pl.ds(k * stream.size, count)
            mine, theirs = slot.at[span], peer.at[span]
        is_mine = info[5 + j] == me
        target = out.at[pl.ds(pl.multiple_of(place * (SKEW * stream.step) + stream.starts[piece], 8), count)]
        own_copy = pltpu.make_async_copy(mine, target, sems.at[piece])
        peer_copy = pltpu.make_async_copy(theirs, target, sems.at[piece])
        pl.when(is_mine)(own_copy.start)
        pl.when(jnp.logical_not(is_mine))(peer_copy.start)
        pending.append(peer_copy)
    for copy in pending:
        copy.wait()


def build_stream(stream, chips, info, slot, peer, packed, peer_packed, earlier):
    rows = stream.total + SKEW * stream.step * (chips - 1)
    return pl.pallas_call(
        functools.partial(build_kernel, stream),
        out_shape=jax.ShapeDtypeStruct((rows, stream.size), jnp.float32),
        in_specs=[SMEM] + [HBM] * 5,
        out_specs=HBM,
        scratch_shapes=[pltpu.SemaphoreType.DMA((len(stream.pieces),))],
        compiler_params=param(4),
        cost_estimate=cost(0, 1000),
    )(info, slot, peer, packed, peer_packed, earlier)


def step_kernel(stream, number, info, own, *refs):
    out, sems = refs[-2:]
    unit = stream.packed // 5
    place = info[2]
    pending = []
    for g in range(stream.step // unit):
        inside = pl.ds(g * unit, unit)
        copy = pltpu.make_async_copy(
            own.at[pl.ds(number * stream.step + g * unit, unit)], out.at[inside], sems.at[g]
        )
        pending.append(copy)
        if number < SKEW:
            copy.start()
            continue
        row = number * stream.step + g * unit - place * (SKEW * stream.step)
        origin = info[5 + stream.panels]
        for j in range(1, stream.panels):
            origin = jnp.where(row >= stream.panel_start(j), info[5 + stream.panels + j], origin)
        passing = pltpu.make_async_copy(refs[0].at[inside], out.at[inside], sems.at[g])
        pl.when(origin < place)(passing.start)
        pl.when(origin >= place)(copy.start)
    for copy in pending:
        copy.wait()


def step_block(stream, number, info, own, got, earlier):
    operands = ([got[number - SKEW]] if number >= SKEW else []) + earlier
    return pl.pallas_call(
        functools.partial(step_kernel, stream, number),
        out_shape=jax.ShapeDtypeStruct((stream.step, stream.size), jnp.float32),
        in_specs=[SMEM] + [HBM] * (1 + len(operands)),
        out_specs=HBM,
        scratch_shapes=[pltpu.SemaphoreType.DMA((stream.step * 5 // stream.packed,))],
        compiler_params=param(4),
        cost_estimate=cost(0, 1000),
    )(info, own, *operands)


def collect_kernel(stream, chips, first, last, info, counts, own, *refs):
    received, out, sems = refs[:-2], refs[-2], refs[-1]
    place = info[2]
    pending = []
    step = stream.step
    edges = [(i * step, (i + 1) * step) for i in range(first, last)]
    for number, (j, i, low, count) in enumerate(stream.cuts(edges)):
        here = info[5 + stream.panels + j] >= place
        target = out.at[pl.ds(low - first * step, count)]
        start = pl.multiple_of(place * (SKEW * step) + low, 8)
        own_copy = pltpu.make_async_copy(own.at[pl.ds(start, count)], target, sems.at[number])
        pl.when(here)(own_copy.start)
        for p in range(1, chips):
            source = received[i + SKEW * (p - 1)].at[pl.ds(low - (first + i) * step, count)]
            copy = pltpu.make_async_copy(source, target, sems.at[number])
            pl.when(jnp.logical_not(here) & (place == p))(copy.start)
        pending.append(own_copy)
    for copy in pending:
        copy.wait()


def collected(stream, chips, first, last, info, counts, own, got):
    received = [got[s] for s in range(first, last + SKEW * (chips - 2))]
    return pl.pallas_call(
        functools.partial(collect_kernel, stream, chips, first, last),
        out_shape=jax.ShapeDtypeStruct(((last - first) * stream.step, stream.size), jnp.float32),
        in_specs=[SMEM, SMEM] + [HBM] * (1 + len(received)),
        out_specs=HBM,
        scratch_shapes=[pltpu.SemaphoreType.DMA(((last - first) * len(stream.pieces),))],
        compiler_params=param(4),
        cost_estimate=cost(0, 1000),
    )(info, counts, own, *received)


def sweep_kernel(stream, n_sec, info, earlier, query, *refs):
    groups = len(GROUPS)
    own, other = refs[:groups], refs[groups : 2 * groups]
    out_high, out_low, done_ref, low_high, low_low, inv_high, inv_low, pending, part_high, part_low = refs[2 * groups : -2]
    arrived, sems = refs[-2:]
    done_ref[...] = jnp.zeros_like(done_ref)
    place, section = info[2], info[4]
    panels, size, step = stream.panels, stream.size, stream.step
    rows = query.shape[0]
    block = rows // n_sec
    tile = size // 4

    slots = arrived.shape[0]
    found = stream.cuts([(first * step, last * step) for first, last in GROUPS])
    copies = []

    def fetch(number):
        j, group, low, count = found[number]
        inside = pl.ds(low - GROUPS[group][0] * step, count)
        target = arrived.at[number % slots, pl.ds(0, count)]
        own_copy = pltpu.make_async_copy(own[group].at[inside], target, sems.at[number])
        other_copy = pltpu.make_async_copy(other[group].at[inside], target, sems.at[number])
        ahead = info[5 + panels + j] > place
        pl.when(ahead)(other_copy.start)
        pl.when(jnp.logical_not(ahead))(own_copy.start)
        copies.append(own_copy)

    for number in range(slots):
        fetch(number)

    for k in range(n_sec):
        start = pl.multiple_of(partner(section, k, n_sec) * block, block)
        for j in range(panels):
            pending[j, k * block : (k + 1) * block, :] = query[pl.ds(start, block), j * size : (j + 1) * size]

    for number, (_, _, low, count) in enumerate(found):
        copies[number].wait()

        @pl.loop(0, count // 64)
        def _(i):
            inside = pl.ds(pl.multiple_of(i * 64, 64), 64)
            span = pl.ds(pl.multiple_of(low + i * 64, 64), 64)
            low_high[span, :], low_low[span, :] = parts_of(arrived[number % slots, inside, :])

        if number + slots < len(found):
            fetch(number + slots)

    for j in range(panels):
        s = stream.panel_start(j + 1) - stream.packed
        for source, target in ((low_high, inv_high), (low_low, inv_low)):
            target[j] = jnp.zeros((size, size), jnp.bfloat16)
            target[j, 3 * tile :, :] = source[s : s + tile, :]
            target[j, 2 * tile : 3 * tile, : 3 * tile] = source[s + tile : s + 2 * tile, : 3 * tile]
            target[j, :tile, :tile] = source[s + tile : s + 2 * tile, 3 * tile :]
            middle = tile + tile // 2
            target[j, tile:middle, : 2 * tile] = source[s + 2 * tile : s + stream.packed, : 2 * tile]
            target[j, middle : 2 * tile, : 2 * tile] = source[s + 2 * tile : s + stream.packed, 2 * tile :]

    def below(j, k):
        span = pl.ds(pl.multiple_of(stream.panel_start(j) + (k - j - 1) * size, 64), size)
        return low_high[span, :], low_low[span, :]

    @pl.loop(0, panels)
    def _(j):
        solved = dot_parts(parts_of(pending[j]), (inv_high[j], inv_low[j]), 1)
        pending[j] = solved
        part_high[...], part_low[...] = parts_of(solved)

        @pl.loop(j + 1, panels)
        def _(k):
            pending[k] = pending[k] - dot_parts((part_high[...], part_low[...]), below(j, k), 1)

    @pl.loop(0, panels)
    def _(step_number):
        j = panels - 1 - step_number

        @pl.loop(j + 1, panels)
        def _(k):
            pending[j] = pending[j] - dot_parts((out_high[k], out_low[k]), below(j, k), 0)

        answer = dot_parts(parts_of(pending[j]), (inv_high[j], inv_low[j]), 0)
        out_high[j], out_low[j] = parts_of(answer)


def swept(stream, n_sec, info, earlier, query, own, other):
    rows = query.shape[0]
    panels, size, total = stream.panels, stream.size, stream.total
    out = jax.ShapeDtypeStruct((panels, rows, size), jnp.bfloat16)
    return pl.pallas_call(
        functools.partial(sweep_kernel, stream, n_sec),
        out_shape=(out, out, jax.ShapeDtypeStruct((8, 128), jnp.float32)),
        in_specs=[SMEM, HBM, VMEM] + [HBM] * (len(own) + len(other)),
        out_specs=(VMEM, VMEM, VMEM),
        scratch_shapes=[
            pltpu.VMEM((total, size), jnp.bfloat16),
            pltpu.VMEM((total, size), jnp.bfloat16),
            pltpu.VMEM((panels, size, size), jnp.bfloat16),
            pltpu.VMEM((panels, size, size), jnp.bfloat16),
            pltpu.VMEM((panels, rows, size), jnp.float32),
            pltpu.VMEM((rows, size), jnp.bfloat16),
            pltpu.VMEM((rows, size), jnp.bfloat16),
            pltpu.VMEM((4, size, size), jnp.float32),
            pltpu.SemaphoreType.DMA((len(stream.pieces) + len(GROUPS),)),
        ],
        compiler_params=param(40),
        cost_estimate=cost(0, 1000),
    )(info, earlier, query, *own, *other)


def score_kernel(n_sec, scale, first, counts, earlier, high, low, *refs):
    blocks = len(refs) - n_sec - 3
    trains, outs = refs[:blocks], refs[blocks : blocks + n_sec]
    train_high, train_low, total = refs[-3:]
    panels, rows, size = high.shape
    length = trains[0].shape[0]
    for b, train in enumerate(trains):
        for p in range(panels):
            span = slice(b * length, (b + 1) * length)
            train_high[p, span, :], train_low[p, span, :] = parts_of(train[:, p * size : (p + 1) * size])
    total[...] = jnp.zeros_like(total)

    @pl.loop(0, panels)
    def _(p):
        total[...] += dot_parts((high[p], low[p]), (train_high[p], train_low[p]), 1)

    col = lax.broadcasted_iota(jnp.int32, (1, blocks * length), 1)
    limit = jnp.full_like(col, counts[0] - first)
    for b in range(1, blocks):
        limit = jnp.where(col >= b * length, counts[b] - first + b * length, limit)
    factor = jnp.where(col < limit, scale, 0.0).astype(jnp.float32)
    share = rows // n_sec
    for k in range(n_sec):
        outs[k][...] = total[k * share : (k + 1) * share, :] * factor


def scored(n_sec, scale, first, counts, earlier, high, low, trains):
    panels, rows, size = high.shape
    cols = sum(t.shape[0] for t in trains)
    return pl.pallas_call(
        functools.partial(score_kernel, n_sec, scale, first),
        out_shape=tuple(jax.ShapeDtypeStruct((rows // n_sec, cols), jnp.float32) for _ in range(n_sec)),
        in_specs=[SMEM, HBM] + [VMEM] * (2 + len(trains)),
        out_specs=tuple(VMEM for _ in range(n_sec)),
        scratch_shapes=[
            pltpu.VMEM((panels, cols, size), jnp.bfloat16),
            pltpu.VMEM((panels, cols, size), jnp.bfloat16),
            pltpu.VMEM((rows, cols), jnp.float32),
        ],
        compiler_params=param(24),
        cost_estimate=cost(0, 1000),
    )(counts, earlier, high, low, *trains)


def body(query_gradient_stack, train_grads, factor_slots, owner, train_count):
    query, train, slot, owners = query_gradient_stack[0], train_grads[0], factor_slots[0, 0], owner[0]
    rows, coords = query.shape
    size = slot.shape[1]
    panels = coords // size
    n_dp, n_sec = lax.axis_size("dp"), lax.axis_size("section")
    chips = n_dp // 2
    stream = Stream(panels, size)
    me = lax.axis_index("dp")
    section = lax.axis_index("section")
    chip, core = lax.shift_right_logical(me, 1), me & 1
    first_core = core == 0
    place = jnp.where(first_core, chip, chips - 1 - chip)
    owner_chip = lax.shift_right_logical(owners, 1)
    owner_place = jnp.where(first_core, owner_chip, chips - 1 - owner_chip)
    info = jnp.concatenate([jnp.stack([chip, core, place, me, section]), owners, owner_place])

    swap_pairs = [(d, d ^ 1) for d in range(n_dp)]
    next_chip = [(d, (d + 2) % n_dp) for d in range(n_dp)]

    def swapped(value):
        return lax.ppermute(value, "dp", swap_pairs)

    cuts = [sum(TRAIN_CUTS[:i]) for i in range(len(TRAIN_CUTS) + 1)]
    first_part, slot = lax.optimization_barrier((train[: cuts[1]], slot))
    far = [lax.ppermute(first_part, "dp", next_chip)]

    def send_train(index, *earlier):
        part = copied(train, cuts[index], cuts[index + 1] - cuts[index], *earlier)
        far.append(lax.ppermute(part, "dp", next_chip))
        return part

    peer = swapped(slot)
    packed = inverted_diagonal(panels, info, slot)
    own_rows = build_stream(stream, chips, info, slot, peer, packed, swapped(packed), corner(far[0]))
    count_2 = lax.ppermute(train_count, "dp", next_chip)
    count_1 = lax.ppermute(train_count, "dp", [(d, (d + 1) % n_dp) for d in range(n_dp)])
    near_counts = jnp.concatenate([count_1, count_2])

    got, own, other = {}, [], []
    steps = CHUNKS + SKEW * (chips - 2)
    for number in range(steps):
        block = step_block(stream, number, info, own_rows, got, [] if number == 0 else [block])
        pairs = []
        for p in range(chips - 1):
            if 0 <= number - SKEW * p < CHUNKS:
                pairs += [(2 * p, 2 * p + 2), (2 * (chips - 1 - p) + 1, 2 * (chips - 2 - p) + 1)]
        got[number] = lax.ppermute(block, "dp", pairs)
        for first, last in GROUPS:
            if number == last - 1 + SKEW * (chips - 2):
                value = collected(stream, chips, first, last, info, near_counts, own_rows, got)
                own.append(value)
                other.append(swapped(value))

    part = send_train(1, swapped(corner(got[steps - 1]) + corner(got[steps - 2])))
    high, low, swept_token = swept(stream, n_sec, info, corner(part), query, own, other)
    send_train(2, swept_token)

    scale = (coords * n_sec) ** (-0.5)

    def summed(parts):
        total = parts[0]
        for k in range(1, n_sec):
            if n_sec & (n_sec - 1) == 0:
                pairs = [(s, s ^ k) for s in range(n_sec)]
            else:
                pairs = [(s, (s + k) % n_sec) for s in range(n_sec)]
            total = total + lax.ppermute(parts[k], "section", pairs)
        return total

    parts = scored(n_sec, scale, 0, train_count, swept_token, high, low, [train])
    own_scores = summed(parts)
    near_scores, far_scores, earlier = [], [], [corner(own_scores)]
    for index, far_part in enumerate(far):
        last = index + 1 == len(far)
        near_part = swapped(chosen(info, train, cuts[index], far_part, *(earlier if last else [swept_token])))
        length = cuts[index + 1] - cuts[index]
        parts = scored(
            n_sec, scale, cuts[index], near_counts, corner(parts[0]), high, low, [near_part, far_part]
        )
        both = summed(parts)
        earlier.append(corner(both))
        near_scores.append(both[:, :length])
        far_scores.append(both[:, length:])
    return jnp.concatenate([own_scores] + near_scores + far_scores, axis=1)[None]


def solution(mesh):
    in_specs = (
        P("section", "dp", None),
        P("section", "dp", None),
        P("section", "dp", None, None),
        P("section", None),
        P("dp"),
    )
    out_specs = P("dp", "section", None)
    return jax.shard_map(body, mesh=mesh, in_specs=in_specs, out_specs=out_specs, check_vma=False)
```

```python
import functools

import jax
import jax.numpy as jnp
from jax import lax
from jax.experimental import pallas as pl
from jax.experimental.pallas import tpu as pltpu
from jax.sharding import PartitionSpec as P

HIGHEST = lax.Precision.HIGHEST
CHUNKS = 17
SKEW = 2
GROUPS = ((0, 9), (9, 14), (14, 17))
TRAIN_CUTS = (96, 320, 96)
MIB = 1024 * 1024
HBM = pl.BlockSpec(memory_space=pltpu.HBM)
SMEM = pl.BlockSpec(memory_space=pltpu.SMEM)
VMEM = pl.BlockSpec(memory_space=pltpu.VMEM)


def dot(a, b, contract, precision=None):
    return lax.dot_general(
        a, b, (((1,), (contract,)), ((), ())), precision=precision, preferred_element_type=jnp.float32
    )


def parts_of(value):
    high = value.astype(jnp.bfloat16)
    return high, (value - high.astype(jnp.float32)).astype(jnp.bfloat16)


def dot_parts(a, b, contract):
    return dot(a[0], b[0], contract) + (dot(a[0], b[1], contract) + dot(a[1], b[0], contract))


def partner(section, k, n_sec):
    if n_sec & (n_sec - 1) == 0:
        return section ^ k
    return lax.rem(section + k, n_sec)


def param(limit_mib):
    return pltpu.CompilerParams(vmem_limit_bytes=limit_mib * MIB)


def cost(flops, moved):
    return pl.CostEstimate(flops=flops, bytes_accessed=moved, transcendentals=0)


def order_kernel(*refs):
    del refs


def ordered(value, *earlier):
    return pl.pallas_call(
        order_kernel,
        out_shape=jax.ShapeDtypeStruct(value.shape, value.dtype),
        in_specs=[HBM] * (1 + len(earlier)),
        out_specs=HBM,
        input_output_aliases={0: 0},
        cost_estimate=cost(0, 1000),
    )(value, *earlier)


def choose_kernel(start, info, train, far, *refs):
    out, sem = refs[-2:]
    own_copy = pltpu.make_async_copy(train.at[pl.ds(start, out.shape[0])], out, sem)
    far_copy = pltpu.make_async_copy(far, out, sem)
    pl.when(info[1] == 0)(own_copy.start)
    pl.when(info[1] != 0)(far_copy.start)
    own_copy.wait()


def chosen(info, train, start, far, *earlier):
    return pl.pallas_call(
        functools.partial(choose_kernel, start),
        out_shape=jax.ShapeDtypeStruct(far.shape, far.dtype),
        in_specs=[SMEM] + [HBM] * (2 + len(earlier)),
        out_specs=HBM,
        scratch_shapes=[pltpu.SemaphoreType.DMA],
        compiler_params=param(4),
        cost_estimate=cost(0, 1000),
    )(info, train, far, *earlier)


def corner(value):
    return value[:8, :128]


def invert_kernel(panels, info, slot, packed_ref, block_ref, sem):
    size = block_ref.shape[0]
    held = 0
    for j in range(1, panels):
        held = jnp.where(info[5 + j] == info[3], j, held)
    copy = pltpu.make_async_copy(slot.at[pl.ds(pl.multiple_of(held * size, size), size)], block_ref, sem)
    copy.start()
    copy.wait()
    count = 4
    tile = size // count
    row = lax.broadcasted_iota(jnp.int32, (tile, tile), 0)
    col = lax.broadcasted_iota(jnp.int32, (tile, tile), 1)
    spans = [slice(i * tile, (i + 1) * tile) for i in range(count)]
    low = [block_ref[s, s] for s in spans]
    inv = []
    for block in low:
        diagonal = jnp.sum(jnp.where(row == col, block, 0.0), axis=1, keepdims=True)
        inv.append(jnp.where(row == col, 1.0 / diagonal, 0.0))
    width = 1
    while width < tile:
        joins = (row // (2 * width) == col // (2 * width)) & (row // width > col // width)
        half = [dot(jnp.where(joins, low[i], 0.0), inv[i], 0, HIGHEST) for i in range(count)]
        inv = [inv[i] - dot(inv[i], half[i], 0, HIGHEST) for i in range(count)]
        width *= 2
    while len(inv) > 1:
        width = inv[0].shape[0]
        zero = jnp.zeros((width, width), jnp.float32)
        merged = []
        for i in range(0, len(inv), 2):
            below = block_ref[(i + 1) * width : (i + 2) * width, i * width : (i + 1) * width]
            corner = -dot(inv[i + 1], dot(below, inv[i], 0, HIGHEST), 0, HIGHEST)
            top = jnp.concatenate([inv[i], zero], axis=1)
            merged.append(jnp.concatenate([top, jnp.concatenate([corner, inv[i + 1]], axis=1)], axis=0))
        inv = merged
    whole = inv[0]
    mid = tile + tile // 2
    packed_ref[0:tile, :] = whole[3 * tile :, :]
    packed_ref[tile : 2 * tile, 0 : 3 * tile] = whole[2 * tile : 3 * tile, 0 : 3 * tile]
    packed_ref[tile : 2 * tile, 3 * tile :] = whole[0:tile, 0:tile]
    packed_ref[2 * tile :, 0 : 2 * tile] = whole[tile:mid, 0 : 2 * tile]
    packed_ref[2 * tile :, 2 * tile :] = whole[mid : 2 * tile, 0 : 2 * tile]


def inverted_diagonal(panels, info, slot):
    size = slot.shape[1]
    rows = size // 2 + size // 8
    return pl.pallas_call(
        functools.partial(invert_kernel, panels),
        out_shape=jax.ShapeDtypeStruct((rows, size), jnp.float32),
        in_specs=[SMEM, HBM],
        out_specs=VMEM,
        scratch_shapes=[pltpu.VMEM((size, size), jnp.float32), pltpu.SemaphoreType.DMA],
        compiler_params=param(16),
        cost_estimate=cost(0, 1000),
    )(info, slot)


class Stream:
    def __init__(self, panels, size):
        self.panels, self.size = panels, size
        self.packed = size // 2 + size // 8
        self.pieces, self.starts, start = [], [], 0
        for j in range(panels):
            for k in [*range(j + 1, panels), None]:
                self.pieces.append((j, k))
                self.starts.append(start)
                start += self.packed if k is None else size
        self.total = start
        self.step = start // CHUNKS

    def rows(self, piece):
        return self.packed if self.pieces[piece][1] is None else self.size

    def panel_start(self, j):
        last = self.panels - 1
        return j * self.packed + self.size * (j * last - (j * (j - 1)) // 2)

    def cuts(self, edges):
        found = []
        for piece, (j, _) in enumerate(self.pieces):
            stop = self.starts[piece] + self.rows(piece)
            for number, (low, high) in enumerate(edges):
                low, high = max(low, self.starts[piece]), min(high, stop)
                if low < high:
                    found.append((j, number, low, high - low))
        return found


def build_kernel(stream, info, slot, peer, packed, peer_packed, out, sems):
    place, me = info[2], info[3]
    pending = []
    for piece, (j, k) in enumerate(stream.pieces):
        count = stream.rows(piece)
        mine, theirs = packed, peer_packed
        if k is not None:
            span = pl.ds(k * stream.size, count)
            mine, theirs = slot.at[span], peer.at[span]
        is_mine = info[5 + j] == me
        target = out.at[pl.ds(pl.multiple_of(place * (SKEW * stream.step) + stream.starts[piece], 8), count)]
        own_copy = pltpu.make_async_copy(mine, target, sems.at[piece])
        peer_copy = pltpu.make_async_copy(theirs, target, sems.at[piece])
        pl.when(is_mine)(own_copy.start)
        pl.when(jnp.logical_not(is_mine))(peer_copy.start)
        pending.append(peer_copy)
    for copy in pending:
        copy.wait()


def build_stream(stream, chips, info, slot, peer, packed, peer_packed):
    rows = stream.total + SKEW * stream.step * (chips - 1)
    return pl.pallas_call(
        functools.partial(build_kernel, stream),
        out_shape=jax.ShapeDtypeStruct((rows, stream.size), jnp.float32),
        in_specs=[SMEM] + [HBM] * 4,
        out_specs=HBM,
        scratch_shapes=[pltpu.SemaphoreType.DMA((len(stream.pieces),))],
        compiler_params=param(4),
        cost_estimate=cost(0, 1000),
    )(info, slot, peer, packed, peer_packed)


def step_kernel(stream, number, info, counts, own, *refs):
    del counts
    out, sems = refs[-2:]
    unit = stream.packed // 5
    place = info[2]
    pending = []
    for g in range(stream.step // unit):
        inside = pl.ds(g * unit, unit)
        copy = pltpu.make_async_copy(
            own.at[pl.ds(number * stream.step + g * unit, unit)], out.at[inside], sems.at[g]
        )
        pending.append(copy)
        if number < SKEW:
            copy.start()
            continue
        row = number * stream.step + g * unit - place * (SKEW * stream.step)
        origin = info[5 + stream.panels]
        for j in range(1, stream.panels):
            origin = jnp.where(row >= stream.panel_start(j), info[5 + stream.panels + j], origin)
        passing = pltpu.make_async_copy(refs[0].at[inside], out.at[inside], sems.at[g])
        pl.when(origin < place)(passing.start)
        pl.when(origin >= place)(copy.start)
    for copy in pending:
        copy.wait()


def step_block(stream, number, info, counts, own, got, earlier):
    operands = ([got[number - SKEW]] if number >= SKEW else []) + earlier
    return pl.pallas_call(
        functools.partial(step_kernel, stream, number),
        out_shape=jax.ShapeDtypeStruct((stream.step, stream.size), jnp.float32),
        in_specs=[SMEM, SMEM] + [HBM] * (1 + len(operands)),
        out_specs=HBM,
        scratch_shapes=[pltpu.SemaphoreType.DMA((stream.step * 5 // stream.packed,))],
        compiler_params=param(4),
        cost_estimate=cost(0, 1000),
    )(info, counts, own, *operands)


def collect_kernel(stream, chips, first, last, info, own, *refs):
    received, out, sems = refs[:-2], refs[-2], refs[-1]
    place = info[2]
    pending = []
    step = stream.step
    edges = [(i * step, (i + 1) * step) for i in range(first, last)]
    for number, (j, i, low, count) in enumerate(stream.cuts(edges)):
        here = info[5 + stream.panels + j] >= place
        target = out.at[pl.ds(low - first * step, count)]
        start = pl.multiple_of(place * (SKEW * step) + low, 8)
        own_copy = pltpu.make_async_copy(own.at[pl.ds(start, count)], target, sems.at[number])
        pl.when(here)(own_copy.start)
        for p in range(1, chips):
            source = received[i + SKEW * (p - 1)].at[pl.ds(low - (first + i) * step, count)]
            copy = pltpu.make_async_copy(source, target, sems.at[number])
            pl.when(jnp.logical_not(here) & (place == p))(copy.start)
        pending.append(own_copy)
    for copy in pending:
        copy.wait()


def collected(stream, chips, first, last, info, own, got):
    received = [got[s] for s in range(first, last + SKEW * (chips - 2))]
    return pl.pallas_call(
        functools.partial(collect_kernel, stream, chips, first, last),
        out_shape=jax.ShapeDtypeStruct(((last - first) * stream.step, stream.size), jnp.float32),
        in_specs=[SMEM] + [HBM] * (1 + len(received)),
        out_specs=HBM,
        scratch_shapes=[pltpu.SemaphoreType.DMA(((last - first) * len(stream.pieces),))],
        compiler_params=param(4),
        cost_estimate=cost(0, 1000),
    )(info, own, *received)


def sweep_kernel(stream, n_sec, info, earlier, query, *refs):
    groups = len(GROUPS)
    own, other = refs[:groups], refs[groups : 2 * groups]
    out_high, out_low, done_ref, low_high, low_low, inv_high, inv_low, pending, part_high, part_low = refs[2 * groups : -2]
    arrived, sems = refs[-2:]
    done_ref[...] = jnp.zeros_like(done_ref)
    place, section = info[2], info[4]
    panels, size, step = stream.panels, stream.size, stream.step
    rows = query.shape[0]
    block = rows // n_sec
    tile = size // 4

    slots = arrived.shape[0]
    found = stream.cuts([(first * step, last * step) for first, last in GROUPS])
    copies = []

    def fetch(number):
        j, group, low, count = found[number]
        inside = pl.ds(low - GROUPS[group][0] * step, count)
        target = arrived.at[number % slots, pl.ds(0, count)]
        own_copy = pltpu.make_async_copy(own[group].at[inside], target, sems.at[number])
        other_copy = pltpu.make_async_copy(other[group].at[inside], target, sems.at[number])
        ahead = info[5 + panels + j] > place
        pl.when(ahead)(other_copy.start)
        pl.when(jnp.logical_not(ahead))(own_copy.start)
        copies.append(own_copy)

    for number in range(slots):
        fetch(number)

    for k in range(n_sec):
        start = pl.multiple_of(partner(section, k, n_sec) * block, block)
        for j in range(panels):
            pending[j, k * block : (k + 1) * block, :] = query[pl.ds(start, block), j * size : (j + 1) * size]

    for number, (_, _, low, count) in enumerate(found):
        copies[number].wait()

        @pl.loop(0, count // 64)
        def _(i):
            inside = pl.ds(pl.multiple_of(i * 64, 64), 64)
            span = pl.ds(pl.multiple_of(low + i * 64, 64), 64)
            low_high[span, :], low_low[span, :] = parts_of(arrived[number % slots, inside, :])

        if number + slots < len(found):
            fetch(number + slots)

    for j in range(panels):
        s = stream.panel_start(j + 1) - stream.packed
        for source, target in ((low_high, inv_high), (low_low, inv_low)):
            target[j] = jnp.zeros((size, size), jnp.bfloat16)
            target[j, 3 * tile :, :] = source[s : s + tile, :]
            target[j, 2 * tile : 3 * tile, : 3 * tile] = source[s + tile : s + 2 * tile, : 3 * tile]
            target[j, :tile, :tile] = source[s + tile : s + 2 * tile, 3 * tile :]
            middle = tile + tile // 2
            target[j, tile:middle, : 2 * tile] = source[s + 2 * tile : s + stream.packed, : 2 * tile]
            target[j, middle : 2 * tile, : 2 * tile] = source[s + 2 * tile : s + stream.packed, 2 * tile :]

    def below(j, k):
        span = pl.ds(pl.multiple_of(stream.panel_start(j) + (k - j - 1) * size, 64), size)
        return low_high[span, :], low_low[span, :]

    @pl.loop(0, panels)
    def _(j):
        solved = dot_parts(parts_of(pending[j]), (inv_high[j], inv_low[j]), 1)
        pending[j] = solved
        part_high[...], part_low[...] = parts_of(solved)

        @pl.loop(j + 1, panels)
        def _(k):
            pending[k] = pending[k] - dot_parts((part_high[...], part_low[...]), below(j, k), 1)

    @pl.loop(0, panels)
    def _(step_number):
        j = panels - 1 - step_number

        @pl.loop(j + 1, panels)
        def _(k):
            pending[j] = pending[j] - dot_parts((out_high[k], out_low[k]), below(j, k), 0)

        answer = dot_parts(parts_of(pending[j]), (inv_high[j], inv_low[j]), 0)
        out_high[j], out_low[j] = parts_of(answer)


def swept(stream, n_sec, info, earlier, query, own, other):
    rows = query.shape[0]
    panels, size, total = stream.panels, stream.size, stream.total
    out = jax.ShapeDtypeStruct((panels, rows, size), jnp.bfloat16)
    return pl.pallas_call(
        functools.partial(sweep_kernel, stream, n_sec),
        out_shape=(out, out, jax.ShapeDtypeStruct((8, 128), jnp.float32)),
        in_specs=[SMEM, HBM, VMEM] + [HBM] * (len(own) + len(other)),
        out_specs=(VMEM, VMEM, VMEM),
        scratch_shapes=[
            pltpu.VMEM((total, size), jnp.bfloat16),
            pltpu.VMEM((total, size), jnp.bfloat16),
            pltpu.VMEM((panels, size, size), jnp.bfloat16),
            pltpu.VMEM((panels, size, size), jnp.bfloat16),
            pltpu.VMEM((panels, rows, size), jnp.float32),
            pltpu.VMEM((rows, size), jnp.bfloat16),
            pltpu.VMEM((rows, size), jnp.bfloat16),
            pltpu.VMEM((4, size, size), jnp.float32),
            pltpu.SemaphoreType.DMA((len(stream.pieces) + len(GROUPS),)),
        ],
        compiler_params=param(32),
        cost_estimate=cost(0, 1000),
    )(info, earlier, query, *own, *other)


def score_kernel(n_sec, scale, first, counts, earlier, high, low, *refs):
    blocks = len(refs) - n_sec - 3
    trains, outs = refs[:blocks], refs[blocks : blocks + n_sec]
    train_high, train_low, total = refs[-3:]
    panels, rows, size = high.shape
    length = trains[0].shape[0]
    for b, train in enumerate(trains):
        for p in range(panels):
            span = slice(b * length, (b + 1) * length)
            train_high[p, span, :], train_low[p, span, :] = parts_of(train[:, p * size : (p + 1) * size])
    total[...] = jnp.zeros_like(total)

    @pl.loop(0, panels)
    def _(p):
        total[...] += dot_parts((high[p], low[p]), (train_high[p], train_low[p]), 1)

    col = lax.broadcasted_iota(jnp.int32, (1, blocks * length), 1)
    limit = jnp.full_like(col, counts[0] - first)
    for b in range(1, blocks):
        limit = jnp.where(col >= b * length, counts[b] - first + b * length, limit)
    factor = jnp.where(col < limit, scale, 0.0).astype(jnp.float32)
    share = rows // n_sec
    for k in range(n_sec):
        outs[k][...] = total[k * share : (k + 1) * share, :] * factor


def scored(n_sec, scale, first, counts, earlier, high, low, trains):
    panels, rows, size = high.shape
    cols = sum(t.shape[0] for t in trains)
    return pl.pallas_call(
        functools.partial(score_kernel, n_sec, scale, first),
        out_shape=tuple(jax.ShapeDtypeStruct((rows // n_sec, cols), jnp.float32) for _ in range(n_sec)),
        in_specs=[SMEM, HBM] + [VMEM] * (2 + len(trains)),
        out_specs=tuple(VMEM for _ in range(n_sec)),
        scratch_shapes=[
            pltpu.VMEM((panels, cols, size), jnp.bfloat16),
            pltpu.VMEM((panels, cols, size), jnp.bfloat16),
            pltpu.VMEM((rows, cols), jnp.float32),
        ],
        compiler_params=param(24),
        cost_estimate=cost(0, 1000),
    )(counts, earlier, high, low, *trains)


def body(query_gradient_stack, train_grads, factor_slots, owner, train_count):
    query, train, slot, owners = query_gradient_stack[0], train_grads[0], factor_slots[0, 0], owner[0]
    rows, coords = query.shape
    size = slot.shape[1]
    panels = coords // size
    n_dp, n_sec = lax.axis_size("dp"), lax.axis_size("section")
    chips = n_dp // 2
    stream = Stream(panels, size)
    me = lax.axis_index("dp")
    section = lax.axis_index("section")
    chip, core = lax.shift_right_logical(me, 1), me & 1
    first_core = core == 0
    place = jnp.where(first_core, chip, chips - 1 - chip)
    owner_chip = lax.shift_right_logical(owners, 1)
    owner_place = jnp.where(first_core, owner_chip, chips - 1 - owner_chip)
    info = jnp.concatenate([jnp.stack([chip, core, place, me, section]), owners, owner_place])

    swap_pairs = [(d, d ^ 1) for d in range(n_dp)]
    next_chip = [(d, (d + 2) % n_dp) for d in range(n_dp)]

    def swapped(value):
        return lax.ppermute(value, "dp", swap_pairs)

    cuts = [sum(TRAIN_CUTS[:i]) for i in range(len(TRAIN_CUTS) + 1)]
    first_part, slot = lax.optimization_barrier((train[: cuts[1]], slot))
    far = [lax.ppermute(first_part, "dp", next_chip)]

    def send_train(index, *earlier):
        part = ordered(train[cuts[index] : cuts[index + 1]], *earlier)
        far.append(lax.ppermute(part, "dp", next_chip))
        return part

    peer = swapped(slot)
    packed = inverted_diagonal(panels, info, slot)
    own_rows = build_stream(stream, chips, info, slot, peer, packed, swapped(packed))
    count_2 = lax.ppermute(train_count, "dp", next_chip)
    count_1 = lax.ppermute(train_count, "dp", [(d, (d + 1) % n_dp) for d in range(n_dp)])
    near_counts = jnp.concatenate([count_1, count_2])

    got, own, other = {}, [], []
    steps = CHUNKS + SKEW * (chips - 2)
    for number in range(steps):
        earlier = [corner(far[0])] if number == 0 else [block]
        for index, (first, last) in enumerate(GROUPS[:-1]):
            if number == last + 2 + SKEW * (chips - 2):
                earlier.append(corner(other[index]))
        block = step_block(stream, number, info, near_counts, own_rows, got, earlier)
        pairs = []
        for p in range(chips - 1):
            if 0 <= number - SKEW * p < CHUNKS:
                pairs += [(2 * p, 2 * p + 2), (2 * (chips - 1 - p) + 1, 2 * (chips - 2 - p) + 1)]
        got[number] = lax.ppermute(block, "dp", pairs)
        for first, last in GROUPS:
            if number == last - 1 + SKEW * (chips - 2):
                value = collected(stream, chips, first, last, info, own_rows, got)
                own.append(value)
                other.append(swapped(value))

    part = send_train(1, corner(other[-1]))
    high, low, swept_token = swept(stream, n_sec, info, corner(part), query, own, other)

    scale = (coords * n_sec) ** (-0.5)

    def summed(parts):
        total = parts[0]
        for k in range(1, n_sec):
            if n_sec & (n_sec - 1) == 0:
                pairs = [(s, s ^ k) for s in range(n_sec)]
            else:
                pairs = [(s, (s + k) % n_sec) for s in range(n_sec)]
            total = total + lax.ppermute(parts[k], "section", pairs)
        return total

    parts = scored(n_sec, scale, 0, train_count, swept_token, high, low, [train])
    own_scores = summed(parts)
    near_scores, far_scores, earlier = [], [], [corner(own_scores)]
    for index in range(len(cuts) - 1):
        if index == 1:
            earlier.append(corner(send_train(2, corner(parts[0]))))
        far_part = far[index]
        near_part = swapped(chosen(info, train, cuts[index], far_part, *(earlier if index else [swept_token])))
        length = cuts[index + 1] - cuts[index]
        parts = scored(
            n_sec, scale, cuts[index], near_counts, corner(parts[0]), high, low, [near_part, far_part]
        )
        both = summed(parts)
        earlier.append(corner(both))
        near_scores.append(both[:, :length])
        far_scores.append(both[:, length:])
    return jnp.concatenate([own_scores] + near_scores + far_scores, axis=1)[None]


def solution(mesh):
    in_specs = (
        P("section", "dp", None),
        P("section", "dp", None),
        P("section", "dp", None, None),
        P("section", None),
        P("dp"),
    )
    out_specs = P("dp", "section", None)
    return jax.shard_map(body, mesh=mesh, in_specs=in_specs, out_specs=out_specs, check_vma=False)
```

```python
import functools

import jax
import jax.numpy as jnp
from jax import lax
from jax.experimental import pallas as pl
from jax.experimental.pallas import tpu as pltpu
from jax.sharding import PartitionSpec as P

HIGHEST = lax.Precision.HIGHEST
CHUNKS = 17
SKEW = 2
GROUPS = ((0, 4), (4, 8), (8, 12), (12, 17))
TRAIN_CUTS = (96, 256, 96, 64)
MIB = 1024 * 1024
HBM = pl.BlockSpec(memory_space=pltpu.HBM)
SMEM = pl.BlockSpec(memory_space=pltpu.SMEM)
VMEM = pl.BlockSpec(memory_space=pltpu.VMEM)


def dot(a, b, contract, precision=None):
    return lax.dot_general(
        a, b, (((1,), (contract,)), ((), ())), precision=precision, preferred_element_type=jnp.float32
    )


def parts_of(value):
    high = value.astype(jnp.bfloat16)
    return high, (value - high.astype(jnp.float32)).astype(jnp.bfloat16)


def dot_parts(a, b, contract):
    return dot(a[0], b[0], contract) + (dot(a[0], b[1], contract) + dot(a[1], b[0], contract))


def partner(section, k, n_sec):
    if n_sec & (n_sec - 1) == 0:
        return section ^ k
    return lax.rem(section + k, n_sec)


def param(limit_mib):
    return pltpu.CompilerParams(vmem_limit_bytes=limit_mib * MIB)


def cost(flops, moved):
    return pl.CostEstimate(flops=flops, bytes_accessed=moved, transcendentals=0)


def order_kernel(*refs):
    del refs


def ordered(value, *earlier):
    return pl.pallas_call(
        order_kernel,
        out_shape=jax.ShapeDtypeStruct(value.shape, value.dtype),
        in_specs=[HBM] * (1 + len(earlier)),
        out_specs=HBM,
        input_output_aliases={0: 0},
        cost_estimate=cost(0, 1000),
    )(value, *earlier)


def choose_kernel(start, info, train, far, *refs):
    out, sem = refs[-2:]
    own_copy = pltpu.make_async_copy(train.at[pl.ds(start, out.shape[0])], out, sem)
    far_copy = pltpu.make_async_copy(far, out, sem)
    pl.when(info[1] == 0)(own_copy.start)
    pl.when(info[1] != 0)(far_copy.start)
    own_copy.wait()


def chosen(info, train, start, far, *earlier):
    return pl.pallas_call(
        functools.partial(choose_kernel, start),
        out_shape=jax.ShapeDtypeStruct(far.shape, far.dtype),
        in_specs=[SMEM] + [HBM] * (2 + len(earlier)),
        out_specs=HBM,
        scratch_shapes=[pltpu.SemaphoreType.DMA],
        compiler_params=param(4),
        cost_estimate=cost(0, 1000),
    )(info, train, far, *earlier)


def corner(value):
    return value[:8, :128]


def invert_kernel(panels, info, slot, packed_ref, block_ref, sem):
    size = block_ref.shape[0]
    held = 0
    for j in range(1, panels):
        held = jnp.where(info[5 + j] == info[3], j, held)
    copy = pltpu.make_async_copy(slot.at[pl.ds(pl.multiple_of(held * size, size), size)], block_ref, sem)
    copy.start()
    copy.wait()
    count = 4
    tile = size // count
    row = lax.broadcasted_iota(jnp.int32, (tile, tile), 0)
    col = lax.broadcasted_iota(jnp.int32, (tile, tile), 1)
    spans = [slice(i * tile, (i + 1) * tile) for i in range(count)]
    low = [block_ref[s, s] for s in spans]
    inv = []
    for block in low:
        diagonal = jnp.sum(jnp.where(row == col, block, 0.0), axis=1, keepdims=True)
        inv.append(jnp.where(row == col, 1.0 / diagonal, 0.0))
    width = 1
    while width < tile:
        joins = (row // (2 * width) == col // (2 * width)) & (row // width > col // width)
        half = [dot(jnp.where(joins, low[i], 0.0), inv[i], 0, HIGHEST) for i in range(count)]
        inv = [inv[i] - dot(inv[i], half[i], 0, HIGHEST) for i in range(count)]
        width *= 2
    while len(inv) > 1:
        width = inv[0].shape[0]
        zero = jnp.zeros((width, width), jnp.float32)
        merged = []
        for i in range(0, len(inv), 2):
            below = block_ref[(i + 1) * width : (i + 2) * width, i * width : (i + 1) * width]
            corner = -dot(inv[i + 1], dot(below, inv[i], 0, HIGHEST), 0, HIGHEST)
            top = jnp.concatenate([inv[i], zero], axis=1)
            merged.append(jnp.concatenate([top, jnp.concatenate([corner, inv[i + 1]], axis=1)], axis=0))
        inv = merged
    whole = inv[0]
    mid = tile + tile // 2
    packed_ref[0:tile, :] = whole[3 * tile :, :]
    packed_ref[tile : 2 * tile, 0 : 3 * tile] = whole[2 * tile : 3 * tile, 0 : 3 * tile]
    packed_ref[tile : 2 * tile, 3 * tile :] = whole[0:tile, 0:tile]
    packed_ref[2 * tile :, 0 : 2 * tile] = whole[tile:mid, 0 : 2 * tile]
    packed_ref[2 * tile :, 2 * tile :] = whole[mid : 2 * tile, 0 : 2 * tile]


def inverted_diagonal(panels, info, slot):
    size = slot.shape[1]
    rows = size // 2 + size // 8
    return pl.pallas_call(
        functools.partial(invert_kernel, panels),
        out_shape=jax.ShapeDtypeStruct((rows, size), jnp.float32),
        in_specs=[SMEM, HBM],
        out_specs=VMEM,
        scratch_shapes=[pltpu.VMEM((size, size), jnp.float32), pltpu.SemaphoreType.DMA],
        compiler_params=param(16),
        cost_estimate=cost(0, 1000),
    )(info, slot)


class Stream:
    def __init__(self, panels, size):
        self.panels, self.size = panels, size
        self.packed = size // 2 + size // 8
        self.pieces, self.starts, start = [], [], 0
        for j in range(panels):
            for k in [*range(j + 1, panels), None]:
                self.pieces.append((j, k))
                self.starts.append(start)
                start += self.packed if k is None else size
        self.total = start
        self.step = start // CHUNKS

    def rows(self, piece):
        return self.packed if self.pieces[piece][1] is None else self.size

    def panel_start(self, j):
        last = self.panels - 1
        return j * self.packed + self.size * (j * last - (j * (j - 1)) // 2)

    def cuts(self, edges):
        found = []
        for piece, (j, _) in enumerate(self.pieces):
            stop = self.starts[piece] + self.rows(piece)
            for number, (low, high) in enumerate(edges):
                low, high = max(low, self.starts[piece]), min(high, stop)
                if low < high:
                    found.append((j, number, low, high - low))
        return found


def build_kernel(stream, info, slot, peer, packed, peer_packed, out, sems):
    place, me = info[2], info[3]
    pending = []
    for piece, (j, k) in enumerate(stream.pieces):
        count = stream.rows(piece)
        mine, theirs = packed, peer_packed
        if k is not None:
            span = pl.ds(k * stream.size, count)
            mine, theirs = slot.at[span], peer.at[span]
        is_mine = info[5 + j] == me
        target = out.at[pl.ds(pl.multiple_of(place * (SKEW * stream.step) + stream.starts[piece], 8), count)]
        own_copy = pltpu.make_async_copy(mine, target, sems.at[piece])
        peer_copy = pltpu.make_async_copy(theirs, target, sems.at[piece])
        pl.when(is_mine)(own_copy.start)
        pl.when(jnp.logical_not(is_mine))(peer_copy.start)
        pending.append(peer_copy)
    for copy in pending:
        copy.wait()


def build_stream(stream, chips, info, slot, peer, packed, peer_packed):
    rows = stream.total + SKEW * stream.step * (chips - 1)
    return pl.pallas_call(
        functools.partial(build_kernel, stream),
        out_shape=jax.ShapeDtypeStruct((rows, stream.size), jnp.float32),
        in_specs=[SMEM] + [HBM] * 4,
        out_specs=HBM,
        scratch_shapes=[pltpu.SemaphoreType.DMA((len(stream.pieces),))],
        compiler_params=param(4),
        cost_estimate=cost(0, 1000),
    )(info, slot, peer, packed, peer_packed)


def step_kernel(stream, number, info, counts, own, *refs):
    del counts
    out, sems = refs[-2:]
    unit = stream.packed // 5
    place = info[2]
    pending = []
    for g in range(stream.step // unit):
        inside = pl.ds(g * unit, unit)
        copy = pltpu.make_async_copy(
            own.at[pl.ds(number * stream.step + g * unit, unit)], out.at[inside], sems.at[g]
        )
        pending.append(copy)
        if number < SKEW:
            copy.start()
            continue
        row = number * stream.step + g * unit - place * (SKEW * stream.step)
        origin = info[5 + stream.panels]
        for j in range(1, stream.panels):
            origin = jnp.where(row >= stream.panel_start(j), info[5 + stream.panels + j], origin)
        passing = pltpu.make_async_copy(refs[0].at[inside], out.at[inside], sems.at[g])
        pl.when(origin < place)(passing.start)
        pl.when(origin >= place)(copy.start)
    for copy in pending:
        copy.wait()


def step_block(stream, number, info, counts, own, got, earlier):
    operands = ([got[number - SKEW]] if number >= SKEW else []) + earlier
    return pl.pallas_call(
        functools.partial(step_kernel, stream, number),
        out_shape=jax.ShapeDtypeStruct((stream.step, stream.size), jnp.float32),
        in_specs=[SMEM, SMEM] + [HBM] * (1 + len(operands)),
        out_specs=HBM,
        scratch_shapes=[pltpu.SemaphoreType.DMA((stream.step * 5 // stream.packed,))],
        compiler_params=param(4),
        cost_estimate=cost(0, 1000),
    )(info, counts, own, *operands)


def collect_kernel(stream, chips, first, last, info, own, *refs):
    received, out, sems = refs[:-2], refs[-2], refs[-1]
    place = info[2]
    pending = []
    step = stream.step
    edges = [(i * step, (i + 1) * step) for i in range(first, last)]
    for number, (j, i, low, count) in enumerate(stream.cuts(edges)):
        here = info[5 + stream.panels + j] >= place
        target = out.at[pl.ds(low - first * step, count)]
        start = pl.multiple_of(place * (SKEW * step) + low, 8)
        own_copy = pltpu.make_async_copy(own.at[pl.ds(start, count)], target, sems.at[number])
        pl.when(here)(own_copy.start)
        for p in range(1, chips):
            source = received[i + SKEW * (p - 1)].at[pl.ds(low - (first + i) * step, count)]
            copy = pltpu.make_async_copy(source, target, sems.at[number])
            pl.when(jnp.logical_not(here) & (place == p))(copy.start)
        pending.append(own_copy)
    for copy in pending:
        copy.wait()


def collected(stream, chips, first, last, info, own, got, earlier):
    received = [got[s] for s in range(first, last + SKEW * (chips - 2))]
    return pl.pallas_call(
        functools.partial(collect_kernel, stream, chips, first, last),
        out_shape=jax.ShapeDtypeStruct(((last - first) * stream.step, stream.size), jnp.float32),
        in_specs=[SMEM] + [HBM] * (1 + len(received) + len(earlier)),
        out_specs=HBM,
        scratch_shapes=[pltpu.SemaphoreType.DMA(((last - first) * len(stream.pieces),))],
        compiler_params=param(4),
        cost_estimate=cost(0, 1000),
    )(info, own, *received, *earlier)


def sweep_kernel(stream, n_sec, info, earlier, query, *refs):
    groups = len(GROUPS)
    own, other = refs[:groups], refs[groups : 2 * groups]
    out_high, out_low, done_ref, low_high, low_low, inv_high, inv_low, pending, part_high, part_low = refs[2 * groups : -2]
    arrived, sems = refs[-2:]
    done_ref[...] = jnp.zeros_like(done_ref)
    place, section = info[2], info[4]
    panels, size, step = stream.panels, stream.size, stream.step
    rows = query.shape[0]
    block = rows // n_sec
    tile = size // 4

    slots = arrived.shape[0]
    found = stream.cuts([(first * step, last * step) for first, last in GROUPS])
    copies = []

    def fetch(number):
        j, group, low, count = found[number]
        inside = pl.ds(low - GROUPS[group][0] * step, count)
        target = arrived.at[number % slots, pl.ds(0, count)]
        own_copy = pltpu.make_async_copy(own[group].at[inside], target, sems.at[number])
        other_copy = pltpu.make_async_copy(other[group].at[inside], target, sems.at[number])
        ahead = info[5 + panels + j] > place
        pl.when(ahead)(other_copy.start)
        pl.when(jnp.logical_not(ahead))(own_copy.start)
        copies.append(own_copy)

    for number in range(slots):
        fetch(number)

    for k in range(n_sec):
        start = pl.multiple_of(partner(section, k, n_sec) * block, block)
        for j in range(panels):
            pending[j, k * block : (k + 1) * block, :] = query[pl.ds(start, block), j * size : (j + 1) * size]

    for number, (_, _, low, count) in enumerate(found):
        copies[number].wait()

        @pl.loop(0, count // 64)
        def _(i):
            inside = pl.ds(pl.multiple_of(i * 64, 64), 64)
            span = pl.ds(pl.multiple_of(low + i * 64, 64), 64)
            low_high[span, :], low_low[span, :] = parts_of(arrived[number % slots, inside, :])

        if number + slots < len(found):
            fetch(number + slots)

    for j in range(panels):
        s = stream.panel_start(j + 1) - stream.packed
        for source, target in ((low_high, inv_high), (low_low, inv_low)):
            target[j] = jnp.zeros((size, size), jnp.bfloat16)
            target[j, 3 * tile :, :] = source[s : s + tile, :]
            target[j, 2 * tile : 3 * tile, : 3 * tile] = source[s + tile : s + 2 * tile, : 3 * tile]
            target[j, :tile, :tile] = source[s + tile : s + 2 * tile, 3 * tile :]
            middle = tile + tile // 2
            target[j, tile:middle, : 2 * tile] = source[s + 2 * tile : s + stream.packed, : 2 * tile]
            target[j, middle : 2 * tile, : 2 * tile] = source[s + 2 * tile : s + stream.packed, 2 * tile :]

    def below(j, k):
        span = pl.ds(pl.multiple_of(stream.panel_start(j) + (k - j - 1) * size, 64), size)
        return low_high[span, :], low_low[span, :]

    @pl.loop(0, panels)
    def _(j):
        solved = dot_parts(parts_of(pending[j]), (inv_high[j], inv_low[j]), 1)
        pending[j] = solved
        part_high[...], part_low[...] = parts_of(solved)

        @pl.loop(j + 1, panels)
        def _(k):
            pending[k] = pending[k] - dot_parts((part_high[...], part_low[...]), below(j, k), 1)

    @pl.loop(0, panels)
    def _(step_number):
        j = panels - 1 - step_number

        @pl.loop(j + 1, panels)
        def _(k):
            pending[j] = pending[j] - dot_parts((out_high[k], out_low[k]), below(j, k), 0)

        answer = dot_parts(parts_of(pending[j]), (inv_high[j], inv_low[j]), 0)
        out_high[j], out_low[j] = parts_of(answer)


def swept(stream, n_sec, info, earlier, query, own, other):
    rows = query.shape[0]
    panels, size, total = stream.panels, stream.size, stream.total
    out = jax.ShapeDtypeStruct((panels, rows, size), jnp.bfloat16)
    return pl.pallas_call(
        functools.partial(sweep_kernel, stream, n_sec),
        out_shape=(out, out, jax.ShapeDtypeStruct((8, 128), jnp.float32)),
        in_specs=[SMEM, HBM, VMEM] + [HBM] * (len(own) + len(other)),
        out_specs=(VMEM, VMEM, VMEM),
        scratch_shapes=[
            pltpu.VMEM((total, size), jnp.bfloat16),
            pltpu.VMEM((total, size), jnp.bfloat16),
            pltpu.VMEM((panels, size, size), jnp.bfloat16),
            pltpu.VMEM((panels, size, size), jnp.bfloat16),
            pltpu.VMEM((panels, rows, size), jnp.float32),
            pltpu.VMEM((rows, size), jnp.bfloat16),
            pltpu.VMEM((rows, size), jnp.bfloat16),
            pltpu.VMEM((4, size, size), jnp.float32),
            pltpu.SemaphoreType.DMA((len(stream.pieces) + len(GROUPS),)),
        ],
        compiler_params=param(32),
        cost_estimate=cost(0, 1000),
    )(info, earlier, query, *own, *other)


def score_kernel(n_sec, scale, blocks, counts, earlier, high, low, *refs):
    trains, outs = refs[: len(blocks)], refs[len(blocks) : len(blocks) + n_sec]
    train_high, train_low, total = refs[-3:]
    panels, rows, size = high.shape
    cols = total.shape[1]
    col = lax.broadcasted_iota(jnp.int32, (1, cols), 1)
    start, limit = 0, None
    for (length, which, first), train in zip(blocks, trains):
        for p in range(panels):
            span = slice(start, start + length)
            train_high[p, span, :], train_low[p, span, :] = parts_of(train[:, p * size : (p + 1) * size])
        bound = jnp.full_like(col, counts[which] - first + start)
        limit = bound if limit is None else jnp.where(col >= start, bound, limit)
        start += length
    total[...] = jnp.zeros_like(total)

    @pl.loop(0, panels)
    def _(p):
        total[...] += dot_parts((high[p], low[p]), (train_high[p], train_low[p]), 1)

    factor = jnp.where(col < limit, scale, 0.0).astype(jnp.float32)
    share = rows // n_sec
    for k in range(n_sec):
        outs[k][...] = total[k * share : (k + 1) * share, :] * factor


def scored(n_sec, scale, counts, earlier, high, low, runs):
    panels, rows, size = high.shape
    blocks = [(train.shape[0], which, first) for train, which, first in runs]
    cols = sum(length for length, _, _ in blocks)
    return pl.pallas_call(
        functools.partial(score_kernel, n_sec, scale, blocks),
        out_shape=tuple(jax.ShapeDtypeStruct((rows // n_sec, cols), jnp.float32) for _ in range(n_sec)),
        in_specs=[SMEM, HBM] + [VMEM] * (2 + len(runs)),
        out_specs=tuple(VMEM for _ in range(n_sec)),
        scratch_shapes=[
            pltpu.VMEM((panels, cols, size), jnp.bfloat16),
            pltpu.VMEM((panels, cols, size), jnp.bfloat16),
            pltpu.VMEM((rows, cols), jnp.float32),
        ],
        compiler_params=param(24),
        cost_estimate=cost(0, 1000),
    )(counts, earlier, high, low, *[train for train, _, _ in runs])


def body(query_gradient_stack, train_grads, factor_slots, owner, train_count):
    query, train, slot, owners = query_gradient_stack[0], train_grads[0], factor_slots[0, 0], owner[0]
    rows, coords = query.shape
    size = slot.shape[1]
    panels = coords // size
    n_dp, n_sec = lax.axis_size("dp"), lax.axis_size("section")
    chips = n_dp // 2
    stream = Stream(panels, size)
    me = lax.axis_index("dp")
    section = lax.axis_index("section")
    chip, core = lax.shift_right_logical(me, 1), me & 1
    first_core = core == 0
    place = jnp.where(first_core, chip, chips - 1 - chip)
    owner_chip = lax.shift_right_logical(owners, 1)
    owner_place = jnp.where(first_core, owner_chip, chips - 1 - owner_chip)
    info = jnp.concatenate([jnp.stack([chip, core, place, me, section]), owners, owner_place])

    swap_pairs = [(d, d ^ 1) for d in range(n_dp)]
    next_chip = [(d, (d + 2) % n_dp) for d in range(n_dp)]

    def swapped(value):
        return lax.ppermute(value, "dp", swap_pairs)

    cuts = [sum(TRAIN_CUTS[:i]) for i in range(len(TRAIN_CUTS) + 1)]
    first_part, slot = lax.optimization_barrier((train[: cuts[1]], slot))
    far = [lax.ppermute(first_part, "dp", next_chip)]

    def send_train(index, *earlier):
        part = ordered(train[cuts[index] : cuts[index + 1]], *earlier)
        far.append(lax.ppermute(part, "dp", next_chip))
        return part

    peer = swapped(slot)
    packed = inverted_diagonal(panels, info, slot)
    own_rows = build_stream(stream, chips, info, slot, peer, packed, swapped(packed))
    count_2 = lax.ppermute(train_count, "dp", next_chip)
    count_1 = lax.ppermute(train_count, "dp", [(d, (d + 1) % n_dp) for d in range(n_dp)])
    counts = jnp.concatenate([train_count, count_1, count_2])

    got, own, other = {}, [], []
    steps = CHUNKS + SKEW * (chips - 2)
    for number in range(steps):
        earlier = [corner(far[0])] if number == 0 else [block]
        block = step_block(stream, number, info, counts, own_rows, got, earlier)
        pairs = []
        for p in range(chips - 1):
            if 0 <= number - SKEW * p < CHUNKS:
                pairs += [(2 * p, 2 * p + 2), (2 * (chips - 1 - p) + 1, 2 * (chips - 2 - p) + 1)]
        got[number] = lax.ppermute(block, "dp", pairs)
        for first, last in GROUPS:
            if number == last - 1 + SKEW * (chips - 2):
                before = [corner(rows_before) for rows_before in other[:2]] if last == CHUNKS else []
                value = collected(stream, chips, first, last, info, own_rows, got, before)
                own.append(value)
                other.append(swapped(value))

    token = corner(other[-1])
    for index in range(1, len(cuts) - 1):
        token = corner(send_train(index, token))
    high, low, swept_token = swept(stream, n_sec, info, token, query, own, other)

    scale = (coords * n_sec) ** (-0.5)

    def summed(parts):
        total = parts[0]
        for k in range(1, n_sec):
            if n_sec & (n_sec - 1) == 0:
                pairs = [(s, s ^ k) for s in range(n_sec)]
            else:
                pairs = [(s, (s + k) % n_sec) for s in range(n_sec)]
            total = total + lax.ppermute(parts[k], "section", pairs)
        return total

    def near_rows(index, *earlier):
        return swapped(chosen(info, train, cuts[index], far[index], *earlier))

    runs = [(train, 0, 0), (near_rows(0, swept_token), 1, 0), (far[0], 2, 0)]
    near_scores, far_scores, summed_corners, earlier = [], [], [], [swept_token]
    for index in range(len(cuts) - 1):
        if index:
            runs = [(near_rows(index, *earlier), 1, cuts[index]), (far[index], 2, cuts[index])]
        parts = scored(n_sec, scale, counts, earlier[0], high, low, runs)
        both = summed(parts)
        summed_corners.append(corner(both))
        earlier = [corner(parts[0])] + (summed_corners if index else [])
        length = cuts[index + 1] - cuts[index]
        if index == 0:
            own_scores, both = both[:, :rows], both[:, rows:]
        near_scores.append(both[:, :length])
        far_scores.append(both[:, length:])
    return jnp.concatenate([own_scores] + near_scores + far_scores, axis=1)[None]


def solution(mesh):
    in_specs = (
        P("section", "dp", None),
        P("section", "dp", None),
        P("section", "dp", None, None),
        P("section", None),
        P("dp"),
    )
    out_specs = P("dp", "section", None)
    return jax.shard_map(body, mesh=mesh, in_specs=in_specs, out_specs=out_specs, check_vma=False)
```

```python
import functools

import jax
import jax.numpy as jnp
from jax import lax
from jax.experimental import pallas as pl
from jax.experimental.pallas import tpu as pltpu
from jax.sharding import PartitionSpec as P

HIGHEST = lax.Precision.HIGHEST
CHUNKS = 17
SKEW = 2
GROUPS = ((0, 4), (4, 8), (8, 12), (12, 17))
TRAIN_CUTS = (96, 256, 96, 64)
MIB = 1024 * 1024
HBM = pl.BlockSpec(memory_space=pltpu.HBM)
SMEM = pl.BlockSpec(memory_space=pltpu.SMEM)
VMEM = pl.BlockSpec(memory_space=pltpu.VMEM)


def dot(a, b, contract, precision=None):
    return lax.dot_general(
        a, b, (((1,), (contract,)), ((), ())), precision=precision, preferred_element_type=jnp.float32
    )


def parts_of(value):
    high = value.astype(jnp.bfloat16)
    return high, (value - high.astype(jnp.float32)).astype(jnp.bfloat16)


def dot_parts(a, b, contract):
    return dot(a[0], b[0], contract) + (dot(a[0], b[1], contract) + dot(a[1], b[0], contract))


def partner(section, k, n_sec):
    if n_sec & (n_sec - 1) == 0:
        return section ^ k
    return lax.rem(section + k, n_sec)


def param(limit_mib):
    return pltpu.CompilerParams(vmem_limit_bytes=limit_mib * MIB)


def cost(flops, moved):
    return pl.CostEstimate(flops=flops, bytes_accessed=moved, transcendentals=0)


def order_kernel(*refs):
    del refs


def ordered(value, *earlier):
    return pl.pallas_call(
        order_kernel,
        out_shape=jax.ShapeDtypeStruct(value.shape, value.dtype),
        in_specs=[HBM] * (1 + len(earlier)),
        out_specs=HBM,
        input_output_aliases={0: 0},
        cost_estimate=cost(0, 1000),
    )(value, *earlier)


def choose_kernel(start, info, train, far, *refs):
    out, sem = refs[-2:]
    own_copy = pltpu.make_async_copy(train.at[pl.ds(start, out.shape[0])], out, sem)
    far_copy = pltpu.make_async_copy(far, out, sem)
    pl.when(info[1] == 0)(own_copy.start)
    pl.when(info[1] != 0)(far_copy.start)
    own_copy.wait()


def chosen(info, train, start, far, *earlier):
    return pl.pallas_call(
        functools.partial(choose_kernel, start),
        out_shape=jax.ShapeDtypeStruct(far.shape, far.dtype),
        in_specs=[SMEM] + [HBM] * (2 + len(earlier)),
        out_specs=HBM,
        scratch_shapes=[pltpu.SemaphoreType.DMA],
        compiler_params=param(4),
        cost_estimate=cost(0, 1000),
    )(info, train, far, *earlier)


def corner(value):
    return value[:8, :128]


def invert_kernel(panels, info, slot, packed_ref, block_ref, sem):
    size = block_ref.shape[0]
    held = 0
    for j in range(1, panels):
        held = jnp.where(info[5 + j] == info[3], j, held)
    copy = pltpu.make_async_copy(slot.at[pl.ds(pl.multiple_of(held * size, size), size)], block_ref, sem)
    copy.start()
    copy.wait()
    count = 4
    tile = size // count
    row = lax.broadcasted_iota(jnp.int32, (tile, tile), 0)
    col = lax.broadcasted_iota(jnp.int32, (tile, tile), 1)
    spans = [slice(i * tile, (i + 1) * tile) for i in range(count)]
    low = [block_ref[s, s] for s in spans]
    inv = []
    for block in low:
        diagonal = jnp.sum(jnp.where(row == col, block, 0.0), axis=1, keepdims=True)
        inv.append(jnp.where(row == col, 1.0 / diagonal, 0.0))
    width = 1
    while width < tile:
        joins = (row // (2 * width) == col // (2 * width)) & (row // width > col // width)
        half = [dot(jnp.where(joins, low[i], 0.0), inv[i], 0, HIGHEST) for i in range(count)]
        inv = [inv[i] - dot(inv[i], half[i], 0, HIGHEST) for i in range(count)]
        width *= 2
    while len(inv) > 1:
        width = inv[0].shape[0]
        zero = jnp.zeros((width, width), jnp.float32)
        merged = []
        for i in range(0, len(inv), 2):
            below = block_ref[(i + 1) * width : (i + 2) * width, i * width : (i + 1) * width]
            corner = -dot(inv[i + 1], dot(below, inv[i], 0, HIGHEST), 0, HIGHEST)
            top = jnp.concatenate([inv[i], zero], axis=1)
            merged.append(jnp.concatenate([top, jnp.concatenate([corner, inv[i + 1]], axis=1)], axis=0))
        inv = merged
    whole = inv[0]
    mid = tile + tile // 2
    packed_ref[0:tile, :] = whole[3 * tile :, :]
    packed_ref[tile : 2 * tile, 0 : 3 * tile] = whole[2 * tile : 3 * tile, 0 : 3 * tile]
    packed_ref[tile : 2 * tile, 3 * tile :] = whole[0:tile, 0:tile]
    packed_ref[2 * tile :, 0 : 2 * tile] = whole[tile:mid, 0 : 2 * tile]
    packed_ref[2 * tile :, 2 * tile :] = whole[mid : 2 * tile, 0 : 2 * tile]


def inverted_diagonal(panels, info, slot):
    size = slot.shape[1]
    rows = size // 2 + size // 8
    return pl.pallas_call(
        functools.partial(invert_kernel, panels),
        out_shape=jax.ShapeDtypeStruct((rows, size), jnp.float32),
        in_specs=[SMEM, HBM],
        out_specs=VMEM,
        scratch_shapes=[pltpu.VMEM((size, size), jnp.float32), pltpu.SemaphoreType.DMA],
        compiler_params=param(16),
        cost_estimate=cost(0, 1000),
    )(info, slot)


class Stream:
    def __init__(self, panels, size):
        self.panels, self.size = panels, size
        self.packed = size // 2 + size // 8
        self.pieces, self.starts, start = [], [], 0
        for j in range(panels):
            for k in [*range(j + 1, panels), None]:
                self.pieces.append((j, k))
                self.starts.append(start)
                start += self.packed if k is None else size
        self.total = start
        self.step = start // CHUNKS

    def rows(self, piece):
        return self.packed if self.pieces[piece][1] is None else self.size

    def panel_start(self, j):
        last = self.panels - 1
        return j * self.packed + self.size * (j * last - (j * (j - 1)) // 2)

    def cuts(self, edges):
        found = []
        for piece, (j, _) in enumerate(self.pieces):
            stop = self.starts[piece] + self.rows(piece)
            for number, (low, high) in enumerate(edges):
                low, high = max(low, self.starts[piece]), min(high, stop)
                if low < high:
                    found.append((j, number, low, high - low))
        return found


def build_kernel(stream, info, slot, peer, packed, peer_packed, out, sems):
    place, me = info[2], info[3]
    pending = []
    for piece, (j, k) in enumerate(stream.pieces):
        count = stream.rows(piece)
        mine, theirs = packed, peer_packed
        if k is not None:
            span = pl.ds(k * stream.size, count)
            mine, theirs = slot.at[span], peer.at[span]
        is_mine = info[5 + j] == me
        target = out.at[pl.ds(pl.multiple_of(place * (SKEW * stream.step) + stream.starts[piece], 8), count)]
        own_copy = pltpu.make_async_copy(mine, target, sems.at[piece])
        peer_copy = pltpu.make_async_copy(theirs, target, sems.at[piece])
        pl.when(is_mine)(own_copy.start)
        pl.when(jnp.logical_not(is_mine))(peer_copy.start)
        pending.append(peer_copy)
    for copy in pending:
        copy.wait()


def build_stream(stream, chips, info, slot, peer, packed, peer_packed):
    rows = stream.total + SKEW * stream.step * (chips - 1)
    return pl.pallas_call(
        functools.partial(build_kernel, stream),
        out_shape=jax.ShapeDtypeStruct((rows, stream.size), jnp.float32),
        in_specs=[SMEM] + [HBM] * 4,
        out_specs=HBM,
        scratch_shapes=[pltpu.SemaphoreType.DMA((len(stream.pieces),))],
        compiler_params=param(4),
        cost_estimate=cost(0, 1000),
    )(info, slot, peer, packed, peer_packed)


def step_kernel(stream, number, info, counts, own, *refs):
    del counts
    out, sems = refs[-2:]
    unit = stream.packed // 5
    place = info[2]
    pending = []
    for g in range(stream.step // unit):
        inside = pl.ds(g * unit, unit)
        copy = pltpu.make_async_copy(
            own.at[pl.ds(number * stream.step + g * unit, unit)], out.at[inside], sems.at[g]
        )
        pending.append(copy)
        if number < SKEW:
            copy.start()
            continue
        row = number * stream.step + g * unit - place * (SKEW * stream.step)
        origin = info[5 + stream.panels]
        for j in range(1, stream.panels):
            origin = jnp.where(row >= stream.panel_start(j), info[5 + stream.panels + j], origin)
        passing = pltpu.make_async_copy(refs[0].at[inside], out.at[inside], sems.at[g])
        pl.when(origin < place)(passing.start)
        pl.when(origin >= place)(copy.start)
    for copy in pending:
        copy.wait()


def step_block(stream, number, info, counts, own, got, earlier):
    operands = ([got[number - SKEW]] if number >= SKEW else []) + earlier
    return pl.pallas_call(
        functools.partial(step_kernel, stream, number),
        out_shape=jax.ShapeDtypeStruct((stream.step, stream.size), jnp.float32),
        in_specs=[SMEM, SMEM] + [HBM] * (1 + len(operands)),
        out_specs=HBM,
        scratch_shapes=[pltpu.SemaphoreType.DMA((stream.step * 5 // stream.packed,))],
        compiler_params=param(4),
        cost_estimate=cost(0, 1000),
    )(info, counts, own, *operands)


def collect_kernel(stream, chips, first, last, info, own, *refs):
    received, out, sems = refs[:-2], refs[-2], refs[-1]
    place = info[2]
    pending = []
    step = stream.step
    edges = [(i * step, (i + 1) * step) for i in range(first, last)]
    for number, (j, i, low, count) in enumerate(stream.cuts(edges)):
        here = info[5 + stream.panels + j] >= place
        target = out.at[pl.ds(low - first * step, count)]
        start = pl.multiple_of(place * (SKEW * step) + low, 8)
        own_copy = pltpu.make_async_copy(own.at[pl.ds(start, count)], target, sems.at[number])
        pl.when(here)(own_copy.start)
        for p in range(1, chips):
            source = received[i + SKEW * (p - 1)].at[pl.ds(low - (first + i) * step, count)]
            copy = pltpu.make_async_copy(source, target, sems.at[number])
            pl.when(jnp.logical_not(here) & (place == p))(copy.start)
        pending.append(own_copy)
    for copy in pending:
        copy.wait()


def collected(stream, chips, first, last, info, own, got, earlier):
    received = [got[s] for s in range(first, last + SKEW * (chips - 2))]
    return pl.pallas_call(
        functools.partial(collect_kernel, stream, chips, first, last),
        out_shape=pltpu.HBM(((last - first) * stream.step, stream.size), jnp.float32),
        in_specs=[SMEM] + [HBM] * (1 + len(received) + len(earlier)),
        out_specs=HBM,
        scratch_shapes=[pltpu.SemaphoreType.DMA(((last - first) * len(stream.pieces),))],
        compiler_params=param(4),
        cost_estimate=cost(0, 1000),
    )(info, own, *received, *earlier)


def sweep_kernel(stream, n_sec, info, earlier, query, *refs):
    groups = len(GROUPS)
    own, other = refs[:groups], refs[groups : 2 * groups]
    out_high, out_low, done_ref, low_high, low_low, inv_high, inv_low, pending, part_high, part_low = refs[2 * groups : -2]
    arrived, sems = refs[-2:]
    done_ref[...] = jnp.zeros_like(done_ref)
    place, section = info[2], info[4]
    panels, size, step = stream.panels, stream.size, stream.step
    rows = query.shape[0]
    block = rows // n_sec
    tile = size // 4

    slots = arrived.shape[0]
    found = stream.cuts([(first * step, last * step) for first, last in GROUPS])
    copies = []

    def fetch(number):
        j, group, low, count = found[number]
        inside = pl.ds(low - GROUPS[group][0] * step, count)
        target = arrived.at[number % slots, pl.ds(0, count)]
        own_copy = pltpu.make_async_copy(own[group].at[inside], target, sems.at[number])
        other_copy = pltpu.make_async_copy(other[group].at[inside], target, sems.at[number])
        ahead = info[5 + panels + j] > place
        pl.when(ahead)(other_copy.start)
        pl.when(jnp.logical_not(ahead))(own_copy.start)
        copies.append(own_copy)

    for number in range(slots):
        fetch(number)

    for k in range(n_sec):
        start = pl.multiple_of(partner(section, k, n_sec) * block, block)
        for j in range(panels):
            pending[j, k * block : (k + 1) * block, :] = query[pl.ds(start, block), j * size : (j + 1) * size]

    for number, (_, _, low, count) in enumerate(found):
        copies[number].wait()

        @pl.loop(0, count // 64)
        def _(i):
            inside = pl.ds(pl.multiple_of(i * 64, 64), 64)
            span = pl.ds(pl.multiple_of(low + i * 64, 64), 64)
            low_high[span, :], low_low[span, :] = parts_of(arrived[number % slots, inside, :])

        if number + slots < len(found):
            fetch(number + slots)

    for j in range(panels):
        s = stream.panel_start(j + 1) - stream.packed
        for source, target in ((low_high, inv_high), (low_low, inv_low)):
            target[j] = jnp.zeros((size, size), jnp.bfloat16)
            target[j, 3 * tile :, :] = source[s : s + tile, :]
            target[j, 2 * tile : 3 * tile, : 3 * tile] = source[s + tile : s + 2 * tile, : 3 * tile]
            target[j, :tile, :tile] = source[s + tile : s + 2 * tile, 3 * tile :]
            middle = tile + tile // 2
            target[j, tile:middle, : 2 * tile] = source[s + 2 * tile : s + stream.packed, : 2 * tile]
            target[j, middle : 2 * tile, : 2 * tile] = source[s + 2 * tile : s + stream.packed, 2 * tile :]

    def below(j, k):
        span = pl.ds(pl.multiple_of(stream.panel_start(j) + (k - j - 1) * size, 64), size)
        return low_high[span, :], low_low[span, :]

    @pl.loop(0, panels)
    def _(j):
        solved = dot_parts(parts_of(pending[j]), (inv_high[j], inv_low[j]), 1)
        pending[j] = solved
        part_high[...], part_low[...] = parts_of(solved)

        @pl.loop(j + 1, panels)
        def _(k):
            pending[k] = pending[k] - dot_parts((part_high[...], part_low[...]), below(j, k), 1)

    @pl.loop(0, panels)
    def _(step_number):
        j = panels - 1 - step_number

        @pl.loop(j + 1, panels)
        def _(k):
            pending[j] = pending[j] - dot_parts((out_high[k], out_low[k]), below(j, k), 0)

        answer = dot_parts(parts_of(pending[j]), (inv_high[j], inv_low[j]), 0)
        out_high[j], out_low[j] = parts_of(answer)


def swept(stream, n_sec, info, earlier, query, own, other):
    rows = query.shape[0]
    panels, size, total = stream.panels, stream.size, stream.total
    out = jax.ShapeDtypeStruct((panels, rows, size), jnp.bfloat16)
    return pl.pallas_call(
        functools.partial(sweep_kernel, stream, n_sec),
        out_shape=(out, out, jax.ShapeDtypeStruct((8, 128), jnp.float32)),
        in_specs=[SMEM, HBM, VMEM] + [HBM] * (len(own) + len(other)),
        out_specs=(VMEM, VMEM, VMEM),
        scratch_shapes=[
            pltpu.VMEM((total, size), jnp.bfloat16),
            pltpu.VMEM((total, size), jnp.bfloat16),
            pltpu.VMEM((panels, size, size), jnp.bfloat16),
            pltpu.VMEM((panels, size, size), jnp.bfloat16),
            pltpu.VMEM((panels, rows, size), jnp.float32),
            pltpu.VMEM((rows, size), jnp.bfloat16),
            pltpu.VMEM((rows, size), jnp.bfloat16),
            pltpu.VMEM((4, size, size), jnp.float32),
            pltpu.SemaphoreType.DMA((len(stream.pieces) + len(GROUPS),)),
        ],
        compiler_params=param(32),
        cost_estimate=cost(0, 1000),
    )(info, earlier, query, *[pltpu.with_memory_space_constraint(x, pltpu.HBM) for x in (*own, *other)])


def score_kernel(n_sec, scale, blocks, counts, earlier, high, low, *refs):
    trains, outs = refs[: len(blocks)], refs[len(blocks) : len(blocks) + n_sec]
    train_high, train_low, total = refs[-3:]
    panels, rows, size = high.shape
    cols = total.shape[1]
    col = lax.broadcasted_iota(jnp.int32, (1, cols), 1)
    start, limit = 0, None
    for (length, which, first), train in zip(blocks, trains):
        for p in range(panels):
            span = slice(start, start + length)
            train_high[p, span, :], train_low[p, span, :] = parts_of(train[:, p * size : (p + 1) * size])
        bound = jnp.full_like(col, counts[which] - first + start)
        limit = bound if limit is None else jnp.where(col >= start, bound, limit)
        start += length
    total[...] = jnp.zeros_like(total)

    @pl.loop(0, panels)
    def _(p):
        total[...] += dot_parts((high[p], low[p]), (train_high[p], train_low[p]), 1)

    factor = jnp.where(col < limit, scale, 0.0).astype(jnp.float32)
    share = rows // n_sec
    for k in range(n_sec):
        outs[k][...] = total[k * share : (k + 1) * share, :] * factor


def scored(n_sec, scale, counts, earlier, high, low, runs):
    panels, rows, size = high.shape
    blocks = [(train.shape[0], which, first) for train, which, first in runs]
    cols = sum(length for length, _, _ in blocks)
    return pl.pallas_call(
        functools.partial(score_kernel, n_sec, scale, blocks),
        out_shape=tuple(jax.ShapeDtypeStruct((rows // n_sec, cols), jnp.float32) for _ in range(n_sec)),
        in_specs=[SMEM, HBM] + [VMEM] * (2 + len(runs)),
        out_specs=tuple(VMEM for _ in range(n_sec)),
        scratch_shapes=[
            pltpu.VMEM((panels, cols, size), jnp.bfloat16),
            pltpu.VMEM((panels, cols, size), jnp.bfloat16),
            pltpu.VMEM((rows, cols), jnp.float32),
        ],
        compiler_params=param(24),
        cost_estimate=cost(0, 1000),
    )(counts, earlier, high, low, *[train for train, _, _ in runs])


def body(query_gradient_stack, train_grads, factor_slots, owner, train_count):
    query, train, slot, owners = query_gradient_stack[0], train_grads[0], factor_slots[0, 0], owner[0]
    rows, coords = query.shape
    size = slot.shape[1]
    panels = coords // size
    n_dp, n_sec = lax.axis_size("dp"), lax.axis_size("section")
    chips = n_dp // 2
    stream = Stream(panels, size)
    me = lax.axis_index("dp")
    section = lax.axis_index("section")
    chip, core = lax.shift_right_logical(me, 1), me & 1
    first_core = core == 0
    place = jnp.where(first_core, chip, chips - 1 - chip)
    owner_chip = lax.shift_right_logical(owners, 1)
    owner_place = jnp.where(first_core, owner_chip, chips - 1 - owner_chip)
    info = jnp.concatenate([jnp.stack([chip, core, place, me, section]), owners, owner_place])

    swap_pairs = [(d, d ^ 1) for d in range(n_dp)]
    next_chip = [(d, (d + 2) % n_dp) for d in range(n_dp)]

    def swapped(value):
        return lax.ppermute(value, "dp", swap_pairs)

    cuts = [sum(TRAIN_CUTS[:i]) for i in range(len(TRAIN_CUTS) + 1)]
    first_part, slot = lax.optimization_barrier((train[: cuts[1]], slot))
    far = [lax.ppermute(first_part, "dp", next_chip)]

    def send_train(index, *earlier):
        part = ordered(train[cuts[index] : cuts[index + 1]], *earlier)
        far.append(lax.ppermute(part, "dp", next_chip))
        return part

    peer = swapped(slot)
    packed = inverted_diagonal(panels, info, slot)
    own_rows = build_stream(stream, chips, info, slot, peer, packed, swapped(packed))
    count_2 = lax.ppermute(train_count, "dp", next_chip)
    count_1 = lax.ppermute(train_count, "dp", [(d, (d + 1) % n_dp) for d in range(n_dp)])
    counts = jnp.concatenate([train_count, count_1, count_2])

    got, own, other = {}, [], []
    steps = CHUNKS + SKEW * (chips - 2)
    for number in range(steps):
        earlier = [corner(far[0])] if number == 0 else [block]
        block = step_block(stream, number, info, counts, own_rows, got, earlier)
        pairs = []
        for p in range(chips - 1):
            if 0 <= number - SKEW * p < CHUNKS:
                pairs += [(2 * p, 2 * p + 2), (2 * (chips - 1 - p) + 1, 2 * (chips - 2 - p) + 1)]
        got[number] = lax.ppermute(block, "dp", pairs)
        for first, last in GROUPS:
            if number == last - 1 + SKEW * (chips - 2):
                before = [corner(rows_before) for rows_before in other[:2]] if last == CHUNKS else []
                value = collected(stream, chips, first, last, info, own_rows, got, before)
                own.append(value)
                other.append(swapped(value))

    part = send_train(1, corner(other[-1]))
    high, low, swept_token = swept(stream, n_sec, info, corner(part), query, own, other)
    for index in range(2, len(cuts) - 1):
        send_train(index, swept_token)

    scale = (coords * n_sec) ** (-0.5)

    def summed(parts):
        total = parts[0]
        for k in range(1, n_sec):
            if n_sec & (n_sec - 1) == 0:
                pairs = [(s, s ^ k) for s in range(n_sec)]
            else:
                pairs = [(s, (s + k) % n_sec) for s in range(n_sec)]
            total = total + lax.ppermute(parts[k], "section", pairs)
        return total

    def near_rows(index, *earlier):
        return swapped(chosen(info, train, cuts[index], far[index], *earlier))

    runs = [(train, 0, 0), (near_rows(0, swept_token), 1, 0), (far[0], 2, 0)]
    near_scores, far_scores, summed_corners, earlier = [], [], [], [swept_token]
    for index in range(len(cuts) - 1):
        if index:
            runs = [(near_rows(index, *earlier), 1, cuts[index]), (far[index], 2, cuts[index])]
        parts = scored(n_sec, scale, counts, earlier[0], high, low, runs)
        both = summed(parts)
        summed_corners.append(corner(both))
        earlier = [corner(parts[0])] + (summed_corners if index else [])
        length = cuts[index + 1] - cuts[index]
        if index == 0:
            own_scores, both = both[:, :rows], both[:, rows:]
        near_scores.append(both[:, :length])
        far_scores.append(both[:, length:])
    return jnp.concatenate([own_scores] + near_scores + far_scores, axis=1)[None]


def solution(mesh):
    in_specs = (
        P("section", "dp", None),
        P("section", "dp", None),
        P("section", "dp", None, None),
        P("section", None),
        P("dp"),
    )
    out_specs = P("dp", "section", None)
    return jax.shard_map(body, mesh=mesh, in_specs=in_specs, out_specs=out_specs, check_vma=False)
```

```python
import functools

import jax
import jax.numpy as jnp
from jax import lax
from jax.experimental import pallas as pl
from jax.experimental.pallas import tpu as pltpu
from jax.sharding import PartitionSpec as P

HIGHEST = lax.Precision.HIGHEST
CHUNKS = 17
SKEW = 2
GROUPS = ((0, 4), (4, 8), (8, 12), (12, 17))
TRAIN_CUTS = (96, 256, 160)
MIB = 1024 * 1024
HBM = pl.BlockSpec(memory_space=pltpu.HBM)
SMEM = pl.BlockSpec(memory_space=pltpu.SMEM)
VMEM = pl.BlockSpec(memory_space=pltpu.VMEM)


def dot(a, b, contract, precision=None):
    return lax.dot_general(
        a, b, (((1,), (contract,)), ((), ())), precision=precision, preferred_element_type=jnp.float32
    )


def parts_of(value):
    high = value.astype(jnp.bfloat16)
    return high, (value - high.astype(jnp.float32)).astype(jnp.bfloat16)


def dot_parts(a, b, contract):
    return dot(a[0], b[0], contract) + (dot(a[0], b[1], contract) + dot(a[1], b[0], contract))


def partner(section, k, n_sec):
    if n_sec & (n_sec - 1) == 0:
        return section ^ k
    return lax.rem(section + k, n_sec)


def param(limit_mib):
    return pltpu.CompilerParams(vmem_limit_bytes=limit_mib * MIB)


def cost(flops, moved):
    return pl.CostEstimate(flops=flops, bytes_accessed=moved, transcendentals=0)


def order_kernel(*refs):
    del refs


def ordered(value, *earlier):
    return pl.pallas_call(
        order_kernel,
        out_shape=jax.ShapeDtypeStruct(value.shape, value.dtype),
        in_specs=[HBM] * (1 + len(earlier)),
        out_specs=HBM,
        input_output_aliases={0: 0},
        cost_estimate=cost(0, 1000),
    )(value, *earlier)


def choose_kernel(start, info, train, far, *refs):
    out, sem = refs[-2:]
    own_copy = pltpu.make_async_copy(train.at[pl.ds(start, out.shape[0])], out, sem)
    far_copy = pltpu.make_async_copy(far, out, sem)
    pl.when(info[1] == 0)(own_copy.start)
    pl.when(info[1] != 0)(far_copy.start)
    own_copy.wait()


def chosen(info, train, start, far, *earlier):
    return pl.pallas_call(
        functools.partial(choose_kernel, start),
        out_shape=jax.ShapeDtypeStruct(far.shape, far.dtype),
        in_specs=[SMEM] + [HBM] * (2 + len(earlier)),
        out_specs=HBM,
        scratch_shapes=[pltpu.SemaphoreType.DMA],
        compiler_params=param(4),
        cost_estimate=cost(0, 1000),
    )(info, train, far, *earlier)


def corner(value):
    return value[:8, :128]


def invert_kernel(panels, info, slot, packed_ref, block_ref, sem):
    size = block_ref.shape[0]
    held = 0
    for j in range(1, panels):
        held = jnp.where(info[5 + j] == info[3], j, held)
    copy = pltpu.make_async_copy(slot.at[pl.ds(pl.multiple_of(held * size, size), size)], block_ref, sem)
    copy.start()
    copy.wait()
    count = 4
    tile = size // count
    row = lax.broadcasted_iota(jnp.int32, (tile, tile), 0)
    col = lax.broadcasted_iota(jnp.int32, (tile, tile), 1)
    spans = [slice(i * tile, (i + 1) * tile) for i in range(count)]
    low = [block_ref[s, s] for s in spans]
    inv = []
    for block in low:
        diagonal = jnp.sum(jnp.where(row == col, block, 0.0), axis=1, keepdims=True)
        inv.append(jnp.where(row == col, 1.0 / diagonal, 0.0))
    width = 1
    while width < tile:
        joins = (row // (2 * width) == col // (2 * width)) & (row // width > col // width)
        half = [dot(jnp.where(joins, low[i], 0.0), inv[i], 0, HIGHEST) for i in range(count)]
        inv = [inv[i] - dot(inv[i], half[i], 0, HIGHEST) for i in range(count)]
        width *= 2
    while len(inv) > 1:
        width = inv[0].shape[0]
        zero = jnp.zeros((width, width), jnp.float32)
        merged = []
        for i in range(0, len(inv), 2):
            below = block_ref[(i + 1) * width : (i + 2) * width, i * width : (i + 1) * width]
            corner = -dot(inv[i + 1], dot(below, inv[i], 0, HIGHEST), 0, HIGHEST)
            top = jnp.concatenate([inv[i], zero], axis=1)
            merged.append(jnp.concatenate([top, jnp.concatenate([corner, inv[i + 1]], axis=1)], axis=0))
        inv = merged
    whole = inv[0]
    mid = tile + tile // 2
    packed_ref[0:tile, :] = whole[3 * tile :, :]
    packed_ref[tile : 2 * tile, 0 : 3 * tile] = whole[2 * tile : 3 * tile, 0 : 3 * tile]
    packed_ref[tile : 2 * tile, 3 * tile :] = whole[0:tile, 0:tile]
    packed_ref[2 * tile :, 0 : 2 * tile] = whole[tile:mid, 0 : 2 * tile]
    packed_ref[2 * tile :, 2 * tile :] = whole[mid : 2 * tile, 0 : 2 * tile]


def inverted_diagonal(panels, info, slot):
    size = slot.shape[1]
    rows = size // 2 + size // 8
    return pl.pallas_call(
        functools.partial(invert_kernel, panels),
        out_shape=jax.ShapeDtypeStruct((rows, size), jnp.float32),
        in_specs=[SMEM, HBM],
        out_specs=VMEM,
        scratch_shapes=[pltpu.VMEM((size, size), jnp.float32), pltpu.SemaphoreType.DMA],
        compiler_params=param(16),
        cost_estimate=cost(0, 1000),
    )(info, slot)


class Stream:
    def __init__(self, panels, size):
        self.panels, self.size = panels, size
        self.packed = size // 2 + size // 8
        self.pieces, self.starts, start = [], [], 0
        for j in range(panels):
            for k in [*range(j + 1, panels), None]:
                self.pieces.append((j, k))
                self.starts.append(start)
                start += self.packed if k is None else size
        self.total = start
        self.step = start // CHUNKS

    def rows(self, piece):
        return self.packed if self.pieces[piece][1] is None else self.size

    def panel_start(self, j):
        last = self.panels - 1
        return j * self.packed + self.size * (j * last - (j * (j - 1)) // 2)

    def cuts(self, edges):
        found = []
        for piece, (j, _) in enumerate(self.pieces):
            stop = self.starts[piece] + self.rows(piece)
            for number, (low, high) in enumerate(edges):
                low, high = max(low, self.starts[piece]), min(high, stop)
                if low < high:
                    found.append((j, number, low, high - low))
        return found


def build_kernel(stream, info, slot, peer, packed, peer_packed, out, sems):
    place, me = info[2], info[3]
    pending = []
    for piece, (j, k) in enumerate(stream.pieces):
        count = stream.rows(piece)
        mine, theirs = packed, peer_packed
        if k is not None:
            span = pl.ds(k * stream.size, count)
            mine, theirs = slot.at[span], peer.at[span]
        is_mine = info[5 + j] == me
        target = out.at[pl.ds(pl.multiple_of(place * (SKEW * stream.step) + stream.starts[piece], 8), count)]
        own_copy = pltpu.make_async_copy(mine, target, sems.at[piece])
        peer_copy = pltpu.make_async_copy(theirs, target, sems.at[piece])
        pl.when(is_mine)(own_copy.start)
        pl.when(jnp.logical_not(is_mine))(peer_copy.start)
        pending.append(peer_copy)
    for copy in pending:
        copy.wait()


def build_stream(stream, chips, info, slot, peer, packed, peer_packed):
    rows = stream.total + SKEW * stream.step * (chips - 1)
    return pl.pallas_call(
        functools.partial(build_kernel, stream),
        out_shape=jax.ShapeDtypeStruct((rows, stream.size), jnp.float32),
        in_specs=[SMEM] + [HBM] * 4,
        out_specs=HBM,
        scratch_shapes=[pltpu.SemaphoreType.DMA((len(stream.pieces),))],
        compiler_params=param(4),
        cost_estimate=cost(0, 1000),
    )(info, slot, peer, packed, peer_packed)


def step_kernel(stream, number, info, counts, own, *refs):
    del counts
    out, sems = refs[-2:]
    unit = stream.packed // 5
    place = info[2]
    pending = []
    for g in range(stream.step // unit):
        inside = pl.ds(g * unit, unit)
        copy = pltpu.make_async_copy(
            own.at[pl.ds(number * stream.step + g * unit, unit)], out.at[inside], sems.at[g]
        )
        pending.append(copy)
        if number < SKEW:
            copy.start()
            continue
        row = number * stream.step + g * unit - place * (SKEW * stream.step)
        origin = info[5 + stream.panels]
        for j in range(1, stream.panels):
            origin = jnp.where(row >= stream.panel_start(j), info[5 + stream.panels + j], origin)
        passing = pltpu.make_async_copy(refs[0].at[inside], out.at[inside], sems.at[g])
        pl.when(origin < place)(passing.start)
        pl.when(origin >= place)(copy.start)
    for copy in pending:
        copy.wait()


def step_block(stream, number, info, counts, own, got, earlier):
    operands = ([got[number - SKEW]] if number >= SKEW else []) + earlier
    return pl.pallas_call(
        functools.partial(step_kernel, stream, number),
        out_shape=jax.ShapeDtypeStruct((stream.step, stream.size), jnp.float32),
        in_specs=[SMEM, SMEM] + [HBM] * (1 + len(operands)),
        out_specs=HBM,
        scratch_shapes=[pltpu.SemaphoreType.DMA((stream.step * 5 // stream.packed,))],
        compiler_params=param(4),
        cost_estimate=cost(0, 1000),
    )(info, counts, own, *operands)


def collect_kernel(stream, chips, first, last, info, own, *refs):
    received, out, sems = refs[:-2], refs[-2], refs[-1]
    place = info[2]
    pending = []
    step = stream.step
    edges = [(i * step, (i + 1) * step) for i in range(first, last)]
    for number, (j, i, low, count) in enumerate(stream.cuts(edges)):
        here = info[5 + stream.panels + j] >= place
        target = out.at[pl.ds(low - first * step, count)]
        start = pl.multiple_of(place * (SKEW * step) + low, 8)
        own_copy = pltpu.make_async_copy(own.at[pl.ds(start, count)], target, sems.at[number])
        pl.when(here)(own_copy.start)
        for p in range(1, chips):
            source = received[i + SKEW * (p - 1)].at[pl.ds(low - (first + i) * step, count)]
            copy = pltpu.make_async_copy(source, target, sems.at[number])
            pl.when(jnp.logical_not(here) & (place == p))(copy.start)
        pending.append(own_copy)
    for copy in pending:
        copy.wait()


def collected(stream, chips, first, last, info, own, got, earlier):
    received = [got[s] for s in range(first, last + SKEW * (chips - 2))]
    return pl.pallas_call(
        functools.partial(collect_kernel, stream, chips, first, last),
        out_shape=pltpu.HBM(((last - first) * stream.step, stream.size), jnp.float32),
        in_specs=[SMEM] + [HBM] * (1 + len(received) + len(earlier)),
        out_specs=HBM,
        scratch_shapes=[pltpu.SemaphoreType.DMA(((last - first) * len(stream.pieces),))],
        compiler_params=param(4),
        cost_estimate=cost(0, 1000),
    )(info, own, *received, *earlier)


def sweep_kernel(stream, n_sec, info, earlier, query, *refs):
    groups = len(GROUPS)
    own, other = refs[:groups], refs[groups : 2 * groups]
    out_high, out_low, done_ref, low_high, low_low, inv_high, inv_low, pending, part_high, part_low = refs[2 * groups : -2]
    arrived, sems = refs[-2:]
    done_ref[...] = jnp.zeros_like(done_ref)
    place, section = info[2], info[4]
    panels, size, step = stream.panels, stream.size, stream.step
    rows = query.shape[0]
    block = rows // n_sec
    tile = size // 4

    slots = arrived.shape[0]
    found = stream.cuts([(first * step, last * step) for first, last in GROUPS])
    copies = []

    def fetch(number):
        j, group, low, count = found[number]
        inside = pl.ds(low - GROUPS[group][0] * step, count)
        target = arrived.at[number % slots, pl.ds(0, count)]
        own_copy = pltpu.make_async_copy(own[group].at[inside], target, sems.at[number])
        other_copy = pltpu.make_async_copy(other[group].at[inside], target, sems.at[number])
        ahead = info[5 + panels + j] > place
        pl.when(ahead)(other_copy.start)
        pl.when(jnp.logical_not(ahead))(own_copy.start)
        copies.append(own_copy)

    for number in range(slots):
        fetch(number)

    for k in range(n_sec):
        start = pl.multiple_of(partner(section, k, n_sec) * block, block)
        for j in range(panels):
            pending[j, k * block : (k + 1) * block, :] = query[pl.ds(start, block), j * size : (j + 1) * size]

    for number, (_, _, low, count) in enumerate(found):
        copies[number].wait()

        @pl.loop(0, count // 64)
        def _(i):
            inside = pl.ds(pl.multiple_of(i * 64, 64), 64)
            span = pl.ds(pl.multiple_of(low + i * 64, 64), 64)
            low_high[span, :], low_low[span, :] = parts_of(arrived[number % slots, inside, :])

        if number + slots < len(found):
            fetch(number + slots)

    for j in range(panels):
        s = stream.panel_start(j + 1) - stream.packed
        for source, target in ((low_high, inv_high), (low_low, inv_low)):
            target[j] = jnp.zeros((size, size), jnp.bfloat16)
            target[j, 3 * tile :, :] = source[s : s + tile, :]
            target[j, 2 * tile : 3 * tile, : 3 * tile] = source[s + tile : s + 2 * tile, : 3 * tile]
            target[j, :tile, :tile] = source[s + tile : s + 2 * tile, 3 * tile :]
            middle = tile + tile // 2
            target[j, tile:middle, : 2 * tile] = source[s + 2 * tile : s + stream.packed, : 2 * tile]
            target[j, middle : 2 * tile, : 2 * tile] = source[s + 2 * tile : s + stream.packed, 2 * tile :]

    def below(j, k):
        span = pl.ds(pl.multiple_of(stream.panel_start(j) + (k - j - 1) * size, 64), size)
        return low_high[span, :], low_low[span, :]

    @pl.loop(0, panels)
    def _(j):
        solved = dot_parts(parts_of(pending[j]), (inv_high[j], inv_low[j]), 1)
        pending[j] = solved
        part_high[...], part_low[...] = parts_of(solved)

        @pl.loop(j + 1, panels)
        def _(k):
            pending[k] = pending[k] - dot_parts((part_high[...], part_low[...]), below(j, k), 1)

    @pl.loop(0, panels)
    def _(step_number):
        j = panels - 1 - step_number

        @pl.loop(j + 1, panels)
        def _(k):
            pending[j] = pending[j] - dot_parts((out_high[k], out_low[k]), below(j, k), 0)

        answer = dot_parts(parts_of(pending[j]), (inv_high[j], inv_low[j]), 0)
        out_high[j], out_low[j] = parts_of(answer)


def swept(stream, n_sec, info, earlier, query, own, other):
    rows = query.shape[0]
    panels, size, total = stream.panels, stream.size, stream.total
    out = jax.ShapeDtypeStruct((panels, rows, size), jnp.bfloat16)
    return pl.pallas_call(
        functools.partial(sweep_kernel, stream, n_sec),
        out_shape=(out, out, jax.ShapeDtypeStruct((8, 128), jnp.float32)),
        in_specs=[SMEM, HBM, VMEM] + [HBM] * (len(own) + len(other)),
        out_specs=(VMEM, VMEM, VMEM),
        scratch_shapes=[
            pltpu.VMEM((total, size), jnp.bfloat16),
            pltpu.VMEM((total, size), jnp.bfloat16),
            pltpu.VMEM((panels, size, size), jnp.bfloat16),
            pltpu.VMEM((panels, size, size), jnp.bfloat16),
            pltpu.VMEM((panels, rows, size), jnp.float32),
            pltpu.VMEM((rows, size), jnp.bfloat16),
            pltpu.VMEM((rows, size), jnp.bfloat16),
            pltpu.VMEM((4, size, size), jnp.float32),
            pltpu.SemaphoreType.DMA((len(stream.pieces) + len(GROUPS),)),
        ],
        compiler_params=param(32),
        cost_estimate=cost(0, 1000),
    )(info, earlier, query, *[pltpu.with_memory_space_constraint(x, pltpu.HBM) for x in (*own, *other)])


def score_kernel(n_sec, scale, blocks, counts, earlier, high, low, *refs):
    trains, outs = refs[: len(blocks)], refs[len(blocks) : len(blocks) + n_sec]
    train_high, train_low, total = refs[-3:]
    panels, rows, size = high.shape
    cols = total.shape[1]
    col = lax.broadcasted_iota(jnp.int32, (1, cols), 1)
    start, limit = 0, None
    for (length, which, first), train in zip(blocks, trains):
        for p in range(panels):
            span = slice(start, start + length)
            train_high[p, span, :], train_low[p, span, :] = parts_of(train[:, p * size : (p + 1) * size])
        bound = jnp.full_like(col, counts[which] - first + start)
        limit = bound if limit is None else jnp.where(col >= start, bound, limit)
        start += length
    total[...] = jnp.zeros_like(total)

    @pl.loop(0, panels)
    def _(p):
        total[...] += dot_parts((high[p], low[p]), (train_high[p], train_low[p]), 1)

    factor = jnp.where(col < limit, scale, 0.0).astype(jnp.float32)
    share = rows // n_sec
    for k in range(n_sec):
        outs[k][...] = total[k * share : (k + 1) * share, :] * factor


def scored(n_sec, scale, counts, earlier, high, low, runs):
    panels, rows, size = high.shape
    blocks = [(train.shape[0], which, first) for train, which, first in runs]
    cols = sum(length for length, _, _ in blocks)
    return pl.pallas_call(
        functools.partial(score_kernel, n_sec, scale, blocks),
        out_shape=tuple(jax.ShapeDtypeStruct((rows // n_sec, cols), jnp.float32) for _ in range(n_sec)),
        in_specs=[SMEM, HBM] + [VMEM] * (2 + len(runs)),
        out_specs=tuple(VMEM for _ in range(n_sec)),
        scratch_shapes=[
            pltpu.VMEM((panels, cols, size), jnp.bfloat16),
            pltpu.VMEM((panels, cols, size), jnp.bfloat16),
            pltpu.VMEM((rows, cols), jnp.float32),
        ],
        compiler_params=param(24),
        cost_estimate=cost(0, 1000),
    )(counts, earlier, high, low, *[train for train, _, _ in runs])


def body(query_gradient_stack, train_grads, factor_slots, owner, train_count):
    query, train, slot, owners = query_gradient_stack[0], train_grads[0], factor_slots[0, 0], owner[0]
    rows, coords = query.shape
    size = slot.shape[1]
    panels = coords // size
    n_dp, n_sec = lax.axis_size("dp"), lax.axis_size("section")
    chips = n_dp // 2
    stream = Stream(panels, size)
    me = lax.axis_index("dp")
    section = lax.axis_index("section")
    chip, core = lax.shift_right_logical(me, 1), me & 1
    first_core = core == 0
    place = jnp.where(first_core, chip, chips - 1 - chip)
    owner_chip = lax.shift_right_logical(owners, 1)
    owner_place = jnp.where(first_core, owner_chip, chips - 1 - owner_chip)
    info = jnp.concatenate([jnp.stack([chip, core, place, me, section]), owners, owner_place])

    swap_pairs = [(d, d ^ 1) for d in range(n_dp)]
    next_chip = [(d, (d + 2) % n_dp) for d in range(n_dp)]

    def swapped(value):
        return lax.ppermute(value, "dp", swap_pairs)

    cuts = [sum(TRAIN_CUTS[:i]) for i in range(len(TRAIN_CUTS) + 1)]
    first_part, slot = lax.optimization_barrier((train[: cuts[1]], slot))
    far = [lax.ppermute(first_part, "dp", next_chip)]

    def send_train(index, *earlier):
        part = ordered(train[cuts[index] : cuts[index + 1]], *earlier)
        far.append(lax.ppermute(part, "dp", next_chip))
        return part

    peer = swapped(slot)
    packed = inverted_diagonal(panels, info, slot)
    own_rows = build_stream(stream, chips, info, slot, peer, packed, swapped(packed))
    count_2 = lax.ppermute(train_count, "dp", next_chip)
    count_1 = lax.ppermute(train_count, "dp", [(d, (d + 1) % n_dp) for d in range(n_dp)])
    counts = jnp.concatenate([train_count, count_1, count_2])

    got, own, other = {}, [], []
    steps = CHUNKS + SKEW * (chips - 2)
    for number in range(steps):
        earlier = [corner(far[0])] if number == 0 else [block]
        block = step_block(stream, number, info, counts, own_rows, got, earlier)
        pairs = []
        for p in range(chips - 1):
            if 0 <= number - SKEW * p < CHUNKS:
                pairs += [(2 * p, 2 * p + 2), (2 * (chips - 1 - p) + 1, 2 * (chips - 2 - p) + 1)]
        got[number] = lax.ppermute(block, "dp", pairs)
        for first, last in GROUPS:
            if number == last - 1 + SKEW * (chips - 2):
                before = [corner(rows_before) for rows_before in other[:2]] if last == CHUNKS else []
                value = collected(stream, chips, first, last, info, own_rows, got, before)
                own.append(value)
                other.append(swapped(value))

    part = send_train(1, corner(other[-1]))
    high, low, swept_token = swept(stream, n_sec, info, corner(part), query, own, other)
    for index in range(2, len(cuts) - 1):
        send_train(index, swept_token)

    scale = (coords * n_sec) ** (-0.5)

    def summed(parts):
        total = parts[0]
        for k in range(1, n_sec):
            if n_sec & (n_sec - 1) == 0:
                pairs = [(s, s ^ k) for s in range(n_sec)]
            else:
                pairs = [(s, (s + k) % n_sec) for s in range(n_sec)]
            total = total + lax.ppermute(parts[k], "section", pairs)
        return total

    def near_rows(index, *earlier):
        return swapped(chosen(info, train, cuts[index], far[index], *earlier))

    runs = [(train, 0, 0), (near_rows(0, swept_token), 1, 0), (far[0], 2, 0)]
    near_scores, far_scores, summed_corners, earlier = [], [], [], [swept_token]
    for index in range(len(cuts) - 1):
        if index:
            runs = [(near_rows(index, *earlier), 1, cuts[index]), (far[index], 2, cuts[index])]
        parts = scored(n_sec, scale, counts, earlier[0], high, low, runs)
        both = summed(parts)
        summed_corners.append(corner(both))
        earlier = [corner(parts[0])] + (summed_corners if index else [])
        length = cuts[index + 1] - cuts[index]
        if index == 0:
            own_scores, both = both[:, :rows], both[:, rows:]
        near_scores.append(both[:, :length])
        far_scores.append(both[:, length:])
    return jnp.concatenate([own_scores] + near_scores + far_scores, axis=1)[None]


def solution(mesh):
    in_specs = (
        P("section", "dp", None),
        P("section", "dp", None),
        P("section", "dp", None, None),
        P("section", None),
        P("dp"),
    )
    out_specs = P("dp", "section", None)
    return jax.shard_map(body, mesh=mesh, in_specs=in_specs, out_specs=out_specs, check_vma=False)
```

```python
import functools

import jax
import jax.numpy as jnp
from jax import lax
from jax.experimental import pallas as pl
from jax.experimental.pallas import tpu as pltpu
from jax.sharding import PartitionSpec as P

HIGHEST = lax.Precision.HIGHEST
CHUNKS = 17
SKEW = 2
GROUPS = ((0, 4), (4, 8), (8, 12), (12, 17))
TRAIN_CUTS = (112, 256, 144)
MIB = 1024 * 1024
HBM = pl.BlockSpec(memory_space=pltpu.HBM)
SMEM = pl.BlockSpec(memory_space=pltpu.SMEM)
VMEM = pl.BlockSpec(memory_space=pltpu.VMEM)


def dot(a, b, contract, precision=None):
    return lax.dot_general(
        a, b, (((1,), (contract,)), ((), ())), precision=precision, preferred_element_type=jnp.float32
    )


def parts_of(value):
    high = value.astype(jnp.bfloat16)
    return high, (value - high.astype(jnp.float32)).astype(jnp.bfloat16)


def dot_parts(a, b, contract):
    return dot(a[0], b[0], contract) + (dot(a[0], b[1], contract) + dot(a[1], b[0], contract))


def partner(section, k, n_sec):
    if n_sec & (n_sec - 1) == 0:
        return section ^ k
    return lax.rem(section + k, n_sec)


def param(limit_mib):
    return pltpu.CompilerParams(vmem_limit_bytes=limit_mib * MIB)


def cost(flops, moved):
    return pl.CostEstimate(flops=flops, bytes_accessed=moved, transcendentals=0)


def order_kernel(*refs):
    del refs


def ordered(value, *earlier):
    return pl.pallas_call(
        order_kernel,
        out_shape=jax.ShapeDtypeStruct(value.shape, value.dtype),
        in_specs=[HBM] * (1 + len(earlier)),
        out_specs=HBM,
        input_output_aliases={0: 0},
        cost_estimate=cost(0, 1000),
    )(value, *earlier)


def choose_kernel(start, info, train, far, *refs):
    out, sem = refs[-2:]
    own_copy = pltpu.make_async_copy(train.at[pl.ds(start, out.shape[0])], out, sem)
    far_copy = pltpu.make_async_copy(far, out, sem)
    pl.when(info[1] == 0)(own_copy.start)
    pl.when(info[1] != 0)(far_copy.start)
    own_copy.wait()


def chosen(info, train, start, far, *earlier):
    return pl.pallas_call(
        functools.partial(choose_kernel, start),
        out_shape=jax.ShapeDtypeStruct(far.shape, far.dtype),
        in_specs=[SMEM] + [HBM] * (2 + len(earlier)),
        out_specs=HBM,
        scratch_shapes=[pltpu.SemaphoreType.DMA],
        compiler_params=param(4),
        cost_estimate=cost(0, 1000),
    )(info, train, far, *earlier)


def corner(value):
    return value[:8, :128]


def invert_kernel(panels, info, slot, packed_ref, block_ref, sem):
    size = block_ref.shape[0]
    held = 0
    for j in range(1, panels):
        held = jnp.where(info[5 + j] == info[3], j, held)
    copy = pltpu.make_async_copy(slot.at[pl.ds(pl.multiple_of(held * size, size), size)], block_ref, sem)
    copy.start()
    copy.wait()
    count = 4
    tile = size // count
    row = lax.broadcasted_iota(jnp.int32, (tile, tile), 0)
    col = lax.broadcasted_iota(jnp.int32, (tile, tile), 1)
    spans = [slice(i * tile, (i + 1) * tile) for i in range(count)]
    low = [block_ref[s, s] for s in spans]
    inv = []
    for block in low:
        diagonal = jnp.sum(jnp.where(row == col, block, 0.0), axis=1, keepdims=True)
        inv.append(jnp.where(row == col, 1.0 / diagonal, 0.0))
    width = 1
    while width < tile:
        joins = (row // (2 * width) == col // (2 * width)) & (row // width > col // width)
        half = [dot(jnp.where(joins, low[i], 0.0), inv[i], 0, HIGHEST) for i in range(count)]
        inv = [inv[i] - dot(inv[i], half[i], 0, HIGHEST) for i in range(count)]
        width *= 2
    while len(inv) > 1:
        width = inv[0].shape[0]
        zero = jnp.zeros((width, width), jnp.float32)
        merged = []
        for i in range(0, len(inv), 2):
            below = block_ref[(i + 1) * width : (i + 2) * width, i * width : (i + 1) * width]
            corner = -dot(inv[i + 1], dot(below, inv[i], 0, HIGHEST), 0, HIGHEST)
            top = jnp.concatenate([inv[i], zero], axis=1)
            merged.append(jnp.concatenate([top, jnp.concatenate([corner, inv[i + 1]], axis=1)], axis=0))
        inv = merged
    whole = inv[0]
    mid = tile + tile // 2
    packed_ref[0:tile, :] = whole[3 * tile :, :]
    packed_ref[tile : 2 * tile, 0 : 3 * tile] = whole[2 * tile : 3 * tile, 0 : 3 * tile]
    packed_ref[tile : 2 * tile, 3 * tile :] = whole[0:tile, 0:tile]
    packed_ref[2 * tile :, 0 : 2 * tile] = whole[tile:mid, 0 : 2 * tile]
    packed_ref[2 * tile :, 2 * tile :] = whole[mid : 2 * tile, 0 : 2 * tile]


def inverted_diagonal(panels, info, slot):
    size = slot.shape[1]
    rows = size // 2 + size // 8
    return pl.pallas_call(
        functools.partial(invert_kernel, panels),
        out_shape=jax.ShapeDtypeStruct((rows, size), jnp.float32),
        in_specs=[SMEM, HBM],
        out_specs=VMEM,
        scratch_shapes=[pltpu.VMEM((size, size), jnp.float32), pltpu.SemaphoreType.DMA],
        compiler_params=param(16),
        cost_estimate=cost(0, 1000),
    )(info, slot)


class Stream:
    def __init__(self, panels, size):
        self.panels, self.size = panels, size
        self.packed = size // 2 + size // 8
        self.pieces, self.starts, start = [], [], 0
        for j in range(panels):
            for k in [*range(j + 1, panels), None]:
                self.pieces.append((j, k))
                self.starts.append(start)
                start += self.packed if k is None else size
        self.total = start
        self.step = start // CHUNKS

    def rows(self, piece):
        return self.packed if self.pieces[piece][1] is None else self.size

    def panel_start(self, j):
        last = self.panels - 1
        return j * self.packed + self.size * (j * last - (j * (j - 1)) // 2)

    def cuts(self, edges):
        found = []
        for piece, (j, _) in enumerate(self.pieces):
            stop = self.starts[piece] + self.rows(piece)
            for number, (low, high) in enumerate(edges):
                low, high = max(low, self.starts[piece]), min(high, stop)
                if low < high:
                    found.append((j, number, low, high - low))
        return found


def build_kernel(stream, info, slot, peer, packed, peer_packed, out, sems):
    place, me = info[2], info[3]
    pending = []
    for piece, (j, k) in enumerate(stream.pieces):
        count = stream.rows(piece)
        mine, theirs = packed, peer_packed
        if k is not None:
            span = pl.ds(k * stream.size, count)
            mine, theirs = slot.at[span], peer.at[span]
        is_mine = info[5 + j] == me
        target = out.at[pl.ds(pl.multiple_of(place * (SKEW * stream.step) + stream.starts[piece], 8), count)]
        own_copy = pltpu.make_async_copy(mine, target, sems.at[piece])
        peer_copy = pltpu.make_async_copy(theirs, target, sems.at[piece])
        pl.when(is_mine)(own_copy.start)
        pl.when(jnp.logical_not(is_mine))(peer_copy.start)
        pending.append(peer_copy)
    for copy in pending:
        copy.wait()


def build_stream(stream, chips, info, slot, peer, packed, peer_packed):
    rows = stream.total + SKEW * stream.step * (chips - 1)
    return pl.pallas_call(
        functools.partial(build_kernel, stream),
        out_shape=jax.ShapeDtypeStruct((rows, stream.size), jnp.float32),
        in_specs=[SMEM] + [HBM] * 4,
        out_specs=HBM,
        scratch_shapes=[pltpu.SemaphoreType.DMA((len(stream.pieces),))],
        compiler_params=param(4),
        cost_estimate=cost(0, 1000),
    )(info, slot, peer, packed, peer_packed)


def step_kernel(stream, number, info, counts, own, *refs):
    del counts
    out, sems = refs[-2:]
    unit = stream.packed // 5
    place = info[2]
    pending = []
    for g in range(stream.step // unit):
        inside = pl.ds(g * unit, unit)
        copy = pltpu.make_async_copy(
            own.at[pl.ds(number * stream.step + g * unit, unit)], out.at[inside], sems.at[g]
        )
        pending.append(copy)
        if number < SKEW:
            copy.start()
            continue
        row = number * stream.step + g * unit - place * (SKEW * stream.step)
        origin = info[5 + stream.panels]
        for j in range(1, stream.panels):
            origin = jnp.where(row >= stream.panel_start(j), info[5 + stream.panels + j], origin)
        passing = pltpu.make_async_copy(refs[0].at[inside], out.at[inside], sems.at[g])
        pl.when(origin < place)(passing.start)
        pl.when(origin >= place)(copy.start)
    for copy in pending:
        copy.wait()


def step_block(stream, number, info, counts, own, got, earlier):
    operands = ([got[number - SKEW]] if number >= SKEW else []) + earlier
    return pl.pallas_call(
        functools.partial(step_kernel, stream, number),
        out_shape=jax.ShapeDtypeStruct((stream.step, stream.size), jnp.float32),
        in_specs=[SMEM, SMEM] + [HBM] * (1 + len(operands)),
        out_specs=HBM,
        scratch_shapes=[pltpu.SemaphoreType.DMA((stream.step * 5 // stream.packed,))],
        compiler_params=param(4),
        cost_estimate=cost(0, 1000),
    )(info, counts, own, *operands)


def collect_kernel(stream, chips, first, last, info, own, *refs):
    received, out, sems = refs[:-2], refs[-2], refs[-1]
    place = info[2]
    pending = []
    step = stream.step
    edges = [(i * step, (i + 1) * step) for i in range(first, last)]
    for number, (j, i, low, count) in enumerate(stream.cuts(edges)):
        here = info[5 + stream.panels + j] >= place
        target = out.at[pl.ds(low - first * step, count)]
        start = pl.multiple_of(place * (SKEW * step) + low, 8)
        own_copy = pltpu.make_async_copy(own.at[pl.ds(start, count)], target, sems.at[number])
        pl.when(here)(own_copy.start)
        for p in range(1, chips):
            source = received[i + SKEW * (p - 1)].at[pl.ds(low - (first + i) * step, count)]
            copy = pltpu.make_async_copy(source, target, sems.at[number])
            pl.when(jnp.logical_not(here) & (place == p))(copy.start)
        pending.append(own_copy)
    for copy in pending:
        copy.wait()


def collected(stream, chips, first, last, info, own, got, earlier):
    received = [got[s] for s in range(first, last + SKEW * (chips - 2))]
    return pl.pallas_call(
        functools.partial(collect_kernel, stream, chips, first, last),
        out_shape=pltpu.HBM(((last - first) * stream.step, stream.size), jnp.float32),
        in_specs=[SMEM] + [HBM] * (1 + len(received) + len(earlier)),
        out_specs=HBM,
        scratch_shapes=[pltpu.SemaphoreType.DMA(((last - first) * len(stream.pieces),))],
        compiler_params=param(4),
        cost_estimate=cost(0, 1000),
    )(info, own, *received, *earlier)


def sweep_kernel(stream, n_sec, info, earlier, query, *refs):
    groups = len(GROUPS)
    own, other = refs[:groups], refs[groups : 2 * groups]
    out_high, out_low, done_ref, low_high, low_low, inv_high, inv_low, pending, part_high, part_low = refs[2 * groups : -2]
    arrived, sems = refs[-2:]
    done_ref[...] = jnp.zeros_like(done_ref)
    place, section = info[2], info[4]
    panels, size, step = stream.panels, stream.size, stream.step
    rows = query.shape[0]
    block = rows // n_sec
    tile = size // 4

    slots = arrived.shape[0]
    found = stream.cuts([(first * step, last * step) for first, last in GROUPS])
    copies = []

    def fetch(number):
        j, group, low, count = found[number]
        inside = pl.ds(low - GROUPS[group][0] * step, count)
        target = arrived.at[number % slots, pl.ds(0, count)]
        own_copy = pltpu.make_async_copy(own[group].at[inside], target, sems.at[number])
        other_copy = pltpu.make_async_copy(other[group].at[inside], target, sems.at[number])
        ahead = info[5 + panels + j] > place
        pl.when(ahead)(other_copy.start)
        pl.when(jnp.logical_not(ahead))(own_copy.start)
        copies.append(own_copy)

    for number in range(slots):
        fetch(number)

    for k in range(n_sec):
        start = pl.multiple_of(partner(section, k, n_sec) * block, block)
        for j in range(panels):
            pending[j, k * block : (k + 1) * block, :] = query[pl.ds(start, block), j * size : (j + 1) * size]

    for number, (_, _, low, count) in enumerate(found):
        copies[number].wait()

        @pl.loop(0, count // 64)
        def _(i):
            inside = pl.ds(pl.multiple_of(i * 64, 64), 64)
            span = pl.ds(pl.multiple_of(low + i * 64, 64), 64)
            low_high[span, :], low_low[span, :] = parts_of(arrived[number % slots, inside, :])

        if number + slots < len(found):
            fetch(number + slots)

    for j in range(panels):
        s = stream.panel_start(j + 1) - stream.packed
        for source, target in ((low_high, inv_high), (low_low, inv_low)):
            target[j] = jnp.zeros((size, size), jnp.bfloat16)
            target[j, 3 * tile :, :] = source[s : s + tile, :]
            target[j, 2 * tile : 3 * tile, : 3 * tile] = source[s + tile : s + 2 * tile, : 3 * tile]
            target[j, :tile, :tile] = source[s + tile : s + 2 * tile, 3 * tile :]
            middle = tile + tile // 2
            target[j, tile:middle, : 2 * tile] = source[s + 2 * tile : s + stream.packed, : 2 * tile]
            target[j, middle : 2 * tile, : 2 * tile] = source[s + 2 * tile : s + stream.packed, 2 * tile :]

    def below(j, k):
        span = pl.ds(pl.multiple_of(stream.panel_start(j) + (k - j - 1) * size, 64), size)
        return low_high[span, :], low_low[span, :]

    @pl.loop(0, panels)
    def _(j):
        solved = dot_parts(parts_of(pending[j]), (inv_high[j], inv_low[j]), 1)
        pending[j] = solved
        part_high[...], part_low[...] = parts_of(solved)

        @pl.loop(j + 1, panels)
        def _(k):
            pending[k] = pending[k] - dot_parts((part_high[...], part_low[...]), below(j, k), 1)

    @pl.loop(0, panels)
    def _(step_number):
        j = panels - 1 - step_number

        @pl.loop(j + 1, panels)
        def _(k):
            pending[j] = pending[j] - dot_parts((out_high[k], out_low[k]), below(j, k), 0)

        answer = dot_parts(parts_of(pending[j]), (inv_high[j], inv_low[j]), 0)
        out_high[j], out_low[j] = parts_of(answer)


def swept(stream, n_sec, info, earlier, query, own, other):
    rows = query.shape[0]
    panels, size, total = stream.panels, stream.size, stream.total
    out = jax.ShapeDtypeStruct((panels, rows, size), jnp.bfloat16)
    return pl.pallas_call(
        functools.partial(sweep_kernel, stream, n_sec),
        out_shape=(out, out, jax.ShapeDtypeStruct((8, 128), jnp.float32)),
        in_specs=[SMEM, HBM, VMEM] + [HBM] * (len(own) + len(other)),
        out_specs=(VMEM, VMEM, VMEM),
        scratch_shapes=[
            pltpu.VMEM((total, size), jnp.bfloat16),
            pltpu.VMEM((total, size), jnp.bfloat16),
            pltpu.VMEM((panels, size, size), jnp.bfloat16),
            pltpu.VMEM((panels, size, size), jnp.bfloat16),
            pltpu.VMEM((panels, rows, size), jnp.float32),
            pltpu.VMEM((rows, size), jnp.bfloat16),
            pltpu.VMEM((rows, size), jnp.bfloat16),
            pltpu.VMEM((4, size, size), jnp.float32),
            pltpu.SemaphoreType.DMA((len(stream.pieces) + len(GROUPS),)),
        ],
        compiler_params=param(32),
        cost_estimate=cost(0, 1000),
    )(info, earlier, query, *[pltpu.with_memory_space_constraint(x, pltpu.HBM) for x in (*own, *other)])


def score_kernel(n_sec, scale, blocks, counts, earlier, high, low, *refs):
    trains, outs = refs[: len(blocks)], refs[len(blocks) : len(blocks) + n_sec]
    train_high, train_low, total = refs[-3:]
    panels, rows, size = high.shape
    cols = total.shape[1]
    col = lax.broadcasted_iota(jnp.int32, (1, cols), 1)
    start, limit = 0, None
    for (length, which, first), train in zip(blocks, trains):
        for p in range(panels):
            span = slice(start, start + length)
            train_high[p, span, :], train_low[p, span, :] = parts_of(train[:, p * size : (p + 1) * size])
        bound = jnp.full_like(col, counts[which] - first + start)
        limit = bound if limit is None else jnp.where(col >= start, bound, limit)
        start += length
    total[...] = jnp.zeros_like(total)

    @pl.loop(0, panels)
    def _(p):
        total[...] += dot_parts((high[p], low[p]), (train_high[p], train_low[p]), 1)

    factor = jnp.where(col < limit, scale, 0.0).astype(jnp.float32)
    share = rows // n_sec
    for k in range(n_sec):
        outs[k][...] = total[k * share : (k + 1) * share, :] * factor


def scored(n_sec, scale, counts, earlier, high, low, runs):
    panels, rows, size = high.shape
    blocks = [(train.shape[0], which, first) for train, which, first in runs]
    cols = sum(length for length, _, _ in blocks)
    return pl.pallas_call(
        functools.partial(score_kernel, n_sec, scale, blocks),
        out_shape=tuple(jax.ShapeDtypeStruct((rows // n_sec, cols), jnp.float32) for _ in range(n_sec)),
        in_specs=[SMEM, HBM] + [VMEM] * (2 + len(runs)),
        out_specs=tuple(VMEM for _ in range(n_sec)),
        scratch_shapes=[
            pltpu.VMEM((panels, cols, size), jnp.bfloat16),
            pltpu.VMEM((panels, cols, size), jnp.bfloat16),
            pltpu.VMEM((rows, cols), jnp.float32),
        ],
        compiler_params=param(24),
        cost_estimate=cost(0, 1000),
    )(counts, earlier, high, low, *[train for train, _, _ in runs])


def body(query_gradient_stack, train_grads, factor_slots, owner, train_count):
    query, train, slot, owners = query_gradient_stack[0], train_grads[0], factor_slots[0, 0], owner[0]
    rows, coords = query.shape
    size = slot.shape[1]
    panels = coords // size
    n_dp, n_sec = lax.axis_size("dp"), lax.axis_size("section")
    chips = n_dp // 2
    stream = Stream(panels, size)
    me = lax.axis_index("dp")
    section = lax.axis_index("section")
    chip, core = lax.shift_right_logical(me, 1), me & 1
    first_core = core == 0
    place = jnp.where(first_core, chip, chips - 1 - chip)
    owner_chip = lax.shift_right_logical(owners, 1)
    owner_place = jnp.where(first_core, owner_chip, chips - 1 - owner_chip)
    info = jnp.concatenate([jnp.stack([chip, core, place, me, section]), owners, owner_place])

    swap_pairs = [(d, d ^ 1) for d in range(n_dp)]
    next_chip = [(d, (d + 2) % n_dp) for d in range(n_dp)]

    def swapped(value):
        return lax.ppermute(value, "dp", swap_pairs)

    cuts = [sum(TRAIN_CUTS[:i]) for i in range(len(TRAIN_CUTS) + 1)]
    first_part, slot = lax.optimization_barrier((train[: cuts[1]], slot))
    far = [lax.ppermute(first_part, "dp", next_chip)]

    def send_train(index, *earlier):
        part = ordered(train[cuts[index] : cuts[index + 1]], *earlier)
        far.append(lax.ppermute(part, "dp", next_chip))
        return part

    peer = swapped(slot)
    packed = inverted_diagonal(panels, info, slot)
    own_rows = build_stream(stream, chips, info, slot, peer, packed, swapped(packed))
    count_2 = lax.ppermute(train_count, "dp", next_chip)
    count_1 = lax.ppermute(train_count, "dp", [(d, (d + 1) % n_dp) for d in range(n_dp)])
    counts = jnp.concatenate([train_count, count_1, count_2])

    got, own, other = {}, [], []
    steps = CHUNKS + SKEW * (chips - 2)
    for number in range(steps):
        earlier = [corner(far[0])] if number == 0 else [block]
        block = step_block(stream, number, info, counts, own_rows, got, earlier)
        pairs = []
        for p in range(chips - 1):
            if 0 <= number - SKEW * p < CHUNKS:
                pairs += [(2 * p, 2 * p + 2), (2 * (chips - 1 - p) + 1, 2 * (chips - 2 - p) + 1)]
        got[number] = lax.ppermute(block, "dp", pairs)
        for first, last in GROUPS:
            if number == last - 1 + SKEW * (chips - 2):
                before = [corner(rows_before) for rows_before in other[:2]] if last == CHUNKS else []
                value = collected(stream, chips, first, last, info, own_rows, got, before)
                own.append(value)
                other.append(swapped(value))

    part = send_train(1, corner(other[-1]))
    high, low, swept_token = swept(stream, n_sec, info, corner(part), query, own, other)
    for index in range(2, len(cuts) - 1):
        send_train(index, swept_token)

    scale = (coords * n_sec) ** (-0.5)

    def summed(parts):
        total = parts[0]
        for k in range(1, n_sec):
            if n_sec & (n_sec - 1) == 0:
                pairs = [(s, s ^ k) for s in range(n_sec)]
            else:
                pairs = [(s, (s + k) % n_sec) for s in range(n_sec)]
            total = total + lax.ppermute(parts[k], "section", pairs)
        return total

    def near_rows(index, *earlier):
        return swapped(chosen(info, train, cuts[index], far[index], *earlier))

    runs = [(train, 0, 0), (near_rows(0, swept_token), 1, 0), (far[0], 2, 0)]
    near_scores, far_scores, summed_corners, earlier = [], [], [], [swept_token]
    for index in range(len(cuts) - 1):
        if index:
            runs = [(near_rows(index, *earlier), 1, cuts[index]), (far[index], 2, cuts[index])]
        parts = scored(n_sec, scale, counts, earlier[0], high, low, runs)
        both = summed(parts)
        summed_corners.append(corner(both))
        earlier = [corner(parts[0])] + (summed_corners if index else [])
        length = cuts[index + 1] - cuts[index]
        if index == 0:
            own_scores, both = both[:, :rows], both[:, rows:]
        near_scores.append(both[:, :length])
        far_scores.append(both[:, length:])
    return jnp.concatenate([own_scores] + near_scores + far_scores, axis=1)[None]


def solution(mesh):
    in_specs = (
        P("section", "dp", None),
        P("section", "dp", None),
        P("section", "dp", None, None),
        P("section", None),
        P("dp"),
    )
    out_specs = P("dp", "section", None)
    return jax.shard_map(body, mesh=mesh, in_specs=in_specs, out_specs=out_specs, check_vma=False)
```
